32 devices in a mesh: groups: 2 (over x), nodes: 16 (over z, y, core).
Axes of the slice: x: 2, y: 2, z: 4, core: 2. Of those that a mesh axis runs over, the one named last changes fastest.
Arguments:
- features: bfloat16 [16384, 128], P(('groups', 'nodes')), parts along dimension 0, may hold values from -6 to 6
- cluster: int32 [16384], P(('groups', 'nodes')), parts along dimension 0, may hold values from 0 to 15, as said below
- slot: int32 [16384], P(('groups', 'nodes')), parts along dimension 0, may hold values from 0 to 511, as said below
- halo_tiles: int32 [32, 64], P(('groups', 'nodes')), parts along dimension 0, may hold values from 0 to 63, as said below
- tile_slots: int32 [128, 64], P(('groups', 'nodes')), parts along dimension 0, may hold values from 0 to 63
- adjacency: bfloat16 [16384, 64, 128], P(('groups', 'nodes')), parts along dimension 0, may hold values from -0.0625 to 0.0625
- labels: int32 [16384], P(('groups', 'nodes')), parts along dimension 0, may hold values from -1 to 171, as said below
- w_self: bfloat16 [128, 256], replicated, may hold values from -0.5 to 0.5
- w_neigh: bfloat16 [128, 256], replicated, may hold values from -0.5 to 0.5
- w_out: bfloat16 [256, 172], replicated, may hold values from -0.375 to 0.375
- b_out: float32 [172], replicated, may hold values from -9 to 9
Outputs:
- hidden: bfloat16 [16384, 256], P(('groups', 'nodes')), parts along dimension 0
- grad_self: float32 [256, 256], P('groups'), parts along dimension 0
- grad_neigh: float32 [256, 256], P('groups'), parts along dimension 0
- grad_out: float32 [512, 172], P('groups'), parts along dimension 0
- class_weight: float32 [344], P('groups'), parts along dimension 0
The draws below stay inside these ranges and needn't reach their ends.
There are 2 independent parts, one for each index of `groups`. The reference program is written for one: setup_inputs(seed, part) draws one part's arguments, and reference() takes and returns one part's arrays. A program takes and returns all parts, laid end to end along the dimension named above; an argument that names none is the same for every part. Nothing has to cross between parts.
Inputs may be any that keep to these rules, and one draw needn't show every extreme that they name: `cluster`: exactly 32 of the rows stored on each device belong to each partition. `slot`: together with cluster, every position of every partition is taken by exactly one stored row. `halo_tiles`: tile g is held in partition order by device g // 4. In each row, no device holds more than 4 of the tiles, and some device holds exactly 4. `labels`: -1 marks an unlabelled node.
All inputs are finite; a program needn't handle non-finite values.
Results may differ from the reference program's by a relative error of at most 0.006.
The reference program's roundings to bfloat16 on the way (of `part_x`, `agg`, `dlogits` and `dpre`) count: a program that leaves them out, or rounds other values in their place, can miss the bound.
Values may be sent and summed in bfloat16 or wider, within the bound.
No kernel may reach another device: no remote copies, remote signals or barrier semaphores. Data moves between devices by JAX's collectives and lax.ppermute only.
A program may use at most 128 MiB of HBM per device.

```python
import jax
import jax.numpy as jnp
from jax import lax

FEAT = 128
HID = 256
CLASSES = 172
TILE = 128
TILES_DEV = 4
NEIGH = 64
HALO = 64
NODE_DEV = 512
NODES = 8192
TILES = 64
N_NODES = 16


def relay_plan(key):
    per_peer = NODE_DEV // N_NODES
    order_keys = jax.random.split(jax.random.fold_in(key, 11), N_NODES)
    order = jax.vmap(lambda k: jax.random.permutation(k, NODE_DEV))(order_keys)
    place_keys = jax.random.split(jax.random.fold_in(key, 12), N_NODES)
    within = jax.vmap(lambda k: jax.random.permutation(k, NODE_DEV))(place_keys)
    position = jnp.arange(NODE_DEV, dtype=jnp.int32)
    target = position // per_peer
    source = jnp.arange(N_NODES, dtype=jnp.int32)[:, None]
    placed = within[target[None, :], source * per_peer + (position % per_peer)[None, :]]
    target_full = jnp.broadcast_to(target[None, :], (N_NODES, NODE_DEV))
    cluster = jnp.zeros((N_NODES, NODE_DEV), jnp.int32).at[source, order].set(target_full)
    slots = jnp.zeros((N_NODES, NODE_DEV), jnp.int32).at[source, order].set(placed.astype(jnp.int32))
    return (cluster.reshape(NODES), slots.reshape(NODES))


def draw_cluster(key, part):
    plan = relay_plan(key)
    return plan[0].astype(jnp.int32)


def draw_slot(key, part):
    plan = relay_plan(key)
    return plan[1].astype(jnp.int32)


def draw_halo_tiles(key, part):
    key = jax.random.fold_in(key, 5)
    offset_key, local_key = jax.random.split(key)
    offset_keys = jax.random.split(offset_key, N_NODES)
    offsets = jax.vmap(lambda k: jax.random.permutation(k, N_NODES))(offset_keys)
    column = jnp.arange(HALO, dtype=jnp.int32) % N_NODES
    shifted = offsets[:, column]
    owner = (jnp.arange(N_NODES, dtype=jnp.int32)[:, None] + shifted) % N_NODES
    local = jax.random.randint(local_key, (N_NODES, HALO), 0, TILES_DEV)
    return (owner * TILES_DEV + local).astype(jnp.int32)


def draw_labels(key, part):
    key = jax.random.fold_in(key, 7)
    coin_key, class_key = jax.random.split(key)
    batch = jnp.arange(NODES, dtype=jnp.int32) // NODE_DEV
    limit = 200 + 600 * batch // max(N_NODES - 1, 1)
    coin = jax.random.randint(coin_key, (NODES,), 0, 1000)
    chosen = jax.random.randint(class_key, (NODES,), 0, CLASSES)
    return jnp.where(coin < limit, chosen, -1).astype(jnp.int32)


def set_ends(drawn, stream_key, least, top_value):
    longest = drawn.shape.index(max(drawn.shape))
    spots = []
    for shift in (0, 1):
        where = [jax.random.randint(jax.random.fold_in(stream_key, axis), (), 0, length) for axis, length in enumerate(drawn.shape)]
        where[longest] = (where[longest] + shift) % drawn.shape[longest]
        spots.append(tuple(where))
    return drawn.at[spots[0]].set(least).at[spots[1]].set(top_value)


def block_scale(rng, shape, shards, low, high):
    factor_of, own = 1.0, jax.random.fold_in(rng, 6)
    for axis_at, blocks in shards:
        heights = jnp.exp(jax.random.uniform(jax.random.fold_in(own, axis_at), (blocks,), jnp.float32, low / len(shards), high / len(shards)))
        factor_of = factor_of * jnp.repeat(heights, shape[axis_at] // blocks).reshape([-1 if axis == axis_at else 1 for axis in range(len(shape))])
    return factor_of


def noise(key, extent, width, bound, cuts=(), kind=jnp.bfloat16):
    result = jax.random.normal(key, extent, jnp.float32) * width
    if len(cuts) > 0:
        result = block_scale(key, extent, cuts, -0.22, 0.18) * result
    return jnp.clip(result, min=-bound, max=bound).astype(kind)


def setup_inputs(seed: int = 0, part: int = 0) -> dict:
    key_list = jax.random.split(jax.random.key(seed), 12)
    part_splits = jax.random.split(jax.random.fold_in(key_list[11], part), 12)
    return {
        "features": noise(part_splits[0], (NODES, FEAT), 1.0, 6.0, ((0, 16),)),
        "cluster": draw_cluster(jax.random.fold_in(jax.random.fold_in(key_list[11], part), 71), part),
        "slot": draw_slot(jax.random.fold_in(jax.random.fold_in(key_list[11], part), 71), part),
        "halo_tiles": draw_halo_tiles(jax.random.fold_in(jax.random.fold_in(key_list[11], part), 71), part),
        "tile_slots": set_ends(jax.random.randint(part_splits[4], (TILES, NEIGH), 0, HALO), jax.random.fold_in(part_splits[4], 1), 0, HALO - 1).astype(jnp.int32),
        "adjacency": noise(part_splits[5], (NODES, NEIGH, TILE), (NEIGH * TILE) ** -0.5, 0.0625, ((0, 16),)),
        "labels": draw_labels(jax.random.fold_in(jax.random.fold_in(key_list[11], part), 71), part),
        "w_self": noise(key_list[7], (FEAT, HID), FEAT ** -0.5, 0.5),
        "w_neigh": noise(key_list[8], (FEAT, HID), FEAT ** -0.5, 0.5),
        "w_out": noise(key_list[9], (HID, CLASSES), HID ** -0.5, 0.375),
        "b_out": noise(key_list[10], (CLASSES,), 3.0, 9.0, (), jnp.float32),
    }


def reference(features, cluster, slot, halo_tiles, tile_slots, adjacency, labels, w_self, w_neigh, w_out, b_out):
    where_to = cluster * NODE_DEV + slot
    part_x = jnp.zeros((NODES, FEAT), jnp.bfloat16).at[where_to].set(features)
    tiles_x = part_x.reshape(TILES, TILE, FEAT)
    adj_blocks = adjacency.reshape(N_NODES, TILES_DEV, TILE, NEIGH, TILE)
    slot_blocks = tile_slots.reshape(N_NODES, TILES_DEV, NEIGH)

    def one_batch(packed):
        weights, slots_here, reads = packed
        chosen = reads[slots_here]
        sources = tiles_x[chosen].astype(jnp.float32)
        return jnp.einsum("tikc,tkcf->tif", weights.astype(jnp.float32), sources, precision=lax.Precision.HIGHEST)

    agg = lax.map(one_batch, (adj_blocks, slot_blocks, halo_tiles)).reshape(NODES, FEAT).astype(jnp.bfloat16)
    pre = jnp.dot(part_x, w_self, preferred_element_type=jnp.float32) + jnp.dot(agg, w_neigh, preferred_element_type=jnp.float32)
    hidden = jnp.maximum(pre, 0.0).astype(jnp.bfloat16)
    logits = jnp.dot(hidden, w_out, preferred_element_type=jnp.float32) + b_out
    lse = jnp.log(jnp.sum(jnp.exp(logits), axis=1))
    classes_row = jnp.arange(CLASSES, dtype=jnp.int32)
    onehot = (labels[:, None] == classes_row[None, :]).astype(jnp.float32)
    picked = jnp.sum(onehot * logits, axis=1)
    ce_rows = lse - picked
    loss_sum = jnp.sum(onehot * ce_rows[:, None], axis=0)
    counts = jnp.sum(onehot, axis=0)
    difficulty = (loss_sum + 1.0) / (counts + 1.0)
    class_weight = difficulty / jnp.mean(difficulty)
    total = jnp.sum(counts)
    row_weight = jnp.sum(onehot * class_weight[None, :], axis=1) / (total + 1.0)
    probs = jnp.exp(logits - lse[:, None])
    dlogits = (row_weight[:, None] * (probs - onehot)).astype(jnp.bfloat16)
    grad_out = jnp.dot(hidden.T, dlogits, preferred_element_type=jnp.float32)
    dhidden = jnp.dot(dlogits, w_out.T, preferred_element_type=jnp.float32)
    dpre = jnp.where(hidden > 0, dhidden, 0.0).astype(jnp.bfloat16)
    grad_self = jnp.dot(part_x.T, dpre, preferred_element_type=jnp.float32)
    grad_neigh = jnp.dot(agg.T, dpre, preferred_element_type=jnp.float32)
    return (hidden, grad_self, grad_neigh, grad_out, class_weight)
```

```python
import jax
import jax.numpy as jnp
from jax import lax
from jax.experimental import pallas as pl
from jax.experimental.pallas import tpu as pltpu
from jax.sharding import PartitionSpec as P

TILE = 128
LANES = 128
SUB = 16
VMEM = 48 << 20
F32 = jnp.float32
BF16 = jnp.bfloat16


def _dot(a, b, contract=((1,), (0,))):
    return lax.dot_general(a, b, (contract, ((), ())), preferred_element_type=F32)


NT = ((1,), (1,))


def _iota(shape, dim):
    return lax.broadcasted_iota(jnp.int32, shape, dim)


def _params():
    return pltpu.CompilerParams(vmem_limit_bytes=VMEM)


def gather_all(block, devices):
    def swap(x, m):
        return lax.ppermute(x, "nodes", [(i, i ^ m) for i in range(devices)])

    have = {0: block}
    m = devices // 2
    while m > 1:
        have.update({k | m: swap(x, m) for k, x in sorted(have.items(), reverse=True)})
        m //= 2
    have.update({k | 1: swap(x, 1) for k, x in sorted(have.items())})
    return [have[m] for m in range(devices)]


def pack_kernel(devices, feat_ref, cluster_ref, slot_ref, label_ref, out_ref):
    rows = feat_ref.shape[0]
    per = rows // devices
    mine = lax.axis_index("nodes") % (LANES // per)
    cluster = cluster_ref[...]
    member = (_iota((devices, rows), 0) == cluster).astype(F32)
    before = (_iota((rows, rows), 0) < _iota((rows, rows), 1)).astype(BF16)
    rank = jnp.sum(member * _dot(member.astype(BF16), before), axis=0, keepdims=True).astype(jnp.int32)
    take = (_iota((rows, rows), 0) == cluster * per + rank).astype(BF16)
    out_ref[0:devices] = _dot(take, feat_ref[...]).astype(BF16).reshape(devices, per, feat_ref.shape[1])
    place = (_iota((LANES, rows), 0) == mine * per + rank).astype(BF16)
    slots = (member * (slot_ref[...] - rows // 2).astype(F32)).astype(BF16)
    out_ref[devices, 0:SUB] = _dot(slots, place, NT).astype(BF16)
    out_ref[devices, SUB : 2 * SUB] = label_ref[...].astype(BF16)


def pack(features, cluster, slot, labels, devices):
    rows, width = features.shape
    per = rows // devices
    padded = jnp.pad(labels.reshape(rows // LANES, LANES).astype(F32), ((0, SUB - rows // LANES), (0, 0)))
    return pl.pallas_call(
        lambda *refs: pack_kernel(devices, *refs),
        out_shape=jax.ShapeDtypeStruct((devices + 1, per, width), BF16),
        compiler_params=_params(),
        name="pack_rows",
    )(features, cluster.reshape(1, rows), slot.reshape(1, rows), padded)


def turn_kernel(a_ref, o_ref):
    side = SUB * SUB
    row = _iota((side, side), 0)
    move = ((row % SUB) * SUB + row // SUB == _iota((side, side), 1)).astype(BF16)
    for b in range(a_ref.shape[0] // SUB):
        for j in range(a_ref.shape[1] // (2 * SUB)):
            halves = [
                a_ref[SUB * b : SUB * (b + 1), SUB * k : SUB * (k + 1), :].reshape(side, LANES)
                for k in (2 * j, 2 * j + 1)
            ]
            moved = _dot(move, jnp.concatenate(halves, axis=1)).astype(BF16)
            for h in range(2):
                k = 2 * j + h
                o_ref[0, SUB * k : SUB * (k + 1), SUB * b : SUB * (b + 1), :] = moved[
                    :, LANES * h : LANES * (h + 1)
                ].reshape(SUB, SUB, LANES)


def turn(adjacency):
    rows, neigh, tile = adjacency.shape
    tiles = rows // tile
    return pl.pallas_call(
        turn_kernel,
        grid=(tiles,),
        in_specs=[pl.BlockSpec((tile, neigh, tile), lambda t: (t, 0, 0))],
        out_specs=pl.BlockSpec((1, neigh, tile, tile), lambda t: (t, 0, 0, 0)),
        out_shape=jax.ShapeDtypeStruct((tiles, neigh, tile, tile), BF16),
        compiler_params=_params(),
        name="turn_adjacency",
    )(adjacency)


def aggregate_kernel(devices, *refs):
    blocks = refs[:devices]
    adj_ref, halo_ref, slots_ref = refs[devices : devices + 3]
    px_ref, labels_ref, agg_ref = refs[devices + 3 : devices + 6]
    got, meta, adj, sems, adj_sems = refs[devices + 6 :]
    me = lax.axis_index("nodes")
    per = blocks[0].shape[1]
    rows = devices * per
    tiles, neigh = adj.shape[0], adj.shape[1]
    group = LANES // per

    adj_copies = [pltpu.make_async_copy(adj_ref.at[t], adj.at[t], adj_sems.at[t]) for t in range(tiles)]
    copies = []
    for m, block in enumerate(blocks):
        owner = me ^ m
        at = pl.ds(pl.multiple_of(owner * per, per), per)
        copies.append(pltpu.make_async_copy(block.at[0:devices], got.at[:, at, :], sems.at[0, m]))
        copies.append(pltpu.make_async_copy(block.at[devices], meta.at[owner], sems.at[1, m]))
    for copy in copies + adj_copies:
        copy.start()
    for copy in copies:
        copy.wait()

    labels_ref[...] = meta[:, SUB : 2 * SUB, :]
    slots = [
        sum(meta[q * group + j, 0:SUB, :].astype(F32) for j in range(group)) for q in range(devices // group)
    ]
    slots = jnp.concatenate(slots, axis=1).astype(jnp.int32)
    position = _iota((rows, rows), 0) - rows // 2
    for p in range(devices):
        put = (position == slots[p : p + 1, :]).astype(BF16)
        px_ref[p * rows : (p + 1) * rows, :] = _dot(put, got[p]).astype(BF16)

    for t in range(tiles):
        adj_copies[t].wait()
        total = jnp.zeros((TILE, px_ref.shape[1]), F32)
        for k in range(0, neigh, 2):
            sources = []
            for j in (k, k + 1):
                tile = halo_ref[0, slots_ref[t, j]]
                sources.append(px_ref[pl.ds(pl.multiple_of(tile * TILE, TILE), TILE), :])
            weights = jnp.concatenate([adj[t, k], adj[t, k + 1]], axis=1)
            total += _dot(weights, jnp.concatenate(sources, axis=0))
        agg_ref[t * TILE : (t + 1) * TILE, :] = total.astype(BF16)


def aggregate(blocks, turned, halo_tiles, tile_slots, devices):
    per, width = blocks[0].shape[1:]
    rows = devices * per
    anywhere = pl.BlockSpec(memory_space=pl.ANY)
    scalars = pl.BlockSpec(memory_space=pltpu.SMEM)
    vmem = pl.BlockSpec(memory_space=pltpu.VMEM)
    return pl.pallas_call(
        lambda *refs: aggregate_kernel(devices, *refs),
        in_specs=[anywhere] * (devices + 1) + [scalars] * 2,
        out_specs=[vmem] * 3,
        out_shape=[
            jax.ShapeDtypeStruct((devices * rows, width), BF16),
            jax.ShapeDtypeStruct((devices, SUB, LANES), BF16),
            jax.ShapeDtypeStruct((rows, width), BF16),
        ],
        scratch_shapes=[
            pltpu.VMEM((devices, rows, width), BF16),
            pltpu.VMEM((devices, 2 * SUB, LANES), BF16),
            pltpu.VMEM(turned.shape, BF16),
            pltpu.SemaphoreType.DMA((2, devices)),
            pltpu.SemaphoreType.DMA((turned.shape[0],)),
        ],
        compiler_params=_params(),
        name="aggregate",
    )(*blocks, turned, halo_tiles, tile_slots)


def learn_kernel(devices, classes, *refs):
    blocks = refs[:devices]
    px_ref, labels_ref, w_in_t_ref, w_out_ref, w_out_t_ref, bias_ref = refs[devices : devices + 6]
    self_ref, neigh_ref, out_ref, class_ref = refs[devices + 6 : devices + 10]
    x, hid, log, lse_all, sems = refs[devices + 10 :]
    me = lax.axis_index("nodes")
    rows, width = blocks[0].shape
    padded = log.shape[1]
    copies = []
    for m, block in enumerate(blocks):
        owner = me ^ m
        copies.append(pltpu.make_async_copy(block, x.at[owner, :, pl.ds(width, width)], sems.at[0, m]))
        source = px_ref.at[pl.ds(pl.multiple_of(m * rows, rows), rows), :]
        copies.append(pltpu.make_async_copy(source, x.at[m, :, pl.ds(0, width)], sems.at[1, m]))
    for copy in copies:
        copy.start()
    for copy in copies:
        copy.wait()

    kinds = _iota((padded, rows), 0)

    def is_class(s):
        held = labels_ref[s].astype(F32)
        label = jnp.concatenate([held[j : j + 1, :] for j in range(rows // LANES)], axis=1)
        return kinds == label.astype(jnp.int32)

    def fold(a):
        return sum(a[:, LANES * j : LANES * (j + 1)] for j in range(rows // LANES))

    def forward(s, carry):
        loss, count = carry
        pre = _dot(w_in_t_ref[...], x[s], NT)
        hidden = jnp.maximum(pre, 0.0).astype(BF16)
        hid[s] = hidden
        logits = _dot(w_out_t_ref[...], hidden) + bias_ref[...]
        log[s] = logits
        lse = jnp.log(jnp.sum(jnp.exp(logits), axis=0, keepdims=True))
        lse_all[s] = lse
        hot = is_class(s)
        picked = jnp.sum(jnp.where(hot, logits, 0.0), axis=0, keepdims=True)
        loss += fold(jnp.where(hot, lse - picked, 0.0))
        count += fold(hot.astype(F32))
        return loss, count

    zero = jnp.zeros((padded, LANES), F32)
    loss, count = lax.fori_loop(0, devices, forward, (zero, zero))
    loss = jnp.sum(loss, axis=1, keepdims=True)
    count = jnp.sum(count, axis=1, keepdims=True)
    real = _iota((padded, 1), 0) < classes
    difficulty = jnp.where(real, (loss + 1.0) / (count + 1.0), 0.0)
    weight = difficulty / (jnp.sum(difficulty, axis=0, keepdims=True) / classes)
    share = 1.0 / (1.0 + jnp.sum(count, axis=0, keepdims=True))
    class_ref[...] = jnp.transpose(jnp.broadcast_to(weight, (padded, LANES)))[0:1, 0:classes]
    scaled = weight * share

    def backward(s, carry):
        grad_in, grad_out = carry
        hot = is_class(s)
        row = jnp.sum(jnp.where(hot, scaled, 0.0), axis=0, keepdims=True)
        probs = jnp.exp(log[s] - lse_all[s])
        dlogits = (row * (probs - hot.astype(F32))).astype(BF16)
        hidden = hid[s]
        grad_out += _dot(hidden, dlogits, NT)
        dhidden = _dot(w_out_ref[...], dlogits)
        dpre = jnp.where(hidden > 0, dhidden, 0.0).astype(BF16)
        grad_in += _dot(dpre, x[s])
        return grad_in, grad_out

    units = hid.shape[1]
    start = (jnp.zeros((units, 2 * width), F32), jnp.zeros((units, padded), F32))
    grad_in, grad_out = lax.fori_loop(0, devices, backward, start)
    grad_in = jnp.transpose(grad_in)
    self_ref[...] = grad_in[0:width]
    neigh_ref[...] = grad_in[width : 2 * width]
    out_ref[...] = grad_out[:, 0:classes]


def learn(blocks, part_x, labels, w_in, w_out, b_out, devices):
    rows, width = blocks[0].shape
    units, classes = w_out.shape
    padded = -(-classes // SUB) * SUB
    extra = padded - classes
    w_out_p = jnp.pad(w_out, ((0, 0), (0, extra)))
    bias = jnp.pad(b_out, (0, extra), constant_values=-1e30).reshape(padded, 1)
    anywhere = pl.BlockSpec(memory_space=pl.ANY)
    vmem = pl.BlockSpec(memory_space=pltpu.VMEM)
    return pl.pallas_call(
        lambda *refs: learn_kernel(devices, classes, *refs),
        in_specs=[anywhere] * (devices + 1) + [vmem] * 5,
        out_specs=[vmem] * 4,
        out_shape=[
            jax.ShapeDtypeStruct((width, units), F32),
            jax.ShapeDtypeStruct((width, units), F32),
            jax.ShapeDtypeStruct((units, classes), F32),
            jax.ShapeDtypeStruct((1, classes), F32),
        ],
        scratch_shapes=[
            pltpu.VMEM((devices, rows, 2 * width), BF16),
            pltpu.VMEM((devices, units, rows), BF16),
            pltpu.VMEM((devices, padded, rows), F32),
            pltpu.VMEM((devices, 1, rows), F32),
            pltpu.SemaphoreType.DMA((2, devices)),
        ],
        compiler_params=_params(),
        name="learn",
    )(*blocks, part_x, labels, w_in.T, w_out_p, w_out_p.T, bias)


def gathered_body(
    features, cluster, slot, halo_tiles, tile_slots, adjacency, labels, w_self, w_neigh, w_out, b_out
):
    rows = features.shape[0]
    devices = lax.axis_size("nodes")
    packed = pack(features, cluster, slot, labels, devices)
    turned = turn(adjacency)
    part_x, all_labels, agg = aggregate(gather_all(packed, devices), turned, halo_tiles, tile_slots, devices)
    w_in = jnp.concatenate([w_self, w_neigh], axis=0)
    mine = lax.dynamic_slice_in_dim(part_x, lax.axis_index("nodes") * rows, rows, 0)
    pre = _dot(jnp.concatenate([mine, agg], axis=1), w_in)
    hidden = jnp.maximum(pre, 0.0).astype(BF16)
    grad_self, grad_neigh, grad_out, class_weight = learn(
        gather_all(agg, devices), part_x, all_labels, w_in, w_out, b_out, devices
    )
    return hidden, grad_self, grad_neigh, grad_out, class_weight.reshape(-1)


def split_body(
    features, cluster, slot, halo_tiles, tile_slots, adjacency, labels, w_self, w_neigh, w_out, b_out
):
    rows = features.shape[0]
    width = features.shape[1]
    devices = lax.axis_size("nodes")
    per_peer = rows // devices
    order = jnp.argsort(cluster, stable=True)
    send_rows = features[order].reshape(devices, per_peer, width)
    send_slots = slot[order].reshape(devices, per_peer)
    recv_rows, recv_slots = (
        lax.all_to_all(send_rows, "nodes", split_axis=0, concat_axis=0, tiled=True),
        lax.all_to_all(send_slots, "nodes", split_axis=0, concat_axis=0, tiled=True),
    )
    part_x = (
        jnp.zeros((rows, width), jnp.bfloat16)
        .at[recv_slots.reshape(rows)]
        .set(recv_rows.reshape(rows, width))
    )
    local_tiles = rows // TILE
    wanted = halo_tiles[0]
    gathered = lax.all_gather(part_x, "nodes", axis=0, tiled=True)
    halo = gathered.reshape(-1, TILE, width)[wanted]
    sources = halo[tile_slots]
    adj_tiles = adjacency.reshape(local_tiles, TILE, adjacency.shape[1], TILE)
    agg = jnp.einsum("tikc,tkcf->tif", adj_tiles, sources, preferred_element_type=jnp.float32)
    agg = agg.reshape(rows, width).astype(jnp.bfloat16)
    pre = jnp.dot(part_x, w_self, preferred_element_type=jnp.float32) + jnp.dot(
        agg, w_neigh, preferred_element_type=jnp.float32
    )
    hidden = jnp.maximum(pre, 0.0).astype(jnp.bfloat16)
    logits = jnp.dot(hidden, w_out, preferred_element_type=jnp.float32) + b_out
    lse = jnp.log(jnp.sum(jnp.exp(logits), axis=1))
    classes_row = jnp.arange(w_out.shape[1], dtype=jnp.int32)
    onehot = (labels[:, None] == classes_row[None, :]).astype(jnp.float32)
    picked = jnp.sum(onehot * logits, axis=1)
    ce_rows = lse - picked
    local_loss = jnp.sum(onehot * ce_rows[:, None], axis=0)
    local_counts = jnp.sum(onehot, axis=0)
    loss_sum, counts = lax.psum((local_loss, local_counts), "nodes")
    difficulty = (loss_sum + 1.0) / (counts + 1.0)
    class_weight = difficulty / jnp.mean(difficulty)
    total = jnp.sum(counts)
    row_weight = jnp.sum(onehot * class_weight[None, :], axis=1) / (total + 1.0)
    probs = jnp.exp(logits - lse[:, None])
    dlogits = (row_weight[:, None] * (probs - onehot)).astype(jnp.bfloat16)
    part_out = jnp.dot(hidden.T, dlogits, preferred_element_type=jnp.float32)
    dhidden = jnp.dot(dlogits, w_out.T, preferred_element_type=jnp.float32)
    dpre = jnp.where(hidden > 0, dhidden, 0.0).astype(jnp.bfloat16)
    part_self = jnp.dot(part_x.T, dpre, preferred_element_type=jnp.float32)
    part_neigh = jnp.dot(agg.T, dpre, preferred_element_type=jnp.float32)
    grad_self, grad_neigh, grad_out = lax.psum((part_self, part_neigh, part_out), "nodes")
    return (hidden, grad_self, grad_neigh, grad_out, class_weight)


def solution(mesh):
    def body(*args):
        devices = mesh.shape["nodes"]
        rows = args[0].shape[0]
        per = rows // devices
        classes = args[9].shape[1]
        fits = devices & (devices - 1) == 0 and devices <= SUB and per == 2 * SUB and rows <= 512 and classes <= 256
        return (gathered_body if fits else split_body)(*args)

    return jax.shard_map(
        body,
        mesh=mesh,
        in_specs=(
            P(("groups", "nodes"), None),
            P(("groups", "nodes")),
            P(("groups", "nodes")),
            P(("groups", "nodes"), None),
            P(("groups", "nodes"), None),
            P(("groups", "nodes"), None, None),
            P(("groups", "nodes")),
            P(),
            P(),
            P(),
            P(),
        ),
        out_specs=(
            P(("groups", "nodes"), None),
            P("groups", None),
            P("groups", None),
            P("groups", None),
            P("groups"),
        ),
        check_vma=False,
    )
```

```python
import jax
import jax.numpy as jnp
from jax import lax
from jax.experimental import pallas as pl
from jax.experimental.pallas import tpu as pltpu
from jax.sharding import PartitionSpec as P

DEVICES = 16
QUAD = 4
TILE = 128
LANES = 128
SUB = 16
F32 = jnp.float32
BF16 = jnp.bfloat16


def _dot(a, b, contract=((1,), (0,))):
    return lax.dot_general(a, b, (contract, ((), ())), preferred_element_type=F32)


NT = ((1,), (1,))


def _iota(shape, dim):
    return lax.broadcasted_iota(jnp.int32, shape, dim)


def _params(mib):
    return pltpu.CompilerParams(vmem_limit_bytes=mib << 20)


def swap(x, m):
    return lax.ppermute(x, "nodes", [(i, i ^ m) for i in range(DEVICES)])


def gather_all(block, work):
    have = {0: block}
    done = []

    def hop(i, m):
        if i < len(work):
            out = work[i](have)
            if len(work) == 1:
                have[m], out = lax.optimization_barrier((have[m], out))
            done.append(out)

    have[8], have[4], have[2], have[1] = (swap(block, m) for m in (8, 4, 2, 1))
    have[3] = swap(have[2], 1)
    hop(0, 8)
    have[12], have[10], have[6] = swap(have[8], 4), swap(have[8], 2), swap(have[4], 2)
    have[5], have[7], have[9] = swap(have[4], 1), swap(have[6], 1), swap(have[8], 1)
    hop(1, 12)
    have[14] = swap(have[12], 2)
    have[11], have[13] = swap(have[10], 1), swap(have[12], 1)
    hop(2, 14)
    have[15] = swap(have[14], 1)
    return have, done


def pack_kernel(devices, *refs):
    sources, out_ref, targets, sems = refs[0:4], refs[4], refs[5:9], refs[9]
    copies = [pltpu.make_async_copy(a, b, sems.at[i]) for i, (a, b) in enumerate(zip(sources, targets))]
    for copy in copies:
        copy.start()
    for copy in copies:
        copy.wait()
    feat_ref, cluster_ref, slot_ref, label_ref = targets
    rows = feat_ref.shape[0]
    per = rows // devices
    mine = lax.axis_index("nodes") % (LANES // per)
    cluster = cluster_ref[...]
    member = (_iota((devices, rows), 0) == cluster).astype(F32)
    before = (_iota((rows, rows), 0) < _iota((rows, rows), 1)).astype(BF16)
    rank = jnp.sum(member * _dot(member.astype(BF16), before), axis=0, keepdims=True).astype(jnp.int32)
    take = (_iota((rows, rows), 0) == cluster * per + rank).astype(BF16)
    out_ref[0:devices] = _dot(take, feat_ref[...]).astype(BF16).reshape(devices, per, feat_ref.shape[1])
    place = (_iota((LANES, rows), 0) == mine * per + rank).astype(BF16)
    slots = (member * (slot_ref[...] - rows // 2).astype(F32)).astype(BF16)
    out_ref[devices, 0:SUB] = _dot(slots, place, NT).astype(BF16)
    labels = jnp.concatenate([label_ref[...].astype(F32), jnp.zeros((SUB - label_ref.shape[0], LANES), F32)], axis=0)
    out_ref[devices, SUB : 2 * SUB] = labels.astype(BF16)


def pack(features, cluster, slot, labels, devices):
    rows, width = features.shape
    per = rows // devices
    inputs = (features, cluster.reshape(1, rows), slot.reshape(1, rows), labels.reshape(rows // LANES, LANES))
    return pl.pallas_call(
        lambda *refs: pack_kernel(devices, *refs),
        in_specs=[pl.BlockSpec(memory_space=pltpu.HBM)] * 4,
        out_specs=pl.BlockSpec(memory_space=pltpu.VMEM),
        out_shape=jax.ShapeDtypeStruct((devices + 1, per, width), BF16),
        scratch_shapes=[*[pltpu.VMEM(x.shape, x.dtype) for x in inputs], pltpu.SemaphoreType.DMA((4,))],
        compiler_params=_params(60),
        name="pack_rows",
    )(*inputs)


def prepare_kernel(adj_ref, self_ref, neigh_ref, w_out_ref, b_ref, *refs):
    turned_ref, in_t_ref, out_t_ref, out_ref, bias_ref, adj, wide, line, sems = refs
    tiles, neigh = turned_ref.shape[0:2]
    classes = w_out_ref.shape[0]
    copies = [pltpu.make_async_copy(adj_ref.at[pl.ds(t * TILE, TILE)], adj.at[t], sems.at[t]) for t in range(tiles)]
    for copy in copies:
        copy.start()

    in_t_ref[...] = jnp.transpose(jnp.concatenate([self_ref[...], neigh_ref[...]], axis=0).astype(F32)).astype(BF16)
    wide[...] = jnp.zeros_like(wide)
    wide[0:classes, :] = w_out_ref[...].astype(F32)
    out_t_ref[...] = wide[...].astype(BF16)
    out_ref[...] = jnp.transpose(wide[...]).astype(BF16)
    line[...] = jnp.full_like(line, -1e30)
    line[:, 0:classes] = b_ref[...]
    bias_ref[...] = jnp.transpose(jnp.broadcast_to(line[...], (LANES, line.shape[1])))[0 : bias_ref.shape[0]]

    side = SUB * SUB
    row = _iota((side, side), 0)
    move = ((row % SUB) * SUB + row // SUB == _iota((side, side), 1)).astype(BF16)
    for t in range(tiles):
        copies[t].wait()
        for b in range(TILE // SUB):
            for j in range(neigh // (2 * SUB)):
                halves = [
                    adj[t, SUB * b : SUB * (b + 1), SUB * k : SUB * (k + 1), :].reshape(side, TILE)
                    for k in (2 * j, 2 * j + 1)
                ]
                moved = _dot(move, jnp.concatenate(halves, axis=1)).astype(BF16)
                for h in range(2):
                    k = 2 * j + h
                    turned_ref[t, SUB * k : SUB * (k + 1), SUB * b : SUB * (b + 1), :] = moved[
                        :, TILE * h : TILE * (h + 1)
                    ].reshape(SUB, SUB, TILE)


def prepare(adjacency, w_self, w_neigh, w_out, b_out):
    rows, neigh, tile = adjacency.shape
    width, units = w_self.shape
    classes = w_out.shape[1]
    padded = -(-classes // SUB) * SUB
    tiles = rows // tile
    vmem = pl.BlockSpec(memory_space=pltpu.VMEM)
    return pl.pallas_call(
        prepare_kernel,
        in_specs=[pl.BlockSpec(memory_space=pltpu.HBM), *[vmem] * 4],
        out_specs=[vmem] * 5,
        out_shape=[
            jax.ShapeDtypeStruct((tiles, neigh, tile, tile), BF16),
            jax.ShapeDtypeStruct((units, 2 * width), BF16),
            jax.ShapeDtypeStruct((padded, units), BF16),
            jax.ShapeDtypeStruct((units, padded), BF16),
            jax.ShapeDtypeStruct((padded, LANES), F32),
        ],
        scratch_shapes=[
            pltpu.VMEM((tiles, tile, neigh, tile), BF16),
            pltpu.VMEM((padded, units), F32),
            pltpu.VMEM((1, 2 * LANES), F32),
            pltpu.SemaphoreType.DMA((tiles,)),
        ],
        cost_estimate=pl.CostEstimate(flops=1 << 31, bytes_accessed=1 << 23, transcendentals=0),
        compiler_params=_params(44),
        name="prepare",
    )(adjacency, w_self, w_neigh, w_out.T, b_out.reshape(1, classes))


def aggregate_kernel(devices, *refs):
    blocks = refs[:devices]
    adj, halo_ref, slots_ref, px_ref, labels_ref, agg_ref, got, meta, sems = refs[devices:]
    tiles, neigh = adj.shape[0:2]
    me = lax.axis_index("nodes")
    per = blocks[0].shape[1]
    rows = devices * per
    group = LANES // per

    copies = []
    for m, block in enumerate(blocks):
        owner = me ^ m
        at = pl.ds(pl.multiple_of(owner * per, per), per)
        copies.append(pltpu.make_async_copy(block.at[0:devices], got.at[:, at, :], sems.at[0, m]))
        copies.append(pltpu.make_async_copy(block.at[devices], meta.at[owner], sems.at[1, m]))
    for copy in copies:
        copy.start()
    for copy in copies:
        copy.wait()

    labels_ref[...] = meta[:, SUB : 2 * SUB, :]
    slots = [
        sum(meta[q * group + j, 0:SUB, :].astype(F32) for j in range(group)) for q in range(devices // group)
    ]
    slots = jnp.concatenate(slots, axis=1).astype(jnp.int32)
    position = _iota((rows, rows), 0) - rows // 2
    for p in range(devices):
        put = (position == slots[p : p + 1, :]).astype(BF16)
        px_ref[p * rows : (p + 1) * rows, :] = _dot(put, got[p]).astype(BF16)

    for t in range(tiles):
        total = jnp.zeros((TILE, px_ref.shape[1]), F32)
        for k in range(0, neigh, 2):
            sources = []
            for j in (k, k + 1):
                tile = halo_ref[0, slots_ref[t, j]]
                sources.append(px_ref[pl.ds(pl.multiple_of(tile * TILE, TILE), TILE), :])
            weights = jnp.concatenate([adj[t, k], adj[t, k + 1]], axis=1)
            total += _dot(weights, jnp.concatenate(sources, axis=0))
        agg_ref[t * TILE : (t + 1) * TILE, :] = total.astype(BF16)


def aggregate(blocks, turned, halo_tiles, tile_slots, devices):
    per, width = blocks[0].shape[1:]
    rows = devices * per
    anywhere = pl.BlockSpec(memory_space=pl.ANY)
    scalars = pl.BlockSpec(memory_space=pltpu.SMEM)
    vmem = pl.BlockSpec(memory_space=pltpu.VMEM)
    return pl.pallas_call(
        lambda *refs: aggregate_kernel(devices, *refs),
        in_specs=[anywhere] * devices + [vmem] + [scalars] * 2,
        out_specs=[vmem] * 3,
        out_shape=[
            jax.ShapeDtypeStruct((devices * rows, width), BF16),
            jax.ShapeDtypeStruct((devices, SUB, LANES), BF16),
            jax.ShapeDtypeStruct((rows, width), BF16),
        ],
        scratch_shapes=[
            pltpu.VMEM((devices, rows, width), BF16),
            pltpu.VMEM((devices, 2 * SUB, LANES), BF16),
            pltpu.SemaphoreType.DMA((2, devices)),
        ],
        compiler_params=_params(20),
        name="aggregate",
    )(*blocks, turned, halo_tiles, tile_slots)


def _hot(kinds, labels_ref, owner):
    held = labels_ref[owner].astype(F32)
    return [kinds == held[j : j + 1, :].astype(jnp.int32) for j in range(QUAD)]


def _forward(quad, blocks, px_ref, labels_ref, in_t_ref, out_t_ref, bias_ref, agg_ref, hid_ref, slope_ref, loss_ref, count_ref):
    me = lax.axis_index("nodes")
    rows, width = blocks[0].shape
    for m, block in enumerate(blocks):
        at = ((me % QUAD) ^ m) * rows
        agg_ref[pl.ds(pl.multiple_of(at, rows), rows), :] = block[...]
    kinds = _iota(bias_ref.shape, 0)
    loss = count = jnp.zeros(bias_ref.shape, F32)
    half = QUAD // 2 * rows
    for h in range(2):
        at = slice(h * half, (h + 1) * half)
        x = px_ref[pl.ds(pl.multiple_of(quad * (2 * half) + h * half, half), half), :]
        hidden = jnp.maximum(_dot(in_t_ref[...], jnp.concatenate([x, agg_ref[at, :]], axis=1), NT), 0.0).astype(BF16)
        hid_ref[:, at] = hidden
        logits = _dot(out_t_ref[...], hidden) + jnp.concatenate([bias_ref[...]] * (half // LANES), axis=1)
        logits -= jnp.log(jnp.sum(jnp.exp(logits), axis=0, keepdims=True))
        probs = jnp.exp(logits)
        for o in range(QUAD // 2):
            owner = quad * QUAD + h * (QUAD // 2) + o
            for j, hot in enumerate(_hot(kinds, labels_ref, owner)):
                lane = o * rows + j * LANES
                one = hot.astype(F32)
                loss -= jnp.where(hot, logits[:, lane : lane + LANES], 0.0)
                count += one
                slope_ref[:, h * half + lane : h * half + lane + LANES] = probs[:, lane : lane + LANES] - one
    loss_ref[...], count_ref[...] = loss, count


def forward_kernel(c, *refs):
    me = lax.axis_index("nodes")
    blocks, shared, outs = refs[:QUAD], refs[QUAD : QUAD + 5], refs[QUAD + 5 :]
    _forward((me // QUAD) ^ c, blocks, *shared, *outs[0:5])
    if c == 0:
        px_ref, in_t_ref = shared[0], shared[2]
        rows = blocks[0].shape[0]
        x = px_ref[pl.ds(pl.multiple_of(me * rows, rows), rows), :]
        pre = _dot(jnp.concatenate([x, blocks[0][...]], axis=1), in_t_ref[...], NT)
        outs[5][...] = jnp.maximum(pre, 0.0).astype(BF16)


def _held(rows, width, units, padded):
    return [
        ((QUAD * rows, width), BF16),
        ((units, QUAD * rows), BF16),
        ((padded, QUAD * rows), F32),
        ((padded, LANES), F32),
        ((padded, LANES), F32),
    ]


def forward(have, c, shared):
    rows, width = have[0].shape
    units, padded = shared[2].shape[0], shared[4].shape[0]
    vmem = pl.BlockSpec(memory_space=pltpu.VMEM)
    shapes = [jax.ShapeDtypeStruct(*x) for x in _held(rows, width, units, padded)]
    if c == 0:
        shapes.append(jax.ShapeDtypeStruct((rows, units), BF16))
    return pl.pallas_call(
        lambda *refs: forward_kernel(c, *refs),
        in_specs=[vmem] * (QUAD + 5),
        out_specs=[vmem] * len(shapes),
        out_shape=shapes,
        cost_estimate=pl.CostEstimate(flops=1 << 30, bytes_accessed=1 << 22, transcendentals=1 << 19),
        compiler_params=_params(16),
        name="forward",
    )(*[have[QUAD * c + m] for m in range(QUAD)], *shared)


def backward_kernel(classes, *refs):
    me = lax.axis_index("nodes")
    blocks, refs = refs[:QUAD], refs[QUAD:]
    early, refs = [refs[5 * c : 5 * c + 5] for c in range(QUAD - 1)], refs[5 * (QUAD - 1) :]
    shared, out_ref = refs[0:5], refs[5]
    px_ref, labels_ref, _, _, bias_ref = shared
    self_ref, neigh_ref, grad_out_ref, class_ref = refs[6:10]
    last, refs = refs[10:15], refs[15:]
    losses, counts, grads_in, grads_out = refs
    rows, width = blocks[0].shape
    padded = bias_ref.shape[0]
    mine = me // QUAD
    _forward(mine ^ (QUAD - 1), blocks, *shared, *last)
    held = [*early, last]

    for c in range(QUAD):
        losses[mine ^ c], counts[mine ^ c] = held[c][3][...], held[c][4][...]
    loss = jnp.sum(sum(losses[q] for q in range(QUAD)), axis=1, keepdims=True)
    count = jnp.sum(sum(counts[q] for q in range(QUAD)), axis=1, keepdims=True)
    real = _iota((padded, 1), 0) < classes
    difficulty = jnp.where(real, (loss + 1.0) / (count + 1.0), 0.0)
    weight = difficulty / (jnp.sum(difficulty, axis=0, keepdims=True) / classes)
    share = 1.0 / (1.0 + jnp.sum(count, axis=0, keepdims=True))
    class_ref[...] = jnp.transpose(jnp.broadcast_to(weight, (padded, LANES)))[0:1, 0:classes]
    scaled = jnp.broadcast_to(weight * share, (padded, LANES))

    kinds = _iota(bias_ref.shape, 0)
    half = QUAD // 2 * rows
    for c, (agg_ref, hid_ref, slope_ref, _, _) in enumerate(held):
        quad = mine ^ c
        grad_in = grad_out = 0.0
        for h in range(2):
            at = slice(h * half, (h + 1) * half)
            parts = []
            for o in range(QUAD // 2):
                for j, hot in enumerate(_hot(kinds, labels_ref, quad * QUAD + h * (QUAD // 2) + o)):
                    row = jnp.sum(jnp.where(hot, scaled, 0.0), axis=0, keepdims=True)
                    lane = h * half + o * rows + j * LANES
                    parts.append((row * slope_ref[:, lane : lane + LANES]).astype(BF16))
            dlogits = jnp.concatenate(parts, axis=1)
            hidden = hid_ref[:, at]
            dpre = jnp.where(hidden > 0, _dot(out_ref[...], dlogits), 0.0).astype(BF16)
            x = px_ref[pl.ds(pl.multiple_of(quad * (2 * half) + h * half, half), half), :]
            grad_out += _dot(dlogits, hidden, NT)
            grad_in += _dot(dpre, jnp.concatenate([x, agg_ref[at, :]], axis=1))
        grads_in[quad], grads_out[quad] = grad_in, grad_out

    grad_out_ref[...] = sum(grads_out[q] for q in range(QUAD))[0:classes]
    grad_in = jnp.transpose(sum(grads_in[q] for q in range(QUAD)))
    self_ref[...] = grad_in[0:width]
    neigh_ref[...] = grad_in[width : 2 * width]


def backward(have, early, shared, out_p, classes):
    rows, width = have[0].shape
    units, padded = out_p.shape
    vmem = pl.BlockSpec(memory_space=pltpu.VMEM)
    operands = [*[have[m] for m in range(DEVICES - QUAD, DEVICES)], *[x for held in early for x in held], *shared, out_p]
    return pl.pallas_call(
        lambda *refs: backward_kernel(classes, *refs),
        in_specs=[vmem] * len(operands),
        out_specs=[vmem] * 4,
        out_shape=[
            jax.ShapeDtypeStruct((width, units), F32),
            jax.ShapeDtypeStruct((width, units), F32),
            jax.ShapeDtypeStruct((classes, units), F32),
            jax.ShapeDtypeStruct((1, classes), F32),
        ],
        scratch_shapes=[
            *[pltpu.VMEM(*x) for x in _held(rows, width, units, padded)],
            pltpu.VMEM((QUAD, padded, LANES), F32),
            pltpu.VMEM((QUAD, padded, LANES), F32),
            pltpu.VMEM((QUAD, units, 2 * width), F32),
            pltpu.VMEM((QUAD, padded, units), F32),
        ],
        compiler_params=_params(24),
        name="backward",
    )(*operands)


def gathered_body(
    features, cluster, slot, halo_tiles, tile_slots, adjacency, labels, w_self, w_neigh, w_out, b_out
):
    packed = pack(features, cluster, slot, labels, DEVICES)
    have, done = gather_all(packed, [lambda _: prepare(adjacency, w_self, w_neigh, w_out, b_out)])
    turned, in_t, out_t, out_p, bias = done[0]
    blocks = [have[m] for m in range(DEVICES)]
    part_x, all_labels, agg = aggregate(blocks, turned, halo_tiles, tile_slots, DEVICES)
    shared = (part_x, all_labels, in_t, out_t, bias)
    have, done = gather_all(agg, [lambda have, c=c: forward(have, c, shared) for c in range(QUAD - 1)])
    hidden = done[0][5]
    early = [out[0:5] for out in done]
    grad_self, grad_neigh, grad_out, class_weight = backward(have, early, shared, out_p, w_out.shape[1])
    return hidden, grad_self, grad_neigh, grad_out.T, class_weight.reshape(-1)


def split_body(
    features, cluster, slot, halo_tiles, tile_slots, adjacency, labels, w_self, w_neigh, w_out, b_out
):
    rows = features.shape[0]
    width = features.shape[1]
    devices = lax.axis_size("nodes")
    per_peer = rows // devices
    order = jnp.argsort(cluster, stable=True)
    send_rows = features[order].reshape(devices, per_peer, width)
    send_slots = slot[order].reshape(devices, per_peer)
    recv_rows, recv_slots = (
        lax.all_to_all(send_rows, "nodes", split_axis=0, concat_axis=0, tiled=True),
        lax.all_to_all(send_slots, "nodes", split_axis=0, concat_axis=0, tiled=True),
    )
    part_x = (
        jnp.zeros((rows, width), jnp.bfloat16)
        .at[recv_slots.reshape(rows)]
        .set(recv_rows.reshape(rows, width))
    )
    local_tiles = rows // TILE
    wanted = halo_tiles[0]
    gathered = lax.all_gather(part_x, "nodes", axis=0, tiled=True)
    halo = gathered.reshape(-1, TILE, width)[wanted]
    sources = halo[tile_slots]
    adj_tiles = adjacency.reshape(local_tiles, TILE, adjacency.shape[1], TILE)
    agg = jnp.einsum("tikc,tkcf->tif", adj_tiles, sources, preferred_element_type=jnp.float32)
    agg = agg.reshape(rows, width).astype(jnp.bfloat16)
    pre = jnp.dot(part_x, w_self, preferred_element_type=jnp.float32) + jnp.dot(
        agg, w_neigh, preferred_element_type=jnp.float32
    )
    hidden = jnp.maximum(pre, 0.0).astype(jnp.bfloat16)
    logits = jnp.dot(hidden, w_out, preferred_element_type=jnp.float32) + b_out
    lse = jnp.log(jnp.sum(jnp.exp(logits), axis=1))
    classes_row = jnp.arange(w_out.shape[1], dtype=jnp.int32)
    onehot = (labels[:, None] == classes_row[None, :]).astype(jnp.float32)
    picked = jnp.sum(onehot * logits, axis=1)
    ce_rows = lse - picked
    local_loss = jnp.sum(onehot * ce_rows[:, None], axis=0)
    local_counts = jnp.sum(onehot, axis=0)
    loss_sum, counts = lax.psum((local_loss, local_counts), "nodes")
    difficulty = (loss_sum + 1.0) / (counts + 1.0)
    class_weight = difficulty / jnp.mean(difficulty)
    total = jnp.sum(counts)
    row_weight = jnp.sum(onehot * class_weight[None, :], axis=1) / (total + 1.0)
    probs = jnp.exp(logits - lse[:, None])
    dlogits = (row_weight[:, None] * (probs - onehot)).astype(jnp.bfloat16)
    part_out = jnp.dot(hidden.T, dlogits, preferred_element_type=jnp.float32)
    dhidden = jnp.dot(dlogits, w_out.T, preferred_element_type=jnp.float32)
    dpre = jnp.where(hidden > 0, dhidden, 0.0).astype(jnp.bfloat16)
    part_self = jnp.dot(part_x.T, dpre, preferred_element_type=jnp.float32)
    part_neigh = jnp.dot(agg.T, dpre, preferred_element_type=jnp.float32)
    grad_self, grad_neigh, grad_out = lax.psum((part_self, part_neigh, part_out), "nodes")
    return (hidden, grad_self, grad_neigh, grad_out, class_weight)


def solution(mesh):
    def body(*args):
        devices = mesh.shape["nodes"]
        rows = args[0].shape[0]
        per = rows // devices
        classes = args[9].shape[1]
        fits = devices == DEVICES and per == 2 * SUB and classes <= 256
        return (gathered_body if fits else split_body)(*args)

    return jax.shard_map(
        body,
        mesh=mesh,
        in_specs=(
            P(("groups", "nodes"), None),
            P(("groups", "nodes")),
            P(("groups", "nodes")),
            P(("groups", "nodes"), None),
            P(("groups", "nodes"), None),
            P(("groups", "nodes"), None, None),
            P(("groups", "nodes")),
            P(),
            P(),
            P(),
            P(),
        ),
        out_specs=(
            P(("groups", "nodes"), None),
            P("groups", None),
            P("groups", None),
            P("groups", None),
            P("groups"),
        ),
        check_vma=False,
    )
```

```python
import jax
import jax.numpy as jnp
from jax import lax
from jax.experimental import pallas as pl
from jax.experimental.pallas import tpu as pltpu
from jax.sharding import PartitionSpec as P

DEVICES = 16
QUAD = 4
TILE = 128
LANES = 128
SUB = 16
F32 = jnp.float32
BF16 = jnp.bfloat16


def _dot(a, b, contract=((1,), (0,))):
    return lax.dot_general(a, b, (contract, ((), ())), preferred_element_type=F32)


NT = ((1,), (1,))


def _iota(shape, dim):
    return lax.broadcasted_iota(jnp.int32, shape, dim)


def _stay(x):
    return pltpu.with_memory_space_constraint(x, pltpu.HBM)


def _fetch(sources, targets, sems):
    copies = [pltpu.make_async_copy(a, b, sems.at[i]) for i, (a, b) in enumerate(zip(sources, targets))]
    for copy in copies:
        copy.start()
    for copy in copies:
        copy.wait()


def _params(mib):
    return pltpu.CompilerParams(vmem_limit_bytes=mib << 20)


def swap(x, m):
    return lax.ppermute(x, "nodes", [(i, i ^ m) for i in range(DEVICES)])


def gather_all(block, work):
    have = {0: block}
    done = []

    def hop(i, m):
        if work[i] is not None:
            have[m], out = lax.optimization_barrier((have[m], work[i](have)))
            done.append(out)

    have[8], have[4], have[2], have[1] = (swap(block, m) for m in (8, 4, 2, 1))
    hop(0, 8)
    have[12], have[10], have[6] = swap(have[8], 4), swap(have[8], 2), swap(have[4], 2)
    have[3], have[5], have[7], have[9] = (swap(have[m], 1) for m in (2, 4, 6, 8))
    hop(1, 12)
    have[14] = swap(have[12], 2)
    have[11], have[13] = swap(have[10], 1), swap(have[12], 1)
    hop(2, 14)
    have[15] = swap(have[14], 1)
    done.extend(w(have) for w in work[3:])
    return have, done


def pack_kernel(devices, *refs):
    sources, out_ref, targets, sems = refs[0:4], refs[4], refs[5:9], refs[9]
    _fetch(sources, targets, sems)
    feat_ref, cluster_ref, slot_ref, label_ref = targets
    rows = feat_ref.shape[0]
    per = rows // devices
    mine = lax.axis_index("nodes") % (LANES // per)
    cluster = cluster_ref[...]
    member = (_iota((devices, rows), 0) == cluster).astype(F32)
    before = (_iota((rows, rows), 0) < _iota((rows, rows), 1)).astype(BF16)
    rank = jnp.sum(member * _dot(member.astype(BF16), before), axis=0, keepdims=True).astype(jnp.int32)
    take = (_iota((rows, rows), 0) == cluster * per + rank).astype(BF16)
    out_ref[0:devices] = _dot(take, feat_ref[...]).astype(BF16).reshape(devices, per, feat_ref.shape[1])
    place = (_iota((LANES, rows), 0) == mine * per + rank).astype(BF16)
    slots = (member * (slot_ref[...] - rows // 2).astype(F32)).astype(BF16)
    out_ref[devices, 0:SUB] = _dot(slots, place, NT).astype(BF16)
    labels = jnp.concatenate([label_ref[...].astype(F32), jnp.zeros((SUB - label_ref.shape[0], LANES), F32)], axis=0)
    out_ref[devices, SUB : 2 * SUB] = labels.astype(BF16)


def pack(features, cluster, slot, labels, devices):
    rows, width = features.shape
    per = rows // devices
    inputs = (features, cluster.reshape(1, rows), slot.reshape(1, rows), labels.reshape(rows // LANES, LANES))
    inputs = [_stay(x) for x in inputs]
    return pl.pallas_call(
        lambda *refs: pack_kernel(devices, *refs),
        in_specs=[pl.BlockSpec(memory_space=pltpu.HBM)] * 4,
        out_specs=pl.BlockSpec(memory_space=pltpu.VMEM),
        out_shape=jax.ShapeDtypeStruct((devices + 1, per, width), BF16),
        scratch_shapes=[*[pltpu.VMEM(x.shape, x.dtype) for x in inputs], pltpu.SemaphoreType.DMA((4,))],
        compiler_params=_params(8),
        name="pack_rows",
    )(*inputs)


def weights_kernel(*refs):
    sources, (in_t_ref, out_t_ref, out_ref, bias_ref), targets = refs[0:4], refs[4:8], refs[8:12]
    wide, line, sems = refs[12:15]
    _fetch(sources, targets, sems)
    self_ref, neigh_ref, w_out_ref, b_ref = targets
    classes = w_out_ref.shape[0]
    in_t_ref[...] = jnp.transpose(jnp.concatenate([self_ref[...], neigh_ref[...]], axis=0).astype(F32)).astype(BF16)
    wide[...] = jnp.zeros_like(wide)
    wide[0:classes, :] = w_out_ref[...].astype(F32)
    out_t_ref[...] = wide[...].astype(BF16)
    out_ref[...] = jnp.transpose(wide[...]).astype(BF16)
    line[...] = jnp.full_like(line, -1e30)
    line[:, 0:classes] = b_ref[...]
    bias_ref[...] = jnp.transpose(jnp.broadcast_to(line[...], (LANES, line.shape[1])))[0 : bias_ref.shape[0]]


def weights(w_self, w_neigh, w_out, b_out):
    width, units = w_self.shape
    classes = w_out.shape[1]
    padded = -(-classes // SUB) * SUB
    inputs = [_stay(x) for x in (w_self, w_neigh, w_out.T, b_out.reshape(1, classes))]
    return pl.pallas_call(
        weights_kernel,
        in_specs=[pl.BlockSpec(memory_space=pltpu.HBM)] * 4,
        out_specs=[pl.BlockSpec(memory_space=pltpu.VMEM)] * 4,
        out_shape=[
            jax.ShapeDtypeStruct((units, 2 * width), BF16),
            jax.ShapeDtypeStruct((padded, units), BF16),
            jax.ShapeDtypeStruct((units, padded), BF16),
            jax.ShapeDtypeStruct((padded, LANES), F32),
        ],
        scratch_shapes=[
            *[pltpu.VMEM(x.shape, x.dtype) for x in inputs],
            pltpu.VMEM((padded, units), F32),
            pltpu.VMEM((1, 2 * LANES), F32),
            pltpu.SemaphoreType.DMA((4,)),
        ],
        cost_estimate=pl.CostEstimate(flops=0, bytes_accessed=1 << 21, transcendentals=0),
        compiler_params=_params(8),
        name="weights",
    )(*inputs)


def turn_kernel(first, adj_ref, turned_ref, adj, sems):
    tiles, neigh = turned_ref.shape[0:2]
    pieces = sems.shape[1]
    part = TILE // pieces
    copies = [
        [
            pltpu.make_async_copy(
                adj_ref.at[pl.ds((first + t) * TILE + i * part, part)], adj.at[t, pl.ds(i * part, part)], sems.at[t, i]
            )
            for i in range(pieces)
        ]
        for t in range(tiles)
    ]
    for copy in sum(copies, []):
        copy.start()
    side = SUB * SUB
    row = _iota((side, side), 0)
    move = ((row % SUB) * SUB + row // SUB == _iota((side, side), 1)).astype(BF16)
    for t in range(tiles):
        for b in range(TILE // SUB):
            if b * SUB % part == 0:
                copies[t][b * SUB // part].wait()
            for j in range(neigh // (2 * SUB)):
                halves = [
                    adj[t, SUB * b : SUB * (b + 1), SUB * k : SUB * (k + 1), :].reshape(side, TILE)
                    for k in (2 * j, 2 * j + 1)
                ]
                moved = _dot(move, jnp.concatenate(halves, axis=1)).astype(BF16)
                for h in range(2):
                    k = 2 * j + h
                    turned_ref[t, SUB * k : SUB * (k + 1), SUB * b : SUB * (b + 1), :] = moved[
                        :, TILE * h : TILE * (h + 1)
                    ].reshape(SUB, SUB, TILE)


def turn(adjacency, first, tiles):
    _, neigh, tile = adjacency.shape
    pieces = 2
    return pl.pallas_call(
        lambda *refs: turn_kernel(first, *refs),
        in_specs=[pl.BlockSpec(memory_space=pltpu.HBM)],
        out_specs=pl.BlockSpec(memory_space=pltpu.VMEM),
        out_shape=jax.ShapeDtypeStruct((tiles, neigh, tile, tile), BF16),
        scratch_shapes=[pltpu.VMEM((tiles, tile, neigh, tile), BF16), pltpu.SemaphoreType.DMA((tiles, pieces))],
        cost_estimate=pl.CostEstimate(flops=tiles << 29, bytes_accessed=tiles << 21, transcendentals=0),
        compiler_params=_params(16),
        name="turn_adjacency",
    )(_stay(adjacency))


def _place(ms, blocks, prior, px_ref, labels_ref, got):
    me = lax.axis_index("nodes")
    per = blocks[0].shape[1]
    rows = DEVICES * per
    if prior:
        labels_ref[...] = prior[1][...]
    slots = []
    for q in range(len(ms) // QUAD):
        held = 0.0
        for m, block in list(zip(ms, blocks))[q * QUAD : (q + 1) * QUAD]:
            at = q * LANES + ((me % QUAD) ^ (m % QUAD)) * per
            got[:, pl.ds(pl.multiple_of(at, per), per), :] = block[0:DEVICES]
            held += block[DEVICES, 0:SUB, :].astype(F32)
            labels_ref[me ^ m] = block[DEVICES, SUB : 2 * SUB, :]
        slots.append(held)
    slots = jnp.concatenate(slots, axis=1).astype(jnp.int32)
    position = _iota((rows, slots.shape[1]), 0) - rows // 2
    for p in range(DEVICES):
        put = (position == slots[p : p + 1, :]).astype(BF16)
        placed = _dot(put, got[p])
        if prior:
            placed += prior[0][p * rows : (p + 1) * rows, :].astype(F32)
        px_ref[p * rows : (p + 1) * rows, :] = placed.astype(BF16)


def _placed(per, width):
    return [
        jax.ShapeDtypeStruct((DEVICES * DEVICES * per, width), BF16),
        jax.ShapeDtypeStruct((DEVICES, SUB, LANES), BF16),
    ]


def place(have, ms):
    per, width = have[0].shape[1:]
    vmem = pl.BlockSpec(memory_space=pltpu.VMEM)
    return pl.pallas_call(
        lambda *refs: _place(ms, refs[: len(ms)], None, *refs[len(ms) :]),
        in_specs=[vmem] * len(ms),
        out_specs=[vmem] * 2,
        out_shape=_placed(per, width),
        scratch_shapes=[pltpu.VMEM((DEVICES, len(ms) * per, width), BF16)],
        cost_estimate=pl.CostEstimate(flops=1 << 30, bytes_accessed=1 << 22, transcendentals=0),
        compiler_params=_params(16),
        name="place",
    )(*[have[m] for m in ms])


def aggregate_kernel(ms, parts, *refs):
    n = len(ms)
    blocks, prior, turned, refs = refs[:n], refs[n : n + 2], refs[n + 2 : n + 2 + parts], refs[n + 2 + parts :]
    halo_ref, slots_ref, px_ref, labels_ref, agg_ref, got = refs
    _place(ms, blocks, prior, px_ref, labels_ref, got)
    neigh = slots_ref.shape[1]
    tiles = [ref.at[t] for ref in turned for t in range(ref.shape[0])]
    for t, adj in enumerate(tiles):
        total = jnp.zeros((TILE, px_ref.shape[1]), F32)
        for k in range(0, neigh, 2):
            sources = []
            for j in (k, k + 1):
                tile = halo_ref[0, slots_ref[t, j]]
                sources.append(px_ref[pl.ds(pl.multiple_of(tile * TILE, TILE), TILE), :])
            total += _dot(jnp.concatenate([adj[k], adj[k + 1]], axis=1), jnp.concatenate(sources, axis=0))
        agg_ref[t * TILE : (t + 1) * TILE, :] = total.astype(BF16)


def aggregate(have, ms, prior, turned, halo_tiles, tile_slots):
    per, width = have[0].shape[1:]
    scalars = pl.BlockSpec(memory_space=pltpu.SMEM)
    vmem = pl.BlockSpec(memory_space=pltpu.VMEM)
    return pl.pallas_call(
        lambda *refs: aggregate_kernel(ms, len(turned), *refs),
        in_specs=[vmem] * (len(ms) + 2 + len(turned)) + [scalars] * 2,
        out_specs=[vmem] * 3,
        out_shape=[*_placed(per, width), jax.ShapeDtypeStruct((DEVICES * per, width), BF16)],
        scratch_shapes=[pltpu.VMEM((DEVICES, len(ms) * per, width), BF16)],
        compiler_params=_params(24),
        name="aggregate",
    )(*[have[m] for m in ms], *prior, *turned, halo_tiles, tile_slots)


def _hot(kinds, labels_ref, owner):
    held = labels_ref[owner].astype(F32)
    return [kinds == held[j : j + 1, :].astype(jnp.int32) for j in range(QUAD)]


def _forward(quad, blocks, px_ref, labels_ref, in_t_ref, out_t_ref, bias_ref, agg_ref, hid_ref, slope_ref, loss_ref, count_ref):
    me = lax.axis_index("nodes")
    rows, width = blocks[0].shape
    for m, block in enumerate(blocks):
        at = ((me % QUAD) ^ m) * rows
        agg_ref[pl.ds(pl.multiple_of(at, rows), rows), :] = block[...]
    kinds = _iota(bias_ref.shape, 0)
    loss = count = jnp.zeros(bias_ref.shape, F32)
    half = QUAD // 2 * rows
    for h in range(2):
        at = slice(h * half, (h + 1) * half)
        x = px_ref[pl.ds(pl.multiple_of(quad * (2 * half) + h * half, half), half), :]
        hidden = jnp.maximum(_dot(in_t_ref[...], jnp.concatenate([x, agg_ref[at, :]], axis=1), NT), 0.0).astype(BF16)
        hid_ref[:, at] = hidden
        logits = _dot(out_t_ref[...], hidden) + jnp.concatenate([bias_ref[...]] * (half // LANES), axis=1)
        logits -= jnp.log(jnp.sum(jnp.exp(logits), axis=0, keepdims=True))
        probs = jnp.exp(logits)
        for o in range(QUAD // 2):
            owner = quad * QUAD + h * (QUAD // 2) + o
            for j, hot in enumerate(_hot(kinds, labels_ref, owner)):
                lane = o * rows + j * LANES
                one = hot.astype(F32)
                loss -= jnp.where(hot, logits[:, lane : lane + LANES], 0.0)
                count += one
                slope_ref[:, h * half + lane : h * half + lane + LANES] = probs[:, lane : lane + LANES] - one
    loss_ref[...], count_ref[...] = loss, count


def forward_kernel(c, *refs):
    me = lax.axis_index("nodes")
    blocks, shared, outs = refs[:QUAD], refs[QUAD : QUAD + 5], refs[QUAD + 5 :]
    _forward((me // QUAD) ^ c, blocks, *shared, *outs[0:5])
    if c == 0:
        px_ref, in_t_ref = shared[0], shared[2]
        rows = blocks[0].shape[0]
        x = px_ref[pl.ds(pl.multiple_of(me * rows, rows), rows), :]
        pre = _dot(jnp.concatenate([x, blocks[0][...]], axis=1), in_t_ref[...], NT)
        outs[5][...] = jnp.maximum(pre, 0.0).astype(BF16)


def _held(rows, width, units, padded):
    return [
        ((QUAD * rows, width), BF16),
        ((units, QUAD * rows), BF16),
        ((padded, QUAD * rows), F32),
        ((padded, LANES), F32),
        ((padded, LANES), F32),
    ]


def forward(have, c, shared):
    rows, width = have[0].shape
    units, padded = shared[2].shape[0], shared[4].shape[0]
    vmem = pl.BlockSpec(memory_space=pltpu.VMEM)
    shapes = [jax.ShapeDtypeStruct(*x) for x in _held(rows, width, units, padded)]
    if c == 0:
        shapes.append(jax.ShapeDtypeStruct((rows, units), BF16))
    return pl.pallas_call(
        lambda *refs: forward_kernel(c, *refs),
        in_specs=[vmem] * (QUAD + 5),
        out_specs=[vmem] * len(shapes),
        out_shape=shapes,
        cost_estimate=pl.CostEstimate(flops=1 << 30, bytes_accessed=1 << 22, transcendentals=1 << 19),
        compiler_params=_params(16),
        name="forward",
    )(*[have[QUAD * c + m] for m in range(QUAD)], *shared)


def backward_kernel(classes, *refs):
    me = lax.axis_index("nodes")
    blocks, refs = refs[:QUAD], refs[QUAD:]
    early, refs = [refs[5 * c : 5 * c + 5] for c in range(QUAD - 1)], refs[5 * (QUAD - 1) :]
    shared, out_ref = refs[0:5], refs[5]
    px_ref, labels_ref, _, _, bias_ref = shared
    self_ref, neigh_ref, grad_out_ref, class_ref = refs[6:10]
    last, refs = refs[10:15], refs[15:]
    losses, counts, grads_in, grads_out = refs
    rows, width = blocks[0].shape
    padded = bias_ref.shape[0]
    mine = me // QUAD
    _forward(mine ^ (QUAD - 1), blocks, *shared, *last)
    held = [*early, last]

    for c in range(QUAD):
        losses[mine ^ c], counts[mine ^ c] = held[c][3][...], held[c][4][...]
    loss = jnp.sum(sum(losses[q] for q in range(QUAD)), axis=1, keepdims=True)
    count = jnp.sum(sum(counts[q] for q in range(QUAD)), axis=1, keepdims=True)
    real = _iota((padded, 1), 0) < classes
    difficulty = jnp.where(real, (loss + 1.0) / (count + 1.0), 0.0)
    weight = difficulty / (jnp.sum(difficulty, axis=0, keepdims=True) / classes)
    share = 1.0 / (1.0 + jnp.sum(count, axis=0, keepdims=True))
    class_ref[...] = jnp.transpose(jnp.broadcast_to(weight, (padded, LANES)))[0:1, 0:classes]
    scaled = jnp.broadcast_to(weight * share, (padded, LANES))

    kinds = _iota(bias_ref.shape, 0)
    half = QUAD // 2 * rows
    for c, (agg_ref, hid_ref, slope_ref, _, _) in enumerate(held):
        quad = mine ^ c
        grad_in = grad_out = 0.0
        for h in range(2):
            at = slice(h * half, (h + 1) * half)
            parts = []
            for o in range(QUAD // 2):
                for j, hot in enumerate(_hot(kinds, labels_ref, quad * QUAD + h * (QUAD // 2) + o)):
                    row = jnp.sum(jnp.where(hot, scaled, 0.0), axis=0, keepdims=True)
                    lane = h * half + o * rows + j * LANES
                    parts.append((row * slope_ref[:, lane : lane + LANES]).astype(BF16))
            dlogits = jnp.concatenate(parts, axis=1)
            hidden = hid_ref[:, at]
            dpre = jnp.where(hidden > 0, _dot(out_ref[...], dlogits), 0.0).astype(BF16)
            x = px_ref[pl.ds(pl.multiple_of(quad * (2 * half) + h * half, half), half), :]
            grad_out += _dot(dlogits, hidden, NT)
            grad_in += _dot(dpre, jnp.concatenate([x, agg_ref[at, :]], axis=1))
        grads_in[quad], grads_out[quad] = grad_in, grad_out

    grad_out_ref[...] = sum(grads_out[q] for q in range(QUAD))[0:classes]
    grad_in = jnp.transpose(sum(grads_in[q] for q in range(QUAD)))
    self_ref[...] = grad_in[0:width]
    neigh_ref[...] = grad_in[width : 2 * width]


def backward(have, early, shared, out_p, classes):
    rows, width = have[0].shape
    units, padded = out_p.shape
    vmem = pl.BlockSpec(memory_space=pltpu.VMEM)
    operands = [*[have[m] for m in range(DEVICES - QUAD, DEVICES)], *[x for held in early for x in held], *shared, out_p]
    return pl.pallas_call(
        lambda *refs: backward_kernel(classes, *refs),
        in_specs=[vmem] * len(operands),
        out_specs=[vmem] * 4,
        out_shape=[
            jax.ShapeDtypeStruct((width, units), F32),
            jax.ShapeDtypeStruct((width, units), F32),
            jax.ShapeDtypeStruct((classes, units), F32),
            jax.ShapeDtypeStruct((1, classes), F32),
        ],
        scratch_shapes=[
            *[pltpu.VMEM(*x) for x in _held(rows, width, units, padded)],
            pltpu.VMEM((QUAD, padded, LANES), F32),
            pltpu.VMEM((QUAD, padded, LANES), F32),
            pltpu.VMEM((QUAD, units, 2 * width), F32),
            pltpu.VMEM((QUAD, padded, units), F32),
        ],
        compiler_params=_params(24),
        name="backward",
    )(*operands)


def gathered_body(
    features, cluster, slot, halo_tiles, tile_slots, adjacency, labels, w_self, w_neigh, w_out, b_out
):
    packed = pack(features, cluster, slot, labels, DEVICES)
    early, late = tuple(range(0, 8)), tuple(range(8, 16))
    half = features.shape[0] // TILE // 2
    work = [
        lambda have: turn(adjacency, 0, half),
        None,
        lambda have: (place(have, early), turn(adjacency, half, half)),
    ]
    have, (near, (prior, far)) = gather_all(packed, work)
    part_x, all_labels, agg = aggregate(have, late, prior, (near, far), halo_tiles, tile_slots)
    ready = []

    def quad(have, c):
        in_t, out_t, _, bias = ready[0]
        return forward(have, c, (part_x, all_labels, in_t, out_t, bias))

    def prepare(have):
        ready.append(weights(w_self, w_neigh, w_out, b_out))
        return ready[0]

    have, (_, *done) = gather_all(agg, [prepare, *[lambda have, c=c: quad(have, c) for c in range(QUAD - 1)]])
    in_t, out_t, out_p, bias = ready[0]
    shared = (part_x, all_labels, in_t, out_t, bias)
    hidden = done[0][5]
    early = [out[0:5] for out in done]
    grad_self, grad_neigh, grad_out, class_weight = backward(have, early, shared, out_p, w_out.shape[1])
    return hidden, grad_self, grad_neigh, grad_out.T, class_weight.reshape(-1)


def split_body(
    features, cluster, slot, halo_tiles, tile_slots, adjacency, labels, w_self, w_neigh, w_out, b_out
):
    rows = features.shape[0]
    width = features.shape[1]
    devices = lax.axis_size("nodes")
    per_peer = rows // devices
    order = jnp.argsort(cluster, stable=True)
    send_rows = features[order].reshape(devices, per_peer, width)
    send_slots = slot[order].reshape(devices, per_peer)
    recv_rows, recv_slots = (
        lax.all_to_all(send_rows, "nodes", split_axis=0, concat_axis=0, tiled=True),
        lax.all_to_all(send_slots, "nodes", split_axis=0, concat_axis=0, tiled=True),
    )
    part_x = (
        jnp.zeros((rows, width), jnp.bfloat16)
        .at[recv_slots.reshape(rows)]
        .set(recv_rows.reshape(rows, width))
    )
    local_tiles = rows // TILE
    wanted = halo_tiles[0]
    gathered = lax.all_gather(part_x, "nodes", axis=0, tiled=True)
    halo = gathered.reshape(-1, TILE, width)[wanted]
    sources = halo[tile_slots]
    adj_tiles = adjacency.reshape(local_tiles, TILE, adjacency.shape[1], TILE)
    agg = jnp.einsum("tikc,tkcf->tif", adj_tiles, sources, preferred_element_type=jnp.float32)
    agg = agg.reshape(rows, width).astype(jnp.bfloat16)
    pre = jnp.dot(part_x, w_self, preferred_element_type=jnp.float32) + jnp.dot(
        agg, w_neigh, preferred_element_type=jnp.float32
    )
    hidden = jnp.maximum(pre, 0.0).astype(jnp.bfloat16)
    logits = jnp.dot(hidden, w_out, preferred_element_type=jnp.float32) + b_out
    lse = jnp.log(jnp.sum(jnp.exp(logits), axis=1))
    classes_row = jnp.arange(w_out.shape[1], dtype=jnp.int32)
    onehot = (labels[:, None] == classes_row[None, :]).astype(jnp.float32)
    picked = jnp.sum(onehot * logits, axis=1)
    ce_rows = lse - picked
    local_loss = jnp.sum(onehot * ce_rows[:, None], axis=0)
    local_counts = jnp.sum(onehot, axis=0)
    loss_sum, counts = lax.psum((local_loss, local_counts), "nodes")
    difficulty = (loss_sum + 1.0) / (counts + 1.0)
    class_weight = difficulty / jnp.mean(difficulty)
    total = jnp.sum(counts)
    row_weight = jnp.sum(onehot * class_weight[None, :], axis=1) / (total + 1.0)
    probs = jnp.exp(logits - lse[:, None])
    dlogits = (row_weight[:, None] * (probs - onehot)).astype(jnp.bfloat16)
    part_out = jnp.dot(hidden.T, dlogits, preferred_element_type=jnp.float32)
    dhidden = jnp.dot(dlogits, w_out.T, preferred_element_type=jnp.float32)
    dpre = jnp.where(hidden > 0, dhidden, 0.0).astype(jnp.bfloat16)
    part_self = jnp.dot(part_x.T, dpre, preferred_element_type=jnp.float32)
    part_neigh = jnp.dot(agg.T, dpre, preferred_element_type=jnp.float32)
    grad_self, grad_neigh, grad_out = lax.psum((part_self, part_neigh, part_out), "nodes")
    return (hidden, grad_self, grad_neigh, grad_out, class_weight)


def solution(mesh):
    def body(*args):
        devices = mesh.shape["nodes"]
        rows = args[0].shape[0]
        per = rows // devices
        classes = args[9].shape[1]
        fits = devices == DEVICES and per == 2 * SUB and classes <= 256
        return (gathered_body if fits else split_body)(*args)

    return jax.shard_map(
        body,
        mesh=mesh,
        in_specs=(
            P(("groups", "nodes"), None),
            P(("groups", "nodes")),
            P(("groups", "nodes")),
            P(("groups", "nodes"), None),
            P(("groups", "nodes"), None),
            P(("groups", "nodes"), None, None),
            P(("groups", "nodes")),
            P(),
            P(),
            P(),
            P(),
        ),
        out_specs=(
            P(("groups", "nodes"), None),
            P("groups", None),
            P("groups", None),
            P("groups", None),
            P("groups"),
        ),
        check_vma=False,
    )
```

```python
import jax
import jax.numpy as jnp
from jax import lax
from jax.experimental import pallas as pl
from jax.experimental.pallas import tpu as pltpu
from jax.sharding import PartitionSpec as P

DEVICES = 16
QUAD = 4
TILE = 128
LANES = 128
SUB = 16
F32 = jnp.float32
BF16 = jnp.bfloat16


def _dot(a, b, contract=((1,), (0,))):
    return lax.dot_general(a, b, (contract, ((), ())), preferred_element_type=F32)


NT = ((1,), (1,))


def _iota(shape, dim):
    return lax.broadcasted_iota(jnp.int32, shape, dim)


def _stay(x):
    return pltpu.with_memory_space_constraint(x, pltpu.HBM)


def _fetch(sources, targets, sems):
    copies = [pltpu.make_async_copy(a, b, sems.at[i]) for i, (a, b) in enumerate(zip(sources, targets))]
    for copy in copies:
        copy.start()
    for copy in copies:
        copy.wait()


def _params(mib):
    return pltpu.CompilerParams(vmem_limit_bytes=mib << 20)


def swap(x, m):
    return lax.ppermute(x, "nodes", [(i, i ^ m) for i in range(DEVICES)])


def gather_all(block, work, cores=True):
    have = {0: block}
    done = []

    def hop(i, m):
        if work[i] is not None:
            have[m], out = lax.optimization_barrier((have[m], work[i](have)))
            done.append(out)

    def cross(*ms):
        if cores:
            have.update({m + 1: swap(have[m], 1) for m in ms})

    have[8], have[4], have[2] = (swap(block, m) for m in (8, 4, 2))
    cross(0)
    hop(0, 8)
    have[12], have[10], have[6] = swap(have[8], 4), swap(have[8], 2), swap(have[4], 2)
    cross(2, 4, 6, 8)
    hop(1, 12)
    have[14] = swap(have[12], 2)
    cross(10, 12)
    hop(2, 14)
    cross(14)
    return have, done


def gather_plane(block, first, second):
    have = {0: block}
    have[8], have[4], have[2], have[6] = (swap(block, m) for m in (8, 4, 2, 6))
    have[8], one = lax.optimization_barrier((have[8], first(have)))
    have[12], have[10], have[14] = swap(have[8], 4), swap(have[8], 2), swap(have[8], 6)
    have[14], two = lax.optimization_barrier((have[14], second(have)))
    return have, one, two


def gather_rows(block, first, second):
    have = {0: block}
    have[8], have[4], have[2] = (swap(block, m) for m in (8, 4, 2))
    (have[8], have[4], have[2]), one = lax.optimization_barrier(((have[8], have[4], have[2]), first(have)))
    have[12], have[10], have[6] = swap(have[8], 4), swap(have[8], 2), swap(have[4], 2)
    have[1], have[3], have[5], have[7], have[9] = (swap(have[m], 1) for m in (0, 2, 4, 6, 8))
    have[14] = swap(have[12], 2)
    have[11], have[13] = swap(have[10], 1), swap(have[12], 1)
    have[14], two = lax.optimization_barrier((have[14], second(have)))
    have[15] = swap(have[14], 1)
    return have, one, two


def pack_kernel(devices, *refs):
    sources, out_ref, targets, sems = refs[0:4], refs[4], refs[5:9], refs[9]
    _fetch(sources, targets, sems)
    feat_ref, cluster_ref, slot_ref, label_ref = targets
    rows = feat_ref.shape[0]
    per = rows // devices
    mine = lax.axis_index("nodes") % (LANES // per)
    cluster = cluster_ref[...]
    member = (_iota((devices, rows), 0) == cluster).astype(F32)
    before = (_iota((rows, rows), 0) < _iota((rows, rows), 1)).astype(BF16)
    rank = jnp.sum(member * _dot(member.astype(BF16), before), axis=0, keepdims=True).astype(jnp.int32)
    take = (_iota((rows, rows), 0) == cluster * per + rank).astype(BF16)
    out_ref[0:devices] = _dot(take, feat_ref[...]).astype(BF16).reshape(devices, per, feat_ref.shape[1])
    place = (_iota((LANES, rows), 0) == mine * per + rank).astype(BF16)
    slots = (member * (slot_ref[...] - rows // 2).astype(F32)).astype(BF16)
    out_ref[devices, 0:SUB] = _dot(slots, place, NT).astype(BF16)
    labels = jnp.concatenate([label_ref[...].astype(F32), jnp.zeros((SUB - label_ref.shape[0], LANES), F32)], axis=0)
    out_ref[devices, SUB : 2 * SUB] = labels.astype(BF16)


def pack(features, cluster, slot, labels, devices):
    rows, width = features.shape
    per = rows // devices
    inputs = (features, cluster.reshape(1, rows), slot.reshape(1, rows), labels.reshape(rows // LANES, LANES))
    inputs = [_stay(x) for x in inputs]
    return pl.pallas_call(
        lambda *refs: pack_kernel(devices, *refs),
        in_specs=[pl.BlockSpec(memory_space=pltpu.HBM)] * 4,
        out_specs=pl.BlockSpec(memory_space=pltpu.VMEM),
        out_shape=jax.ShapeDtypeStruct((devices + 1, per, width), BF16),
        scratch_shapes=[*[pltpu.VMEM(x.shape, x.dtype) for x in inputs], pltpu.SemaphoreType.DMA((4,))],
        compiler_params=_params(8),
        name="pack_rows",
    )(*inputs)


def weights_kernel(*refs):
    sources, (in_t_ref, out_t_ref, out_ref, bias_ref), targets = refs[0:4], refs[4:8], refs[8:12]
    wide, line, sems = refs[12:15]
    _fetch(sources, targets, sems)
    self_ref, neigh_ref, w_out_ref, b_ref = targets
    classes = w_out_ref.shape[0]
    in_t_ref[...] = jnp.transpose(jnp.concatenate([self_ref[...], neigh_ref[...]], axis=0).astype(F32)).astype(BF16)
    wide[...] = jnp.zeros_like(wide)
    wide[0:classes, :] = w_out_ref[...].astype(F32)
    out_t_ref[...] = wide[...].astype(BF16)
    out_ref[...] = jnp.transpose(wide[...]).astype(BF16)
    line[...] = jnp.full_like(line, -1e30)
    line[:, 0:classes] = b_ref[...]
    bias_ref[...] = jnp.transpose(jnp.broadcast_to(line[...], (LANES, line.shape[1])))[0 : bias_ref.shape[0]]


def weights(w_self, w_neigh, w_out, b_out):
    width, units = w_self.shape
    classes = w_out.shape[1]
    padded = -(-classes // SUB) * SUB
    inputs = [_stay(x) for x in (w_self, w_neigh, w_out.T, b_out.reshape(1, classes))]
    return pl.pallas_call(
        weights_kernel,
        in_specs=[pl.BlockSpec(memory_space=pltpu.HBM)] * 4,
        out_specs=[pl.BlockSpec(memory_space=pltpu.VMEM)] * 4,
        out_shape=[
            jax.ShapeDtypeStruct((units, 2 * width), BF16),
            jax.ShapeDtypeStruct((padded, units), BF16),
            jax.ShapeDtypeStruct((units, padded), BF16),
            jax.ShapeDtypeStruct((padded, LANES), F32),
        ],
        scratch_shapes=[
            *[pltpu.VMEM(x.shape, x.dtype) for x in inputs],
            pltpu.VMEM((padded, units), F32),
            pltpu.VMEM((1, 2 * LANES), F32),
            pltpu.SemaphoreType.DMA((4,)),
        ],
        cost_estimate=pl.CostEstimate(flops=0, bytes_accessed=1 << 21, transcendentals=0),
        compiler_params=_params(8),
        name="weights",
    )(*inputs)


def turn_kernel(first, adj_ref, turned_ref, adj, sems):
    tiles, neigh = turned_ref.shape[0:2]
    pieces = sems.shape[1]
    part = TILE // pieces
    copies = [
        [
            pltpu.make_async_copy(
                adj_ref.at[pl.ds((first + t) * TILE + i * part, part)], adj.at[t, pl.ds(i * part, part)], sems.at[t, i]
            )
            for i in range(pieces)
        ]
        for t in range(tiles)
    ]
    for copy in sum(copies, []):
        copy.start()
    side = SUB * SUB
    row = _iota((side, side), 0)
    move = ((row % SUB) * SUB + row // SUB == _iota((side, side), 1)).astype(BF16)
    for t in range(tiles):
        for b in range(TILE // SUB):
            if b * SUB % part == 0:
                copies[t][b * SUB // part].wait()
            for j in range(neigh // (2 * SUB)):
                halves = [
                    adj[t, SUB * b : SUB * (b + 1), SUB * k : SUB * (k + 1), :].reshape(side, TILE)
                    for k in (2 * j, 2 * j + 1)
                ]
                moved = _dot(move, jnp.concatenate(halves, axis=1)).astype(BF16)
                for h in range(2):
                    k = 2 * j + h
                    turned_ref[t, SUB * k : SUB * (k + 1), SUB * b : SUB * (b + 1), :] = moved[
                        :, TILE * h : TILE * (h + 1)
                    ].reshape(SUB, SUB, TILE)


def turn(adjacency, first, tiles):
    _, neigh, tile = adjacency.shape
    pieces = 2
    return pl.pallas_call(
        lambda *refs: turn_kernel(first, *refs),
        in_specs=[pl.BlockSpec(memory_space=pltpu.HBM)],
        out_specs=pl.BlockSpec(memory_space=pltpu.VMEM),
        out_shape=jax.ShapeDtypeStruct((tiles, neigh, tile, tile), BF16),
        scratch_shapes=[pltpu.VMEM((tiles, tile, neigh, tile), BF16), pltpu.SemaphoreType.DMA((tiles, pieces))],
        cost_estimate=pl.CostEstimate(flops=tiles << 29, bytes_accessed=tiles << 21, transcendentals=0),
        compiler_params=_params(16),
        name="turn_adjacency",
    )(_stay(adjacency))


def _place(ms, blocks, prior, px_ref, labels_ref, got):
    me = lax.axis_index("nodes")
    per = blocks[0].shape[1]
    rows = DEVICES * per
    if prior:
        labels_ref[...] = prior[1][...]
    slots = []
    for q in range(len(ms) // QUAD):
        held = 0.0
        for m, block in list(zip(ms, blocks))[q * QUAD : (q + 1) * QUAD]:
            at = q * LANES + ((me % QUAD) ^ (m % QUAD)) * per
            got[:, pl.ds(pl.multiple_of(at, per), per), :] = block[0:DEVICES]
            held += block[DEVICES, 0:SUB, :].astype(F32)
            labels_ref[me ^ m] = block[DEVICES, SUB : 2 * SUB, :]
        slots.append(held)
    slots = jnp.concatenate(slots, axis=1).astype(jnp.int32)
    position = _iota((rows, slots.shape[1]), 0) - rows // 2
    for p in range(DEVICES):
        put = (position == slots[p : p + 1, :]).astype(BF16)
        placed = _dot(put, got[p])
        if prior:
            placed += prior[0][p * rows : (p + 1) * rows, :].astype(F32)
        px_ref[p * rows : (p + 1) * rows, :] = placed.astype(BF16)


def _placed(per, width):
    return [
        jax.ShapeDtypeStruct((DEVICES * DEVICES * per, width), BF16),
        jax.ShapeDtypeStruct((DEVICES, SUB, LANES), BF16),
    ]


def place(have, ms):
    per, width = have[0].shape[1:]
    vmem = pl.BlockSpec(memory_space=pltpu.VMEM)
    return pl.pallas_call(
        lambda *refs: _place(ms, refs[: len(ms)], None, *refs[len(ms) :]),
        in_specs=[vmem] * len(ms),
        out_specs=[vmem] * 2,
        out_shape=_placed(per, width),
        scratch_shapes=[pltpu.VMEM((DEVICES, len(ms) * per, width), BF16)],
        cost_estimate=pl.CostEstimate(flops=1 << 30, bytes_accessed=1 << 22, transcendentals=0),
        compiler_params=_params(16),
        name="place",
    )(*[have[m] for m in ms])


def aggregate_kernel(ms, parts, *refs):
    n = len(ms)
    blocks, prior, turned, refs = refs[:n], refs[n : n + 2], refs[n + 2 : n + 2 + parts], refs[n + 2 + parts :]
    halo_ref, slots_ref, px_ref, labels_ref, agg_ref, got = refs
    _place(ms, blocks, prior, px_ref, labels_ref, got)
    neigh = slots_ref.shape[1]
    tiles = [ref.at[t] for ref in turned for t in range(ref.shape[0])]
    for t, adj in enumerate(tiles):
        total = jnp.zeros((TILE, px_ref.shape[1]), F32)
        for k in range(0, neigh, 2):
            sources = []
            for j in (k, k + 1):
                tile = halo_ref[0, slots_ref[t, j]]
                sources.append(px_ref[pl.ds(pl.multiple_of(tile * TILE, TILE), TILE), :])
            total += _dot(jnp.concatenate([adj[k], adj[k + 1]], axis=1), jnp.concatenate(sources, axis=0))
        agg_ref[t * TILE : (t + 1) * TILE, :] = total.astype(BF16)


def aggregate(have, ms, prior, turned, halo_tiles, tile_slots):
    per, width = have[0].shape[1:]
    scalars = pl.BlockSpec(memory_space=pltpu.SMEM)
    vmem = pl.BlockSpec(memory_space=pltpu.VMEM)
    return pl.pallas_call(
        lambda *refs: aggregate_kernel(ms, len(turned), *refs),
        in_specs=[vmem] * (len(ms) + 2 + len(turned)) + [scalars] * 2,
        out_specs=[vmem] * 3,
        out_shape=[*_placed(per, width), jax.ShapeDtypeStruct((DEVICES * per, width), BF16)],
        scratch_shapes=[pltpu.VMEM((DEVICES, len(ms) * per, width), BF16)],
        compiler_params=_params(24),
        name="aggregate",
    )(*[have[m] for m in ms], *prior, *turned, halo_tiles, tile_slots)


def _owner(pair, o):
    return pair * QUAD + 2 * o + lax.axis_index("nodes") % 2


def _hot(kinds, labels_ref, owner):
    held = labels_ref[owner].astype(F32)
    return [kinds == held[j : j + 1, :].astype(jnp.int32) for j in range(QUAD)]


def _inputs(pair, px_ref, agg_ref):
    rows = agg_ref.shape[0] // 2
    x = [px_ref[pl.ds(pl.multiple_of(_owner(pair, o) * rows, rows), rows), :] for o in range(2)]
    return jnp.concatenate([jnp.concatenate(x, axis=0), agg_ref[...]], axis=1)


def _forward(c, blocks, px_ref, labels_ref, in_t_ref, out_t_ref, bias_ref, agg_ref, hid_ref, slope_ref, loss_ref, count_ref):
    me = lax.axis_index("nodes")
    pair = (me // QUAD) ^ c
    rows = blocks[0].shape[0]
    for o, block in enumerate(blocks):
        at = ((me // 2 % 2) ^ o) * rows
        agg_ref[pl.ds(pl.multiple_of(at, rows), rows), :] = block[...]
    hidden = jnp.maximum(_dot(in_t_ref[...], _inputs(pair, px_ref, agg_ref), NT), 0.0).astype(BF16)
    hid_ref[...] = hidden
    logits = _dot(out_t_ref[...], hidden) + jnp.concatenate([bias_ref[...]] * (2 * rows // LANES), axis=1)
    logits -= jnp.log(jnp.sum(jnp.exp(logits), axis=0, keepdims=True))
    probs = jnp.exp(logits)
    kinds = _iota(bias_ref.shape, 0)
    loss = count = jnp.zeros(bias_ref.shape, F32)
    for o in range(2):
        for j, hot in enumerate(_hot(kinds, labels_ref, _owner(pair, o))):
            cut = slice(o * rows + j * LANES, o * rows + (j + 1) * LANES)
            one = hot.astype(F32)
            loss -= jnp.where(hot, logits[:, cut], 0.0)
            count += one
            slope_ref[:, cut] = probs[:, cut] - one
    loss_ref[...], count_ref[...] = loss, count


def own_kernel(px_ref, agg_ref, in_t_ref, hidden_ref):
    rows = agg_ref.shape[0]
    x = px_ref[pl.ds(pl.multiple_of(lax.axis_index("nodes") * rows, rows), rows), :]
    pre = _dot(jnp.concatenate([x, agg_ref[...]], axis=1), in_t_ref[...], NT)
    hidden_ref[...] = jnp.maximum(pre, 0.0).astype(BF16)


def own(part_x, agg, in_t):
    vmem = pl.BlockSpec(memory_space=pltpu.VMEM)
    return pl.pallas_call(
        own_kernel,
        in_specs=[vmem] * 3,
        out_specs=vmem,
        out_shape=jax.ShapeDtypeStruct((agg.shape[0], in_t.shape[0]), BF16),
        cost_estimate=pl.CostEstimate(flops=1 << 26, bytes_accessed=1 << 18, transcendentals=0),
        compiler_params=_params(8),
        name="own",
    )(part_x, agg, in_t)


def forward_kernel(c, before, *refs):
    blocks, shared, refs = refs[0:2], refs[2:7], refs[7:]
    prior, outs = refs[: 2 * before], refs[2 * before :]
    _forward(c, blocks, *shared, *outs[0:5])
    if before:
        losses, counts = outs[6:8]
        mine = lax.axis_index("nodes") // QUAD
        for i in range(before):
            losses[mine ^ i], counts[mine ^ i] = prior[2 * i][...], prior[2 * i + 1][...]
        losses[mine ^ c], counts[mine ^ c] = outs[3][...], outs[4][...]
        loss, count = (jnp.sum(sum(x[q] for q in range(QUAD)), axis=1, keepdims=True) for x in (losses, counts))
        outs[5][...] = jnp.where(_iota(outs[5].shape, 1) == 0, loss, count)


def forward(have, c, shared, prior=()):
    rows, width = have[0].shape
    units, padded = shared[2].shape[0], shared[4].shape[0]
    vmem = pl.BlockSpec(memory_space=pltpu.VMEM)
    shapes = [
        jax.ShapeDtypeStruct((2 * rows, width), BF16),
        jax.ShapeDtypeStruct((units, 2 * rows), BF16),
        jax.ShapeDtypeStruct((padded, 2 * rows), F32),
        jax.ShapeDtypeStruct((padded, LANES), F32),
        jax.ShapeDtypeStruct((padded, LANES), F32),
    ]
    scratch = []
    if prior:
        shapes.append(jax.ShapeDtypeStruct((padded, LANES), F32))
        scratch = [pltpu.VMEM((QUAD, padded, LANES), F32)] * 2
    stats = [x for held in prior for x in held[3:5]]
    return pl.pallas_call(
        lambda *refs: forward_kernel(c, len(prior), *refs),
        in_specs=[vmem] * (7 + len(stats)),
        out_specs=[vmem] * len(shapes),
        out_shape=shapes,
        scratch_shapes=scratch,
        cost_estimate=pl.CostEstimate(flops=1 << 29, bytes_accessed=1 << 21, transcendentals=1 << 18),
        compiler_params=_params(12),
        name="forward",
    )(have[4 * c], have[4 * c + 2], *shared, *stats)


def backward_kernel(classes, *refs):
    held, refs = [refs[3 * c : 3 * c + 3] for c in range(QUAD)], refs[3 * QUAD :]
    px_ref, labels_ref, out_ref, mine_ref, other_ref, sums_ref, class_ref, grads = refs
    me = lax.axis_index("nodes")
    padded = mine_ref.shape[0]
    units = out_ref.shape[0]

    both = mine_ref[...] + other_ref[...]
    loss, count = both[:, 0:1], both[:, 1:2]
    real = _iota((padded, 1), 0) < classes
    difficulty = jnp.where(real, (loss + 1.0) / (count + 1.0), 0.0)
    weight = difficulty / (jnp.sum(difficulty, axis=0, keepdims=True) / classes)
    share = 1.0 / (1.0 + jnp.sum(count, axis=0, keepdims=True))
    class_ref[...] = jnp.transpose(jnp.broadcast_to(weight, (padded, LANES)))[0:1, 0:classes]
    scaled = jnp.broadcast_to(weight * share, (padded, LANES))

    kinds = _iota((padded, LANES), 0)
    for c, (agg_ref, hid_ref, slope_ref) in enumerate(held):
        pair = (me // QUAD) ^ c
        parts = []
        for o in range(2):
            for hot in _hot(kinds, labels_ref, _owner(pair, o)):
                row = jnp.sum(jnp.where(hot, scaled, 0.0), axis=0, keepdims=True)
                cut = slice(LANES * len(parts), LANES * (len(parts) + 1))
                parts.append((row * slope_ref[:, cut]).astype(BF16))
        dlogits = jnp.concatenate(parts, axis=1)
        hidden = hid_ref[...]
        dpre = jnp.where(hidden > 0, _dot(out_ref[...], dlogits), 0.0).astype(BF16)
        grads[pair, 0:units] = _dot(dpre, _inputs(pair, px_ref, agg_ref))
        grads[pair, units : units + padded] = _dot(dlogits, hidden, NT)
    sums_ref[...] = sum(grads[q] for q in range(QUAD))


def backward(held, part_x, labels, out_p, mine, other, classes):
    units, padded = out_p.shape
    vmem = pl.BlockSpec(memory_space=pltpu.VMEM)
    operands = [*[x for h in held for x in h[0:3]], part_x, labels, out_p, mine, other]
    return pl.pallas_call(
        lambda *refs: backward_kernel(classes, *refs),
        in_specs=[vmem] * len(operands),
        out_specs=[vmem] * 2,
        out_shape=[
            jax.ShapeDtypeStruct((units + padded, 2 * part_x.shape[1]), F32),
            jax.ShapeDtypeStruct((1, classes), F32),
        ],
        scratch_shapes=[pltpu.VMEM((QUAD, units + padded, 2 * part_x.shape[1]), F32)],
        compiler_params=_params(20),
        name="backward",
    )(*operands)


def total_kernel(mine_ref, other_ref, self_ref, neigh_ref, out_ref):
    width, units = self_ref.shape
    classes = out_ref.shape[0]
    grad_in = jnp.transpose(mine_ref[0:units] + other_ref[0:units])
    self_ref[...] = grad_in[0:width]
    neigh_ref[...] = grad_in[width : 2 * width]
    out_ref[...] = (mine_ref[units:] + other_ref[units:])[0:classes]


def total(mine, other, width, units, classes):
    vmem = pl.BlockSpec(memory_space=pltpu.VMEM)
    return pl.pallas_call(
        total_kernel,
        in_specs=[vmem] * 2,
        out_specs=[vmem] * 3,
        out_shape=[
            jax.ShapeDtypeStruct((width, units), F32),
            jax.ShapeDtypeStruct((width, units), F32),
            jax.ShapeDtypeStruct((classes, units), F32),
        ],
        compiler_params=_params(8),
        name="total",
    )(mine, other)


def gathered_body(
    features, cluster, slot, halo_tiles, tile_slots, adjacency, labels, w_self, w_neigh, w_out, b_out
):
    packed = pack(features, cluster, slot, labels, DEVICES)
    early, late = tuple(range(0, 8)), tuple(range(8, 16))
    half = features.shape[0] // TILE // 2
    have, near, (prior, far) = gather_rows(
        packed,
        lambda have: turn(adjacency, 0, half),
        lambda have: (place(have, early), turn(adjacency, half, half)),
    )
    part_x, all_labels, agg = aggregate(have, late, prior, (near, far), halo_tiles, tile_slots)
    weighed = []

    def first(have):
        weighed.extend(weights(w_self, w_neigh, w_out, b_out))
        return weighed, own(part_x, agg, weighed[0])

    def ahead(have):
        in_t, out_t, _, bias = weighed
        return [forward(have, c, (part_x, all_labels, in_t, out_t, bias)) for c in range(QUAD - 1)]

    have, (_, hidden), held = gather_plane(agg, first, ahead)
    in_t, out_t, out_p, bias = weighed
    shared = (part_x, all_labels, in_t, out_t, bias)
    *last, mine = forward(have, QUAD - 1, shared, held)
    classes = w_out.shape[1]
    sums, class_weight = backward([*held, last], part_x, all_labels, out_p, mine, swap(mine, 1), classes)
    grad_self, grad_neigh, grad_out = total(sums, swap(sums, 1), *w_self.shape, classes)
    return hidden, grad_self, grad_neigh, grad_out.T, class_weight.reshape(-1)


def split_body(
    features, cluster, slot, halo_tiles, tile_slots, adjacency, labels, w_self, w_neigh, w_out, b_out
):
    rows = features.shape[0]
    width = features.shape[1]
    devices = lax.axis_size("nodes")
    per_peer = rows // devices
    order = jnp.argsort(cluster, stable=True)
    send_rows = features[order].reshape(devices, per_peer, width)
    send_slots = slot[order].reshape(devices, per_peer)
    recv_rows, recv_slots = (
        lax.all_to_all(send_rows, "nodes", split_axis=0, concat_axis=0, tiled=True),
        lax.all_to_all(send_slots, "nodes", split_axis=0, concat_axis=0, tiled=True),
    )
    part_x = (
        jnp.zeros((rows, width), jnp.bfloat16)
        .at[recv_slots.reshape(rows)]
        .set(recv_rows.reshape(rows, width))
    )
    local_tiles = rows // TILE
    wanted = halo_tiles[0]
    gathered = lax.all_gather(part_x, "nodes", axis=0, tiled=True)
    halo = gathered.reshape(-1, TILE, width)[wanted]
    sources = halo[tile_slots]
    adj_tiles = adjacency.reshape(local_tiles, TILE, adjacency.shape[1], TILE)
    agg = jnp.einsum("tikc,tkcf->tif", adj_tiles, sources, preferred_element_type=jnp.float32)
    agg = agg.reshape(rows, width).astype(jnp.bfloat16)
    pre = jnp.dot(part_x, w_self, preferred_element_type=jnp.float32) + jnp.dot(
        agg, w_neigh, preferred_element_type=jnp.float32
    )
    hidden = jnp.maximum(pre, 0.0).astype(jnp.bfloat16)
    logits = jnp.dot(hidden, w_out, preferred_element_type=jnp.float32) + b_out
    lse = jnp.log(jnp.sum(jnp.exp(logits), axis=1))
    classes_row = jnp.arange(w_out.shape[1], dtype=jnp.int32)
    onehot = (labels[:, None] == classes_row[None, :]).astype(jnp.float32)
    picked = jnp.sum(onehot * logits, axis=1)
    ce_rows = lse - picked
    local_loss = jnp.sum(onehot * ce_rows[:, None], axis=0)
    local_counts = jnp.sum(onehot, axis=0)
    loss_sum, counts = lax.psum((local_loss, local_counts), "nodes")
    difficulty = (loss_sum + 1.0) / (counts + 1.0)
    class_weight = difficulty / jnp.mean(difficulty)
    total = jnp.sum(counts)
    row_weight = jnp.sum(onehot * class_weight[None, :], axis=1) / (total + 1.0)
    probs = jnp.exp(logits - lse[:, None])
    dlogits = (row_weight[:, None] * (probs - onehot)).astype(jnp.bfloat16)
    part_out = jnp.dot(hidden.T, dlogits, preferred_element_type=jnp.float32)
    dhidden = jnp.dot(dlogits, w_out.T, preferred_element_type=jnp.float32)
    dpre = jnp.where(hidden > 0, dhidden, 0.0).astype(jnp.bfloat16)
    part_self = jnp.dot(part_x.T, dpre, preferred_element_type=jnp.float32)
    part_neigh = jnp.dot(agg.T, dpre, preferred_element_type=jnp.float32)
    grad_self, grad_neigh, grad_out = lax.psum((part_self, part_neigh, part_out), "nodes")
    return (hidden, grad_self, grad_neigh, grad_out, class_weight)


def solution(mesh):
    def body(*args):
        devices = mesh.shape["nodes"]
        rows = args[0].shape[0]
        per = rows // devices
        classes = args[9].shape[1]
        fits = devices == DEVICES and per == 2 * SUB and classes <= 256
        return (gathered_body if fits else split_body)(*args)

    return jax.shard_map(
        body,
        mesh=mesh,
        in_specs=(
            P(("groups", "nodes"), None),
            P(("groups", "nodes")),
            P(("groups", "nodes")),
            P(("groups", "nodes"), None),
            P(("groups", "nodes"), None),
            P(("groups", "nodes"), None, None),
            P(("groups", "nodes")),
            P(),
            P(),
            P(),
            P(),
        ),
        out_specs=(
            P(("groups", "nodes"), None),
            P("groups", None),
            P("groups", None),
            P("groups", None),
            P("groups"),
        ),
        check_vma=False,
    )
```

```python
import jax
import jax.numpy as jnp
from jax import lax
from jax.experimental import pallas as pl
from jax.experimental.pallas import tpu as pltpu
from jax.sharding import PartitionSpec as P

DEVICES = 16
QUAD = 4
TILE = 128
LANES = 128
SUB = 16
F32 = jnp.float32
BF16 = jnp.bfloat16


def _dot(a, b, contract=((1,), (0,))):
    return lax.dot_general(a, b, (contract, ((), ())), preferred_element_type=F32)


NT = ((1,), (1,))


def _iota(shape, dim):
    return lax.broadcasted_iota(jnp.int32, shape, dim)


def _stay(x):
    return pltpu.with_memory_space_constraint(x, pltpu.HBM)


def _fetch(sources, targets, sems):
    copies = [pltpu.make_async_copy(a, b, sems.at[i]) for i, (a, b) in enumerate(zip(sources, targets))]
    for copy in copies:
        copy.start()
    for copy in copies:
        copy.wait()


def _params(mib):
    return pltpu.CompilerParams(vmem_limit_bytes=mib << 20)


def swap(x, m):
    return lax.ppermute(x, "nodes", [(i, i ^ m) for i in range(DEVICES)])


def gather_all(block, work, cores=True):
    have = {0: block}
    done = []

    def hop(i, m):
        if work[i] is not None:
            have[m], out = lax.optimization_barrier((have[m], work[i](have)))
            done.append(out)

    def cross(*ms):
        if cores:
            have.update({m + 1: swap(have[m], 1) for m in ms})

    have[8], have[4], have[2] = (swap(block, m) for m in (8, 4, 2))
    cross(0)
    hop(0, 8)
    have[12], have[10], have[6] = swap(have[8], 4), swap(have[8], 2), swap(have[4], 2)
    cross(2, 4, 6, 8)
    hop(1, 12)
    have[14] = swap(have[12], 2)
    cross(10, 12)
    hop(2, 14)
    cross(14)
    return have, done


def gather_plane(block, first, second):
    have = {0: block}
    have[8], have[4], have[2], have[6] = (swap(block, m) for m in (8, 4, 2, 6))
    have[8], one = lax.optimization_barrier((have[8], first(have)))
    have[12], have[10], have[14] = swap(have[8], 4), swap(have[8], 2), swap(have[8], 6)
    have[14], two = lax.optimization_barrier((have[14], second(have)))
    return have, one, two


def gather_rows(block, first, second):
    have = {0: block}
    have[8], have[4], have[2] = (swap(block, m) for m in (8, 4, 2))
    (have[8], have[4], have[2]), one = lax.optimization_barrier(((have[8], have[4], have[2]), first(have)))
    have[12], have[10], have[6] = swap(have[8], 4), swap(have[8], 2), swap(have[4], 2)
    have[1], have[3], have[5], have[7], have[9] = (swap(have[m], 1) for m in (0, 2, 4, 6, 8))
    have[14] = swap(have[12], 2)
    have[11], have[13] = swap(have[10], 1), swap(have[12], 1)
    have[14], two = lax.optimization_barrier((have[14], second(have)))
    have[15] = swap(have[14], 1)
    return have, one, two


def pack_kernel(devices, *refs):
    sources, out_ref, targets, sems = refs[0:4], refs[4], refs[5:9], refs[9]
    _fetch(sources, targets, sems)
    feat_ref, cluster_ref, slot_ref, label_ref = targets
    rows = feat_ref.shape[0]
    per = rows // devices
    mine = lax.axis_index("nodes") % (LANES // per)
    cluster = cluster_ref[...]
    member = (_iota((devices, rows), 0) == cluster).astype(F32)
    before = (_iota((rows, rows), 0) < _iota((rows, rows), 1)).astype(BF16)
    rank = jnp.sum(member * _dot(member.astype(BF16), before), axis=0, keepdims=True).astype(jnp.int32)
    take = (_iota((rows, rows), 0) == cluster * per + rank).astype(BF16)
    out_ref[0:devices] = _dot(take, feat_ref[...]).astype(BF16).reshape(devices, per, feat_ref.shape[1])
    place = (_iota((LANES, rows), 0) == mine * per + rank).astype(BF16)
    slots = (member * (slot_ref[...] - rows // 2).astype(F32)).astype(BF16)
    out_ref[devices, 0:SUB] = _dot(slots, place, NT).astype(BF16)
    labels = jnp.concatenate([label_ref[...].astype(F32), jnp.zeros((SUB - label_ref.shape[0], LANES), F32)], axis=0)
    out_ref[devices, SUB : 2 * SUB] = labels.astype(BF16)


def pack(features, cluster, slot, labels, devices):
    rows, width = features.shape
    per = rows // devices
    inputs = (features, cluster.reshape(1, rows), slot.reshape(1, rows), labels.reshape(rows // LANES, LANES))
    inputs = [_stay(x) for x in inputs]
    return pl.pallas_call(
        lambda *refs: pack_kernel(devices, *refs),
        in_specs=[pl.BlockSpec(memory_space=pltpu.HBM)] * 4,
        out_specs=pl.BlockSpec(memory_space=pltpu.VMEM),
        out_shape=jax.ShapeDtypeStruct((devices + 1, per, width), BF16),
        scratch_shapes=[*[pltpu.VMEM(x.shape, x.dtype) for x in inputs], pltpu.SemaphoreType.DMA((4,))],
        compiler_params=_params(8),
        name="pack_rows",
    )(*inputs)


def weights_kernel(*refs):
    sources, (in_t_ref, out_t_ref, out_ref, bias_ref), targets = refs[0:4], refs[4:8], refs[8:12]
    wide, line, sems = refs[12:15]
    _fetch(sources, targets, sems)
    self_ref, neigh_ref, w_out_ref, b_ref = targets
    classes = w_out_ref.shape[0]
    in_t_ref[...] = jnp.transpose(jnp.concatenate([self_ref[...], neigh_ref[...]], axis=0).astype(F32)).astype(BF16)
    wide[...] = jnp.zeros_like(wide)
    wide[0:classes, :] = w_out_ref[...].astype(F32)
    out_t_ref[...] = wide[...].astype(BF16)
    out_ref[...] = jnp.transpose(wide[...]).astype(BF16)
    line[...] = jnp.full_like(line, -1e30)
    line[:, 0:classes] = b_ref[...]
    bias_ref[...] = jnp.transpose(jnp.broadcast_to(line[...], (LANES, line.shape[1])))[0 : bias_ref.shape[0]]


def weights(w_self, w_neigh, w_out, b_out):
    width, units = w_self.shape
    classes = w_out.shape[1]
    padded = -(-classes // SUB) * SUB
    inputs = [_stay(x) for x in (w_self, w_neigh, w_out.T, b_out.reshape(1, classes))]
    return pl.pallas_call(
        weights_kernel,
        in_specs=[pl.BlockSpec(memory_space=pltpu.HBM)] * 4,
        out_specs=[pl.BlockSpec(memory_space=pltpu.VMEM)] * 4,
        out_shape=[
            jax.ShapeDtypeStruct((units, 2 * width), BF16),
            jax.ShapeDtypeStruct((padded, units), BF16),
            jax.ShapeDtypeStruct((units, padded), BF16),
            jax.ShapeDtypeStruct((padded, LANES), F32),
        ],
        scratch_shapes=[
            *[pltpu.VMEM(x.shape, x.dtype) for x in inputs],
            pltpu.VMEM((padded, units), F32),
            pltpu.VMEM((1, 2 * LANES), F32),
            pltpu.SemaphoreType.DMA((4,)),
        ],
        cost_estimate=pl.CostEstimate(flops=0, bytes_accessed=1 << 21, transcendentals=0),
        compiler_params=_params(8),
        name="weights",
    )(*inputs)


def _turn(adj, turned_ref, arrived=None):
    tiles, neigh = turned_ref.shape[0:2]
    side = SUB * SUB
    row = _iota((side, side), 0)
    move = ((row % SUB) * SUB + row // SUB == _iota((side, side), 1)).astype(BF16)
    for t in range(tiles):
        for b in range(TILE // SUB):
            if arrived:
                arrived(t, b)
            for j in range(neigh // (2 * SUB)):
                halves = [
                    adj[t, SUB * b : SUB * (b + 1), SUB * k : SUB * (k + 1), :].reshape(side, TILE)
                    for k in (2 * j, 2 * j + 1)
                ]
                moved = _dot(move, jnp.concatenate(halves, axis=1)).astype(BF16)
                for h in range(2):
                    k = 2 * j + h
                    turned_ref[t, SUB * k : SUB * (k + 1), SUB * b : SUB * (b + 1), :] = moved[
                        :, TILE * h : TILE * (h + 1)
                    ].reshape(SUB, SUB, TILE)


def turn_kernel(adj_ref, turned_ref, rest_ref, adj, sems, rest_sem):
    tiles = turned_ref.shape[0]
    pieces = sems.shape[1]
    part = TILE // pieces
    copies = [
        [
            pltpu.make_async_copy(
                adj_ref.at[pl.ds(t * TILE + i * part, part)], adj.at[t, pl.ds(i * part, part)], sems.at[t, i]
            )
            for i in range(pieces)
        ]
        for t in range(tiles)
    ]
    rest = pltpu.make_async_copy(adj_ref.at[pl.ds(tiles * TILE, rest_ref.shape[0])], rest_ref, rest_sem)
    for copy in sum(copies, []):
        copy.start()
    rest.start()

    def arrived(t, b):
        if b * SUB % part == 0:
            copies[t][b * SUB // part].wait()

    _turn(adj, turned_ref, arrived)
    rest.wait()


def turn(adjacency):
    rows, neigh, tile = adjacency.shape
    tiles = rows // tile // 2
    pieces = 2
    return pl.pallas_call(
        turn_kernel,
        in_specs=[pl.BlockSpec(memory_space=pltpu.HBM)],
        out_specs=[pl.BlockSpec(memory_space=pltpu.VMEM)] * 2,
        out_shape=[
            jax.ShapeDtypeStruct((tiles, neigh, tile, tile), BF16),
            jax.ShapeDtypeStruct((rows - tiles * tile, neigh, tile), BF16),
        ],
        scratch_shapes=[
            pltpu.VMEM((tiles, tile, neigh, tile), BF16),
            pltpu.SemaphoreType.DMA((tiles, pieces)),
            pltpu.SemaphoreType.DMA,
        ],
        cost_estimate=pl.CostEstimate(flops=tiles << 29, bytes_accessed=tiles << 22, transcendentals=0),
        compiler_params=_params(16),
        name="turn_adjacency",
    )(_stay(adjacency))


def turn_rest(rest):
    rows, neigh, tile = rest.shape
    shape = (rows // tile, neigh, tile, tile)
    vmem = pl.BlockSpec(memory_space=pltpu.VMEM)
    return pl.pallas_call(
        _turn,
        in_specs=[vmem],
        out_specs=vmem,
        out_shape=jax.ShapeDtypeStruct(shape, BF16),
        cost_estimate=pl.CostEstimate(flops=shape[0] << 29, bytes_accessed=shape[0] << 21, transcendentals=0),
        compiler_params=_params(12),
        name="turn_rest",
    )(rest.reshape(rows // tile, tile, neigh, tile))


def _place(ms, blocks, prior, px_ref, labels_ref, got):
    me = lax.axis_index("nodes")
    per = blocks[0].shape[1]
    rows = DEVICES * per
    if prior:
        labels_ref[...] = prior[1][...]
    slots = []
    for q in range(len(ms) // QUAD):
        held = 0.0
        for m, block in list(zip(ms, blocks))[q * QUAD : (q + 1) * QUAD]:
            at = q * LANES + ((me % QUAD) ^ (m % QUAD)) * per
            got[:, pl.ds(pl.multiple_of(at, per), per), :] = block[0:DEVICES]
            held += block[DEVICES, 0:SUB, :].astype(F32)
            labels_ref[me ^ m] = block[DEVICES, SUB : 2 * SUB, :]
        slots.append(held)
    slots = jnp.concatenate(slots, axis=1).astype(jnp.int32)
    position = _iota((rows, slots.shape[1]), 0) - rows // 2
    for p in range(DEVICES):
        put = (position == slots[p : p + 1, :]).astype(BF16)
        placed = _dot(put, got[p])
        if prior:
            placed += prior[0][p * rows : (p + 1) * rows, :].astype(F32)
        px_ref[p * rows : (p + 1) * rows, :] = placed.astype(BF16)


def _placed(per, width):
    return [
        jax.ShapeDtypeStruct((DEVICES * DEVICES * per, width), BF16),
        jax.ShapeDtypeStruct((DEVICES, SUB, LANES), BF16),
    ]


def place(have, ms):
    per, width = have[0].shape[1:]
    vmem = pl.BlockSpec(memory_space=pltpu.VMEM)
    return pl.pallas_call(
        lambda *refs: _place(ms, refs[: len(ms)], None, *refs[len(ms) :]),
        in_specs=[vmem] * len(ms),
        out_specs=[vmem] * 2,
        out_shape=_placed(per, width),
        scratch_shapes=[pltpu.VMEM((DEVICES, len(ms) * per, width), BF16)],
        cost_estimate=pl.CostEstimate(flops=1 << 30, bytes_accessed=1 << 22, transcendentals=0),
        compiler_params=_params(16),
        name="place",
    )(*[have[m] for m in ms])


def aggregate_kernel(ms, parts, *refs):
    n = len(ms)
    blocks, prior, turned, refs = refs[:n], refs[n : n + 2], refs[n + 2 : n + 2 + parts], refs[n + 2 + parts :]
    halo_ref, slots_ref, px_ref, labels_ref, agg_ref, got = refs
    _place(ms, blocks, prior, px_ref, labels_ref, got)
    neigh = slots_ref.shape[1]
    tiles = [ref.at[t] for ref in turned for t in range(ref.shape[0])]
    for t, adj in enumerate(tiles):
        total = jnp.zeros((TILE, px_ref.shape[1]), F32)
        for k in range(0, neigh, 2):
            sources = []
            for j in (k, k + 1):
                tile = halo_ref[0, slots_ref[t, j]]
                sources.append(px_ref[pl.ds(pl.multiple_of(tile * TILE, TILE), TILE), :])
            total += _dot(jnp.concatenate([adj[k], adj[k + 1]], axis=1), jnp.concatenate(sources, axis=0))
        agg_ref[t * TILE : (t + 1) * TILE, :] = total.astype(BF16)


def aggregate(have, ms, prior, turned, halo_tiles, tile_slots):
    per, width = have[0].shape[1:]
    scalars = pl.BlockSpec(memory_space=pltpu.SMEM)
    vmem = pl.BlockSpec(memory_space=pltpu.VMEM)
    return pl.pallas_call(
        lambda *refs: aggregate_kernel(ms, len(turned), *refs),
        in_specs=[vmem] * (len(ms) + 2 + len(turned)) + [scalars] * 2,
        out_specs=[vmem] * 3,
        out_shape=[*_placed(per, width), jax.ShapeDtypeStruct((DEVICES * per, width), BF16)],
        scratch_shapes=[pltpu.VMEM((DEVICES, len(ms) * per, width), BF16)],
        compiler_params=_params(24),
        name="aggregate",
    )(*[have[m] for m in ms], *prior, *turned, halo_tiles, tile_slots)


def _owner(pair, o):
    return pair * QUAD + 2 * o + lax.axis_index("nodes") % 2


def _hot(kinds, labels_ref, owner):
    held = labels_ref[owner].astype(F32)
    return [kinds == held[j : j + 1, :].astype(jnp.int32) for j in range(QUAD)]


def _rows(owner, px_ref, rows):
    return px_ref[pl.ds(pl.multiple_of(owner * rows, rows), rows), :]


def _inputs(pair, px_ref, agg_ref):
    rows = agg_ref.shape[0] // 2
    x = [_rows(_owner(pair, o), px_ref, rows) for o in range(2)]
    return jnp.concatenate([jnp.concatenate(x, axis=0), agg_ref[...]], axis=1)


def _forward(owners, inputs, labels_ref, in_t_ref, out_t_ref, bias_ref, keep):
    hidden = jnp.maximum(_dot(in_t_ref[...], inputs, NT), 0.0).astype(BF16)
    logits = _dot(out_t_ref[...], hidden) + jnp.concatenate([bias_ref[...]] * (hidden.shape[1] // LANES), axis=1)
    logits -= jnp.log(jnp.sum(jnp.exp(logits), axis=0, keepdims=True))
    probs = jnp.exp(logits)
    kinds = _iota(bias_ref.shape, 0)
    loss = count = jnp.zeros(bias_ref.shape, F32)
    lane = 0
    for owner in owners:
        for hot in _hot(kinds, labels_ref, owner):
            cut = slice(lane, lane + LANES)
            one = hot.astype(F32)
            loss -= jnp.where(hot, logits[:, cut], 0.0)
            count += one
            keep(cut, probs[:, cut] - one)
            lane += LANES
    return hidden, loss, count


def pair_kernel(c, *refs):
    blocks, (px_ref, *shared), outs = refs[0:2], refs[2:7], refs[7:12]
    agg_ref, hid_ref, slope_ref, loss_ref, count_ref = outs
    me = lax.axis_index("nodes")
    pair = (me // QUAD) ^ c
    rows = blocks[0].shape[0]
    for o, block in enumerate(blocks):
        at = ((me // 2 % 2) ^ o) * rows
        agg_ref[pl.ds(pl.multiple_of(at, rows), rows), :] = block[...]

    def keep(cut, x):
        slope_ref[:, cut] = x

    owners = [_owner(pair, o) for o in range(2)]
    hid_ref[...], loss_ref[...], count_ref[...] = _forward(owners, _inputs(pair, px_ref, agg_ref), *shared, keep)


def one_kernel(m, *refs):
    block, (px_ref, *shared), (hid_ref, slope_ref, loss_ref, count_ref) = refs[0], refs[1:6], refs[6:10]
    owner = lax.axis_index("nodes") ^ m
    inputs = jnp.concatenate([_rows(owner, px_ref, block.shape[0]), block[...]], axis=1)

    def keep(cut, x):
        slope_ref[:, cut] = x

    hid_ref[...], loss_ref[...], count_ref[...] = _forward([owner], inputs, *shared, keep)


def last_kernel(m, *refs):
    blocks, (px_ref, *shared), partner, prior = refs[0:2], refs[2:7], refs[7:11], refs[11:17]
    agg_ref, hid_ref, slope_ref, stats_ref, part, losses, counts = refs[17:]
    me = lax.axis_index("nodes")
    rows = blocks[0].shape[0]
    at = [pl.ds(pl.multiple_of(((me // 2 % 2) ^ o) * rows, rows), rows) for o in range(2)]
    for o, block in enumerate(blocks):
        agg_ref[at[o], :] = block[...]
    hid_ref[:, at[0]], slope_ref[:, at[0]] = partner[0][...], partner[1][...]

    def keep(cut, x):
        part[:, cut] = x

    inputs = jnp.concatenate([_rows(me ^ m, px_ref, rows), blocks[1][...]], axis=1)
    hidden, loss, count = _forward([me ^ m], inputs, *shared, keep)
    hid_ref[:, at[1]], slope_ref[:, at[1]] = hidden, part[...]
    mine = me // QUAD
    for c in range(QUAD - 1):
        losses[mine ^ c], counts[mine ^ c] = prior[2 * c][...], prior[2 * c + 1][...]
    losses[mine ^ (QUAD - 1)], counts[mine ^ (QUAD - 1)] = loss + partner[2][...], count + partner[3][...]
    loss, count = (jnp.sum(sum(x[q] for q in range(QUAD)), axis=1, keepdims=True) for x in (losses, counts))
    stats_ref[...] = jnp.where(_iota(stats_ref.shape, 1) == 0, loss, count)


def own_kernel(px_ref, agg_ref, in_t_ref, hidden_ref):
    rows = agg_ref.shape[0]
    x = px_ref[pl.ds(pl.multiple_of(lax.axis_index("nodes") * rows, rows), rows), :]
    pre = _dot(jnp.concatenate([x, agg_ref[...]], axis=1), in_t_ref[...], NT)
    hidden_ref[...] = jnp.maximum(pre, 0.0).astype(BF16)


def own(part_x, agg, in_t):
    vmem = pl.BlockSpec(memory_space=pltpu.VMEM)
    return pl.pallas_call(
        own_kernel,
        in_specs=[vmem] * 3,
        out_specs=vmem,
        out_shape=jax.ShapeDtypeStruct((agg.shape[0], in_t.shape[0]), BF16),
        cost_estimate=pl.CostEstimate(flops=1 << 26, bytes_accessed=1 << 18, transcendentals=0),
        compiler_params=_params(8),
        name="own",
    )(part_x, agg, in_t)


def _call(kernel, name, shapes, operands, scratch=()):
    vmem = pl.BlockSpec(memory_space=pltpu.VMEM)
    return pl.pallas_call(
        kernel,
        in_specs=[vmem] * len(operands),
        out_specs=[vmem] * len(shapes),
        out_shape=[jax.ShapeDtypeStruct(*x) for x in shapes],
        scratch_shapes=[pltpu.VMEM(*x) for x in scratch],
        cost_estimate=pl.CostEstimate(flops=1 << 29, bytes_accessed=1 << 21, transcendentals=1 << 18),
        compiler_params=_params(12),
        name=name,
    )(*operands)


def forward_pair(have, c, shared):
    rows, width = have[0].shape
    units, padded = shared[2].shape[0], shared[4].shape[0]
    stat = ((padded, LANES), F32)
    shapes = [((2 * rows, width), BF16), ((units, 2 * rows), BF16), ((padded, 2 * rows), F32), stat, stat]
    return _call(lambda *refs: pair_kernel(c, *refs), "forward_pair", shapes, [have[4 * c], have[4 * c + 2], *shared])


def forward_one(have, m, shared):
    rows, units, padded = have[0].shape[0], shared[2].shape[0], shared[4].shape[0]
    stat = ((padded, LANES), F32)
    shapes = [((units, rows), BF16), ((padded, rows), F32), stat, stat]
    return _call(lambda *refs: one_kernel(m, *refs), "forward_one", shapes, [have[m], *shared])


def forward_last(have, m, shared, partner, prior):
    rows, width = have[0].shape
    units, padded = shared[2].shape[0], shared[4].shape[0]
    stat = ((padded, LANES), F32)
    shapes = [((2 * rows, width), BF16), ((units, 2 * rows), BF16), ((padded, 2 * rows), F32), stat]
    stats = [x for held in prior for x in held[3:5]]
    scratch = [((padded, rows), F32)] + [((QUAD, padded, LANES), F32)] * 2
    operands = [have[m - 2], have[m], *shared, *partner, *stats]
    return _call(lambda *refs: last_kernel(m, *refs), "forward_last", shapes, operands, scratch)


def backward_kernel(classes, *refs):
    held, refs = [refs[3 * c : 3 * c + 3] for c in range(QUAD)], refs[3 * QUAD :]
    px_ref, labels_ref, out_ref, mine_ref, other_ref, sums_ref, class_ref, grads = refs
    me = lax.axis_index("nodes")
    padded = mine_ref.shape[0]
    units = out_ref.shape[0]

    both = mine_ref[...] + other_ref[...]
    loss, count = both[:, 0:1], both[:, 1:2]
    real = _iota((padded, 1), 0) < classes
    difficulty = jnp.where(real, (loss + 1.0) / (count + 1.0), 0.0)
    weight = difficulty / (jnp.sum(difficulty, axis=0, keepdims=True) / classes)
    share = 1.0 / (1.0 + jnp.sum(count, axis=0, keepdims=True))
    class_ref[...] = jnp.transpose(jnp.broadcast_to(weight, (padded, LANES)))[0:1, 0:classes]
    scaled = jnp.broadcast_to(weight * share, (padded, LANES))

    kinds = _iota((padded, LANES), 0)
    for c, (agg_ref, hid_ref, slope_ref) in enumerate(held):
        pair = (me // QUAD) ^ c
        parts = []
        for o in range(2):
            for hot in _hot(kinds, labels_ref, _owner(pair, o)):
                row = jnp.sum(jnp.where(hot, scaled, 0.0), axis=0, keepdims=True)
                cut = slice(LANES * len(parts), LANES * (len(parts) + 1))
                parts.append((row * slope_ref[:, cut]).astype(BF16))
        dlogits = jnp.concatenate(parts, axis=1)
        hidden = hid_ref[...]
        dpre = jnp.where(hidden > 0, _dot(out_ref[...], dlogits), 0.0).astype(BF16)
        grads[pair, 0:units] = _dot(dpre, _inputs(pair, px_ref, agg_ref))
        grads[pair, units : units + padded] = _dot(dlogits, hidden, NT)
    sums_ref[...] = sum(grads[q] for q in range(QUAD))


def backward(held, part_x, labels, out_p, mine, other, classes):
    units, padded = out_p.shape
    vmem = pl.BlockSpec(memory_space=pltpu.VMEM)
    operands = [*[x for h in held for x in h[0:3]], part_x, labels, out_p, mine, other]
    return pl.pallas_call(
        lambda *refs: backward_kernel(classes, *refs),
        in_specs=[vmem] * len(operands),
        out_specs=[vmem] * 2,
        out_shape=[
            jax.ShapeDtypeStruct((units + padded, 2 * part_x.shape[1]), F32),
            jax.ShapeDtypeStruct((1, classes), F32),
        ],
        scratch_shapes=[pltpu.VMEM((QUAD, units + padded, 2 * part_x.shape[1]), F32)],
        compiler_params=_params(20),
        name="backward",
    )(*operands)


def total_kernel(mine_ref, other_ref, self_ref, neigh_ref, out_ref):
    width, units = self_ref.shape
    classes = out_ref.shape[0]
    grad_in = jnp.transpose(mine_ref[0:units] + other_ref[0:units])
    self_ref[...] = grad_in[0:width]
    neigh_ref[...] = grad_in[width : 2 * width]
    out_ref[...] = (mine_ref[units:] + other_ref[units:])[0:classes]


def total(mine, other, width, units, classes):
    vmem = pl.BlockSpec(memory_space=pltpu.VMEM)
    return pl.pallas_call(
        total_kernel,
        in_specs=[vmem] * 2,
        out_specs=[vmem] * 3,
        out_shape=[
            jax.ShapeDtypeStruct((width, units), F32),
            jax.ShapeDtypeStruct((width, units), F32),
            jax.ShapeDtypeStruct((classes, units), F32),
        ],
        compiler_params=_params(8),
        name="total",
    )(mine, other)


def gathered_body(
    features, cluster, slot, halo_tiles, tile_slots, adjacency, labels, w_self, w_neigh, w_out, b_out
):
    packed = pack(features, cluster, slot, labels, DEVICES)
    early, late = tuple(range(0, 8)), tuple(range(8, 16))
    raw = []

    def first(have):
        raw.extend(turn(adjacency))
        return raw

    have, (near, _), (prior, far) = gather_rows(packed, first, lambda have: (place(have, early), turn_rest(raw[1])))
    part_x, all_labels, agg = aggregate(have, late, prior, (near, far), halo_tiles, tile_slots)
    weighed = []

    def first(have):
        weighed.extend(weights(w_self, w_neigh, w_out, b_out))
        return weighed, own(part_x, agg, weighed[0])

    def ahead(have):
        in_t, out_t, _, bias = weighed
        shared = (part_x, all_labels, in_t, out_t, bias)
        return [forward_pair(have, c, shared) for c in range(QUAD - 1)], forward_one(have, DEVICES - QUAD, shared)

    have, (_, hidden), (held, partner) = gather_plane(agg, first, ahead)
    in_t, out_t, out_p, bias = weighed
    shared = (part_x, all_labels, in_t, out_t, bias)
    *last, mine = forward_last(have, DEVICES - 2, shared, partner, held)
    classes = w_out.shape[1]
    sums, class_weight = backward([*held, last], part_x, all_labels, out_p, mine, swap(mine, 1), classes)
    grad_self, grad_neigh, grad_out = total(sums, swap(sums, 1), *w_self.shape, classes)
    return hidden, grad_self, grad_neigh, grad_out.T, class_weight.reshape(-1)


def split_body(
    features, cluster, slot, halo_tiles, tile_slots, adjacency, labels, w_self, w_neigh, w_out, b_out
):
    rows = features.shape[0]
    width = features.shape[1]
    devices = lax.axis_size("nodes")
    per_peer = rows // devices
    order = jnp.argsort(cluster, stable=True)
    send_rows = features[order].reshape(devices, per_peer, width)
    send_slots = slot[order].reshape(devices, per_peer)
    recv_rows, recv_slots = (
        lax.all_to_all(send_rows, "nodes", split_axis=0, concat_axis=0, tiled=True),
        lax.all_to_all(send_slots, "nodes", split_axis=0, concat_axis=0, tiled=True),
    )
    part_x = (
        jnp.zeros((rows, width), jnp.bfloat16)
        .at[recv_slots.reshape(rows)]
        .set(recv_rows.reshape(rows, width))
    )
    local_tiles = rows // TILE
    wanted = halo_tiles[0]
    gathered = lax.all_gather(part_x, "nodes", axis=0, tiled=True)
    halo = gathered.reshape(-1, TILE, width)[wanted]
    sources = halo[tile_slots]
    adj_tiles = adjacency.reshape(local_tiles, TILE, adjacency.shape[1], TILE)
    agg = jnp.einsum("tikc,tkcf->tif", adj_tiles, sources, preferred_element_type=jnp.float32)
    agg = agg.reshape(rows, width).astype(jnp.bfloat16)
    pre = jnp.dot(part_x, w_self, preferred_element_type=jnp.float32) + jnp.dot(
        agg, w_neigh, preferred_element_type=jnp.float32
    )
    hidden = jnp.maximum(pre, 0.0).astype(jnp.bfloat16)
    logits = jnp.dot(hidden, w_out, preferred_element_type=jnp.float32) + b_out
    lse = jnp.log(jnp.sum(jnp.exp(logits), axis=1))
    classes_row = jnp.arange(w_out.shape[1], dtype=jnp.int32)
    onehot = (labels[:, None] == classes_row[None, :]).astype(jnp.float32)
    picked = jnp.sum(onehot * logits, axis=1)
    ce_rows = lse - picked
    local_loss = jnp.sum(onehot * ce_rows[:, None], axis=0)
    local_counts = jnp.sum(onehot, axis=0)
    loss_sum, counts = lax.psum((local_loss, local_counts), "nodes")
    difficulty = (loss_sum + 1.0) / (counts + 1.0)
    class_weight = difficulty / jnp.mean(difficulty)
    total = jnp.sum(counts)
    row_weight = jnp.sum(onehot * class_weight[None, :], axis=1) / (total + 1.0)
    probs = jnp.exp(logits - lse[:, None])
    dlogits = (row_weight[:, None] * (probs - onehot)).astype(jnp.bfloat16)
    part_out = jnp.dot(hidden.T, dlogits, preferred_element_type=jnp.float32)
    dhidden = jnp.dot(dlogits, w_out.T, preferred_element_type=jnp.float32)
    dpre = jnp.where(hidden > 0, dhidden, 0.0).astype(jnp.bfloat16)
    part_self = jnp.dot(part_x.T, dpre, preferred_element_type=jnp.float32)
    part_neigh = jnp.dot(agg.T, dpre, preferred_element_type=jnp.float32)
    grad_self, grad_neigh, grad_out = lax.psum((part_self, part_neigh, part_out), "nodes")
    return (hidden, grad_self, grad_neigh, grad_out, class_weight)


def solution(mesh):
    def body(*args):
        devices = mesh.shape["nodes"]
        rows = args[0].shape[0]
        per = rows // devices
        classes = args[9].shape[1]
        fits = devices == DEVICES and per == 2 * SUB and classes <= 256
        return (gathered_body if fits else split_body)(*args)

    return jax.shard_map(
        body,
        mesh=mesh,
        in_specs=(
            P(("groups", "nodes"), None),
            P(("groups", "nodes")),
            P(("groups", "nodes")),
            P(("groups", "nodes"), None),
            P(("groups", "nodes"), None),
            P(("groups", "nodes"), None, None),
            P(("groups", "nodes")),
            P(),
            P(),
            P(),
            P(),
        ),
        out_specs=(
            P(("groups", "nodes"), None),
            P("groups", None),
            P("groups", None),
            P("groups", None),
            P("groups"),
        ),
        check_vma=False,
    )
```

```python
import jax
import jax.numpy as jnp
from jax import lax
from jax.experimental import pallas as pl
from jax.experimental.pallas import tpu as pltpu
from jax.sharding import PartitionSpec as P

DEVICES = 16
QUAD = 4
TILE = 128
LANES = 128
SUB = 16
F32 = jnp.float32
BF16 = jnp.bfloat16


def _dot(a, b, contract=((1,), (0,))):
    return lax.dot_general(a, b, (contract, ((), ())), preferred_element_type=F32)


NT = ((1,), (1,))


def _iota(shape, dim):
    return lax.broadcasted_iota(jnp.int32, shape, dim)


def _stay(x):
    return pltpu.with_memory_space_constraint(x, pltpu.HBM)


def _fetch(sources, targets, sems):
    copies = [pltpu.make_async_copy(a, b, sems.at[i]) for i, (a, b) in enumerate(zip(sources, targets))]
    for copy in copies:
        copy.start()
    for copy in copies:
        copy.wait()


def _params(mib):
    return pltpu.CompilerParams(vmem_limit_bytes=mib << 20)


def swap(x, m):
    return lax.ppermute(x, "nodes", [(i, i ^ m) for i in range(DEVICES)])


def gather_all(block, work, cores=True):
    have = {0: block}
    done = []

    def hop(i, m):
        if work[i] is not None:
            have[m], out = lax.optimization_barrier((have[m], work[i](have)))
            done.append(out)

    def cross(*ms):
        if cores:
            have.update({m + 1: swap(have[m], 1) for m in ms})

    have[8], have[4], have[2] = (swap(block, m) for m in (8, 4, 2))
    cross(0)
    hop(0, 8)
    have[12], have[10], have[6] = swap(have[8], 4), swap(have[8], 2), swap(have[4], 2)
    cross(2, 4, 6, 8)
    hop(1, 12)
    have[14] = swap(have[12], 2)
    cross(10, 12)
    hop(2, 14)
    cross(14)
    return have, done


def gather_plane(block, first, second, third):
    have = {0: block}
    have[8], have[4], have[2], have[6] = (swap(block, m) for m in (8, 4, 2, 6))
    have[8], one = lax.optimization_barrier((have[8], first(have)))
    have[12], have[10], have[14] = swap(have[8], 4), swap(have[8], 2), swap(have[8], 6)
    have[10], two = lax.optimization_barrier((have[10], second(have)))
    have[12], three = lax.optimization_barrier((have[12], third(have)))
    return have, one, two, three


def gather_rows(block, first, second, third):
    have = {0: block}
    have[8], have[4], have[2] = (swap(block, m) for m in (8, 4, 2))
    (have[8], have[4], have[2]), one = lax.optimization_barrier(((have[8], have[4], have[2]), first(have)))
    have[12], have[10], have[6] = swap(have[8], 4), swap(have[8], 2), swap(have[4], 2)
    have[1], have[3], have[5], have[7], have[9] = (swap(have[m], 1) for m in (0, 2, 4, 6, 8))
    have[14] = swap(have[12], 2)
    have[11], have[13] = swap(have[10], 1), swap(have[12], 1)
    have[14], two = lax.optimization_barrier((have[14], second(have)))
    have[15] = swap(have[14], 1)
    have[15], three = lax.optimization_barrier((have[15], third(have, two)))
    return have, one, two, three


def pack_kernel(devices, *refs):
    sources, out_ref, targets, sems = refs[0:4], refs[4], refs[5:9], refs[9]
    _fetch(sources, targets, sems)
    feat_ref, cluster_ref, slot_ref, label_ref = targets
    rows = feat_ref.shape[0]
    per = rows // devices
    mine = lax.axis_index("nodes") % (LANES // per)
    cluster = cluster_ref[...]
    member = (_iota((devices, rows), 0) == cluster).astype(F32)
    before = (_iota((rows, rows), 0) < _iota((rows, rows), 1)).astype(BF16)
    rank = jnp.sum(member * _dot(member.astype(BF16), before), axis=0, keepdims=True).astype(jnp.int32)
    take = (_iota((rows, rows), 0) == cluster * per + rank).astype(BF16)
    out_ref[0:devices] = _dot(take, feat_ref[...]).astype(BF16).reshape(devices, per, feat_ref.shape[1])
    place = (_iota((LANES, rows), 0) == mine * per + rank).astype(BF16)
    slots = (member * (slot_ref[...] - rows // 2).astype(F32)).astype(BF16)
    out_ref[devices, 0:SUB] = _dot(slots, place, NT).astype(BF16)
    labels = jnp.concatenate([label_ref[...].astype(F32), jnp.zeros((SUB - label_ref.shape[0], LANES), F32)], axis=0)
    out_ref[devices, SUB : 2 * SUB] = labels.astype(BF16)


def pack(features, cluster, slot, labels, devices):
    rows, width = features.shape
    per = rows // devices
    inputs = (features, cluster.reshape(1, rows), slot.reshape(1, rows), labels.reshape(rows // LANES, LANES))
    inputs = [_stay(x) for x in inputs]
    return pl.pallas_call(
        lambda *refs: pack_kernel(devices, *refs),
        in_specs=[pl.BlockSpec(memory_space=pltpu.HBM)] * 4,
        out_specs=pl.BlockSpec(memory_space=pltpu.VMEM),
        out_shape=jax.ShapeDtypeStruct((devices + 1, per, width), BF16),
        scratch_shapes=[*[pltpu.VMEM(x.shape, x.dtype) for x in inputs], pltpu.SemaphoreType.DMA((4,))],
        compiler_params=_params(8),
        name="pack_rows",
    )(*inputs)


def weights_kernel(*refs):
    sources, (in_t_ref, out_t_ref, out_ref, bias_ref), targets = refs[0:4], refs[4:8], refs[8:12]
    wide, line, sems = refs[12:15]
    _fetch(sources, targets, sems)
    self_ref, neigh_ref, w_out_ref, b_ref = targets
    classes = w_out_ref.shape[0]
    in_t_ref[...] = jnp.transpose(jnp.concatenate([self_ref[...], neigh_ref[...]], axis=0).astype(F32)).astype(BF16)
    wide[...] = jnp.zeros_like(wide)
    wide[0:classes, :] = w_out_ref[...].astype(F32)
    out_t_ref[...] = wide[...].astype(BF16)
    out_ref[...] = jnp.transpose(wide[...]).astype(BF16)
    line[...] = jnp.full_like(line, -1e30)
    line[:, 0:classes] = b_ref[...]
    bias_ref[...] = jnp.transpose(jnp.broadcast_to(line[...], (LANES, line.shape[1])))[0 : bias_ref.shape[0]]


def weights(w_self, w_neigh, w_out, b_out):
    width, units = w_self.shape
    classes = w_out.shape[1]
    padded = -(-classes // SUB) * SUB
    inputs = [_stay(x) for x in (w_self, w_neigh, w_out.T, b_out.reshape(1, classes))]
    return pl.pallas_call(
        weights_kernel,
        in_specs=[pl.BlockSpec(memory_space=pltpu.HBM)] * 4,
        out_specs=[pl.BlockSpec(memory_space=pltpu.VMEM)] * 4,
        out_shape=[
            jax.ShapeDtypeStruct((units, 2 * width), BF16),
            jax.ShapeDtypeStruct((padded, units), BF16),
            jax.ShapeDtypeStruct((units, padded), BF16),
            jax.ShapeDtypeStruct((padded, LANES), F32),
        ],
        scratch_shapes=[
            *[pltpu.VMEM(x.shape, x.dtype) for x in inputs],
            pltpu.VMEM((padded, units), F32),
            pltpu.VMEM((1, 2 * LANES), F32),
            pltpu.SemaphoreType.DMA((4,)),
        ],
        cost_estimate=pl.CostEstimate(flops=0, bytes_accessed=1 << 21, transcendentals=0),
        compiler_params=_params(8),
        name="weights",
    )(*inputs)


def _turn(adj, turned_ref, arrived=None):
    tiles, neigh = turned_ref.shape[0:2]
    side = SUB * SUB
    row = _iota((side, side), 0)
    move = ((row % SUB) * SUB + row // SUB == _iota((side, side), 1)).astype(BF16)
    for t in range(tiles):
        for b in range(TILE // SUB):
            if arrived:
                arrived(t, b)
            for j in range(neigh // (2 * SUB)):
                halves = [
                    adj[t, SUB * b : SUB * (b + 1), SUB * k : SUB * (k + 1), :].reshape(side, TILE)
                    for k in (2 * j, 2 * j + 1)
                ]
                moved = _dot(move, jnp.concatenate(halves, axis=1)).astype(BF16)
                for h in range(2):
                    k = 2 * j + h
                    turned_ref[t, SUB * k : SUB * (k + 1), SUB * b : SUB * (b + 1), :] = moved[
                        :, TILE * h : TILE * (h + 1)
                    ].reshape(SUB, SUB, TILE)


def turn_kernel(adj_ref, turned_ref, rest_ref, adj, sems, rest_sem):
    tiles = turned_ref.shape[0]
    pieces = sems.shape[1]
    part = TILE // pieces
    copies = [
        [
            pltpu.make_async_copy(
                adj_ref.at[pl.ds(t * TILE + i * part, part)], adj.at[t, pl.ds(i * part, part)], sems.at[t, i]
            )
            for i in range(pieces)
        ]
        for t in range(tiles)
    ]
    rest = pltpu.make_async_copy(adj_ref.at[pl.ds(tiles * TILE, rest_ref.shape[0])], rest_ref, rest_sem)
    for copy in sum(copies, []):
        copy.start()
    rest.start()

    def arrived(t, b):
        if b * SUB % part == 0:
            copies[t][b * SUB // part].wait()

    _turn(adj, turned_ref, arrived)
    rest.wait()


def turn(adjacency):
    rows, neigh, tile = adjacency.shape
    tiles = rows // tile // 2
    pieces = 2
    return pl.pallas_call(
        turn_kernel,
        in_specs=[pl.BlockSpec(memory_space=pltpu.HBM)],
        out_specs=[pl.BlockSpec(memory_space=pltpu.VMEM)] * 2,
        out_shape=[
            jax.ShapeDtypeStruct((tiles, neigh, tile, tile), BF16),
            jax.ShapeDtypeStruct((rows - tiles * tile, neigh, tile), BF16),
        ],
        scratch_shapes=[
            pltpu.VMEM((tiles, tile, neigh, tile), BF16),
            pltpu.SemaphoreType.DMA((tiles, pieces)),
            pltpu.SemaphoreType.DMA,
        ],
        cost_estimate=pl.CostEstimate(flops=tiles << 29, bytes_accessed=tiles << 22, transcendentals=0),
        compiler_params=_params(16),
        name="turn_adjacency",
    )(_stay(adjacency))


def turn_rest(rest):
    rows, neigh, tile = rest.shape
    shape = (rows // tile, neigh, tile, tile)
    vmem = pl.BlockSpec(memory_space=pltpu.VMEM)
    return pl.pallas_call(
        _turn,
        in_specs=[vmem],
        out_specs=vmem,
        out_shape=jax.ShapeDtypeStruct(shape, BF16),
        cost_estimate=pl.CostEstimate(flops=shape[0] << 29, bytes_accessed=shape[0] << 21, transcendentals=0),
        compiler_params=_params(12),
        name="turn_rest",
    )(rest.reshape(rows // tile, tile, neigh, tile))


def _place(ms, blocks, prior, px_ref, labels_ref, got):
    me = lax.axis_index("nodes")
    per = blocks[0].shape[1]
    rows = DEVICES * per
    if prior:
        labels_ref[...] = prior[1][...]
    slots = []
    for q in range(len(ms) // QUAD):
        held = 0.0
        for m, block in list(zip(ms, blocks))[q * QUAD : (q + 1) * QUAD]:
            at = q * LANES + ((me % QUAD) ^ (m % QUAD)) * per
            got[:, pl.ds(pl.multiple_of(at, per), per), :] = block[0:DEVICES]
            held += block[DEVICES, 0:SUB, :].astype(F32)
            labels_ref[me ^ m] = block[DEVICES, SUB : 2 * SUB, :]
        slots.append(held)
    slots = jnp.concatenate(slots, axis=1).astype(jnp.int32)
    position = _iota((rows, slots.shape[1]), 0) - rows // 2
    for p in range(DEVICES):
        put = (position == slots[p : p + 1, :]).astype(BF16)
        placed = _dot(put, got[p])
        if prior:
            placed += prior[0][p * rows : (p + 1) * rows, :].astype(F32)
        px_ref[p * rows : (p + 1) * rows, :] = placed.astype(BF16)


def _placed(per, width):
    return [
        jax.ShapeDtypeStruct((DEVICES * DEVICES * per, width), BF16),
        jax.ShapeDtypeStruct((DEVICES, SUB, LANES), BF16),
    ]


def place(have, ms, prior=()):
    per, width = have[0].shape[1:]
    vmem = pl.BlockSpec(memory_space=pltpu.VMEM)
    n = len(ms) + len(prior)
    return pl.pallas_call(
        lambda *refs: _place(ms, refs[: len(ms)], refs[len(ms) : n], *refs[n:]),
        in_specs=[vmem] * n,
        out_specs=[vmem] * 2,
        out_shape=_placed(per, width),
        scratch_shapes=[pltpu.VMEM((DEVICES, len(ms) * per, width), BF16)],
        cost_estimate=pl.CostEstimate(flops=1 << 30, bytes_accessed=1 << 22, transcendentals=0),
        compiler_params=_params(16),
        name="place",
    )(*[have[m] for m in ms], *prior)


def aggregate_kernel(ms, parts, *refs):
    n = len(ms)
    blocks, prior, turned, refs = refs[:n], refs[n : n + 2], refs[n + 2 : n + 2 + parts], refs[n + 2 + parts :]
    halo_ref, slots_ref, px_ref, labels_ref, agg_ref, got = refs
    _place(ms, blocks, prior, px_ref, labels_ref, got)
    neigh = slots_ref.shape[1]
    tiles = [ref.at[t] for ref in turned for t in range(ref.shape[0])]
    for t, adj in enumerate(tiles):
        total = jnp.zeros((TILE, px_ref.shape[1]), F32)
        for k in range(0, neigh, 2):
            sources = []
            for j in (k, k + 1):
                tile = halo_ref[0, slots_ref[t, j]]
                sources.append(px_ref[pl.ds(pl.multiple_of(tile * TILE, TILE), TILE), :])
            total += _dot(jnp.concatenate([adj[k], adj[k + 1]], axis=1), jnp.concatenate(sources, axis=0))
        agg_ref[t * TILE : (t + 1) * TILE, :] = total.astype(BF16)


def aggregate(have, ms, prior, turned, halo_tiles, tile_slots):
    per, width = have[0].shape[1:]
    scalars = pl.BlockSpec(memory_space=pltpu.SMEM)
    vmem = pl.BlockSpec(memory_space=pltpu.VMEM)
    return pl.pallas_call(
        lambda *refs: aggregate_kernel(ms, len(turned), *refs),
        in_specs=[vmem] * (len(ms) + 2 + len(turned)) + [scalars] * 2,
        out_specs=[vmem] * 3,
        out_shape=[*_placed(per, width), jax.ShapeDtypeStruct((DEVICES * per, width), BF16)],
        scratch_shapes=[pltpu.VMEM((DEVICES, len(ms) * per, width), BF16)],
        compiler_params=_params(24),
        name="aggregate",
    )(*[have[m] for m in ms], *prior, *turned, halo_tiles, tile_slots)


def _owner(pair, o):
    return pair * QUAD + 2 * o + lax.axis_index("nodes") % 2


def _hot(kinds, labels_ref, owner):
    held = labels_ref[owner].astype(F32)
    return [kinds == held[j : j + 1, :].astype(jnp.int32) for j in range(QUAD)]


def _rows(owner, px_ref, rows):
    return px_ref[pl.ds(pl.multiple_of(owner * rows, rows), rows), :]


def _inputs(pair, px_ref, agg_ref):
    rows = agg_ref.shape[0] // 2
    x = [_rows(_owner(pair, o), px_ref, rows) for o in range(2)]
    return jnp.concatenate([jnp.concatenate(x, axis=0), agg_ref[...]], axis=1)


def _forward(owners, inputs, labels_ref, in_t_ref, out_t_ref, bias_ref, keep):
    hidden = jnp.maximum(_dot(in_t_ref[...], inputs, NT), 0.0).astype(BF16)
    logits = _dot(out_t_ref[...], hidden) + jnp.concatenate([bias_ref[...]] * (hidden.shape[1] // LANES), axis=1)
    logits -= jnp.log(jnp.sum(jnp.exp(logits), axis=0, keepdims=True))
    probs = jnp.exp(logits)
    kinds = _iota(bias_ref.shape, 0)
    loss = count = jnp.zeros(bias_ref.shape, F32)
    lane = 0
    for owner in owners:
        for hot in _hot(kinds, labels_ref, owner):
            cut = slice(lane, lane + LANES)
            one = hot.astype(F32)
            loss -= jnp.where(hot, logits[:, cut], 0.0)
            count += one
            keep(cut, probs[:, cut] - one)
            lane += LANES
    return hidden, loss, count


def pair_kernel(c, *refs):
    blocks, (px_ref, *shared), outs = refs[0:2], refs[2:7], refs[7:12]
    agg_ref, hid_ref, slope_ref, loss_ref, count_ref = outs
    me = lax.axis_index("nodes")
    pair = (me // QUAD) ^ c
    rows = blocks[0].shape[0]
    for o, block in enumerate(blocks):
        at = ((me // 2 % 2) ^ o) * rows
        agg_ref[pl.ds(pl.multiple_of(at, rows), rows), :] = block[...]

    def keep(cut, x):
        slope_ref[:, cut] = x

    owners = [_owner(pair, o) for o in range(2)]
    hid_ref[...], loss_ref[...], count_ref[...] = _forward(owners, _inputs(pair, px_ref, agg_ref), *shared, keep)


def one_kernel(m, *refs):
    block, (px_ref, *shared), (hid_ref, slope_ref, loss_ref, count_ref) = refs[0], refs[1:6], refs[6:10]
    owner = lax.axis_index("nodes") ^ m
    inputs = jnp.concatenate([_rows(owner, px_ref, block.shape[0]), block[...]], axis=1)

    def keep(cut, x):
        slope_ref[:, cut] = x

    hid_ref[...], loss_ref[...], count_ref[...] = _forward([owner], inputs, *shared, keep)


def last_kernel(m, *refs):
    blocks, (px_ref, *shared), partner, prior = refs[0:2], refs[2:7], refs[7:11], refs[11:17]
    agg_ref, hid_ref, slope_ref, stats_ref, part, losses, counts = refs[17:]
    me = lax.axis_index("nodes")
    rows = blocks[0].shape[0]
    at = [pl.ds(pl.multiple_of(((me // 2 % 2) ^ o) * rows, rows), rows) for o in range(2)]
    for o, block in enumerate(blocks):
        agg_ref[at[o], :] = block[...]
    hid_ref[:, at[0]], slope_ref[:, at[0]] = partner[0][...], partner[1][...]

    def keep(cut, x):
        part[:, cut] = x

    inputs = jnp.concatenate([_rows(me ^ m, px_ref, rows), blocks[1][...]], axis=1)
    hidden, loss, count = _forward([me ^ m], inputs, *shared, keep)
    hid_ref[:, at[1]], slope_ref[:, at[1]] = hidden, part[...]
    mine = me // QUAD
    for c in range(QUAD - 1):
        losses[mine ^ c], counts[mine ^ c] = prior[2 * c][...], prior[2 * c + 1][...]
    losses[mine ^ (QUAD - 1)], counts[mine ^ (QUAD - 1)] = loss + partner[2][...], count + partner[3][...]
    loss, count = (jnp.sum(sum(x[q] for q in range(QUAD)), axis=1, keepdims=True) for x in (losses, counts))
    stats_ref[...] = jnp.where(_iota(stats_ref.shape, 1) == 0, loss, count)


def own_kernel(px_ref, agg_ref, in_t_ref, hidden_ref):
    rows = agg_ref.shape[0]
    x = px_ref[pl.ds(pl.multiple_of(lax.axis_index("nodes") * rows, rows), rows), :]
    pre = _dot(jnp.concatenate([x, agg_ref[...]], axis=1), in_t_ref[...], NT)
    hidden_ref[...] = jnp.maximum(pre, 0.0).astype(BF16)


def own(part_x, agg, in_t):
    vmem = pl.BlockSpec(memory_space=pltpu.VMEM)
    return pl.pallas_call(
        own_kernel,
        in_specs=[vmem] * 3,
        out_specs=vmem,
        out_shape=jax.ShapeDtypeStruct((agg.shape[0], in_t.shape[0]), BF16),
        cost_estimate=pl.CostEstimate(flops=1 << 26, bytes_accessed=1 << 18, transcendentals=0),
        compiler_params=_params(8),
        name="own",
    )(part_x, agg, in_t)


def _call(kernel, name, shapes, operands, scratch=()):
    vmem = pl.BlockSpec(memory_space=pltpu.VMEM)
    return pl.pallas_call(
        kernel,
        in_specs=[vmem] * len(operands),
        out_specs=[vmem] * len(shapes),
        out_shape=[jax.ShapeDtypeStruct(*x) for x in shapes],
        scratch_shapes=[pltpu.VMEM(*x) for x in scratch],
        cost_estimate=pl.CostEstimate(flops=1 << 29, bytes_accessed=1 << 21, transcendentals=1 << 18),
        compiler_params=_params(12),
        name=name,
    )(*operands)


def forward_pair(have, c, shared):
    rows, width = have[0].shape
    units, padded = shared[2].shape[0], shared[4].shape[0]
    stat = ((padded, LANES), F32)
    shapes = [((2 * rows, width), BF16), ((units, 2 * rows), BF16), ((padded, 2 * rows), F32), stat, stat]
    return _call(lambda *refs: pair_kernel(c, *refs), "forward_pair", shapes, [have[4 * c], have[4 * c + 2], *shared])


def forward_one(have, m, shared):
    rows, units, padded = have[0].shape[0], shared[2].shape[0], shared[4].shape[0]
    stat = ((padded, LANES), F32)
    shapes = [((units, rows), BF16), ((padded, rows), F32), stat, stat]
    return _call(lambda *refs: one_kernel(m, *refs), "forward_one", shapes, [have[m], *shared])


def forward_last(have, m, shared, partner, prior):
    rows, width = have[0].shape
    units, padded = shared[2].shape[0], shared[4].shape[0]
    stat = ((padded, LANES), F32)
    shapes = [((2 * rows, width), BF16), ((units, 2 * rows), BF16), ((padded, 2 * rows), F32), stat]
    stats = [x for held in prior for x in held[3:5]]
    scratch = [((padded, rows), F32)] + [((QUAD, padded, LANES), F32)] * 2
    operands = [have[m - 2], have[m], *shared, *partner, *stats]
    return _call(lambda *refs: last_kernel(m, *refs), "forward_last", shapes, operands, scratch)


def backward_kernel(classes, *refs):
    held, refs = [refs[3 * c : 3 * c + 3] for c in range(QUAD)], refs[3 * QUAD :]
    px_ref, labels_ref, out_ref, mine_ref, other_ref, sums_ref, class_ref, grads = refs
    me = lax.axis_index("nodes")
    padded = mine_ref.shape[0]
    units = out_ref.shape[0]

    both = mine_ref[...] + other_ref[...]
    loss, count = both[:, 0:1], both[:, 1:2]
    real = _iota((padded, 1), 0) < classes
    difficulty = jnp.where(real, (loss + 1.0) / (count + 1.0), 0.0)
    weight = difficulty / (jnp.sum(difficulty, axis=0, keepdims=True) / classes)
    share = 1.0 / (1.0 + jnp.sum(count, axis=0, keepdims=True))
    class_ref[...] = jnp.transpose(jnp.broadcast_to(weight, (padded, LANES)))[0:1, 0:classes]
    scaled = jnp.broadcast_to(weight * share, (padded, LANES))

    kinds = _iota((padded, LANES), 0)
    for c, (agg_ref, hid_ref, slope_ref) in enumerate(held):
        pair = (me // QUAD) ^ c
        parts = []
        for o in range(2):
            for hot in _hot(kinds, labels_ref, _owner(pair, o)):
                row = jnp.sum(jnp.where(hot, scaled, 0.0), axis=0, keepdims=True)
                cut = slice(LANES * len(parts), LANES * (len(parts) + 1))
                parts.append((row * slope_ref[:, cut]).astype(BF16))
        dlogits = jnp.concatenate(parts, axis=1)
        hidden = hid_ref[...]
        dpre = jnp.where(hidden > 0, _dot(out_ref[...], dlogits), 0.0).astype(BF16)
        grads[pair, 0:units] = _dot(dpre, _inputs(pair, px_ref, agg_ref))
        grads[pair, units : units + padded] = _dot(dlogits, hidden, NT)
    sums_ref[...] = sum(grads[q] for q in range(QUAD))


def backward(held, part_x, labels, out_p, mine, other, classes):
    units, padded = out_p.shape
    vmem = pl.BlockSpec(memory_space=pltpu.VMEM)
    operands = [*[x for h in held for x in h[0:3]], part_x, labels, out_p, mine, other]
    return pl.pallas_call(
        lambda *refs: backward_kernel(classes, *refs),
        in_specs=[vmem] * len(operands),
        out_specs=[vmem] * 2,
        out_shape=[
            jax.ShapeDtypeStruct((units + padded, 2 * part_x.shape[1]), F32),
            jax.ShapeDtypeStruct((1, classes), F32),
        ],
        scratch_shapes=[pltpu.VMEM((QUAD, units + padded, 2 * part_x.shape[1]), F32)],
        compiler_params=_params(20),
        name="backward",
    )(*operands)


def total_kernel(mine_ref, other_ref, self_ref, neigh_ref, out_ref):
    width, units = self_ref.shape
    classes = out_ref.shape[0]
    grad_in = jnp.transpose(mine_ref[0:units] + other_ref[0:units])
    self_ref[...] = grad_in[0:width]
    neigh_ref[...] = grad_in[width : 2 * width]
    out_ref[...] = (mine_ref[units:] + other_ref[units:])[0:classes]


def total(mine, other, width, units, classes):
    vmem = pl.BlockSpec(memory_space=pltpu.VMEM)
    return pl.pallas_call(
        total_kernel,
        in_specs=[vmem] * 2,
        out_specs=[vmem] * 3,
        out_shape=[
            jax.ShapeDtypeStruct((width, units), F32),
            jax.ShapeDtypeStruct((width, units), F32),
            jax.ShapeDtypeStruct((classes, units), F32),
        ],
        compiler_params=_params(8),
        name="total",
    )(mine, other)


def gathered_body(
    features, cluster, slot, halo_tiles, tile_slots, adjacency, labels, w_self, w_neigh, w_out, b_out
):
    packed = pack(features, cluster, slot, labels, DEVICES)
    raw = []

    def first(have):
        raw.extend(turn(adjacency))
        return raw

    have, (near, _), (_, far), prior = gather_rows(
        packed,
        first,
        lambda have: (place(have, range(0, 8)), turn_rest(raw[1])),
        lambda have, done: place(have, range(8, 12), done[0]),
    )
    late = range(12, 16)
    part_x, all_labels, agg = aggregate(have, late, prior, (near, far), halo_tiles, tile_slots)
    weighed = []

    def first(have):
        weighed.extend(weights(w_self, w_neigh, w_out, b_out))
        return weighed, own(part_x, agg, weighed[0])

    def ahead(cs):
        def work(have):
            in_t, out_t, _, bias = weighed
            return [forward_pair(have, c, (part_x, all_labels, in_t, out_t, bias)) for c in cs]

        return work

    have, (_, hidden), two, three = gather_plane(agg, first, ahead((0, 1)), ahead((2,)))
    held = [*two, *three]
    in_t, out_t, out_p, bias = weighed
    shared = (part_x, all_labels, in_t, out_t, bias)
    partner = forward_one(have, DEVICES - QUAD, shared)
    *last, mine = forward_last(have, DEVICES - 2, shared, partner, held)
    classes = w_out.shape[1]
    sums, class_weight = backward([*held, last], part_x, all_labels, out_p, mine, swap(mine, 1), classes)
    grad_self, grad_neigh, grad_out = total(sums, swap(sums, 1), *w_self.shape, classes)
    return hidden, grad_self, grad_neigh, grad_out.T, class_weight.reshape(-1)


def split_body(
    features, cluster, slot, halo_tiles, tile_slots, adjacency, labels, w_self, w_neigh, w_out, b_out
):
    rows = features.shape[0]
    width = features.shape[1]
    devices = lax.axis_size("nodes")
    per_peer = rows // devices
    order = jnp.argsort(cluster, stable=True)
    send_rows = features[order].reshape(devices, per_peer, width)
    send_slots = slot[order].reshape(devices, per_peer)
    recv_rows, recv_slots = (
        lax.all_to_all(send_rows, "nodes", split_axis=0, concat_axis=0, tiled=True),
        lax.all_to_all(send_slots, "nodes", split_axis=0, concat_axis=0, tiled=True),
    )
    part_x = (
        jnp.zeros((rows, width), jnp.bfloat16)
        .at[recv_slots.reshape(rows)]
        .set(recv_rows.reshape(rows, width))
    )
    local_tiles = rows // TILE
    wanted = halo_tiles[0]
    gathered = lax.all_gather(part_x, "nodes", axis=0, tiled=True)
    halo = gathered.reshape(-1, TILE, width)[wanted]
    sources = halo[tile_slots]
    adj_tiles = adjacency.reshape(local_tiles, TILE, adjacency.shape[1], TILE)
    agg = jnp.einsum("tikc,tkcf->tif", adj_tiles, sources, preferred_element_type=jnp.float32)
    agg = agg.reshape(rows, width).astype(jnp.bfloat16)
    pre = jnp.dot(part_x, w_self, preferred_element_type=jnp.float32) + jnp.dot(
        agg, w_neigh, preferred_element_type=jnp.float32
    )
    hidden = jnp.maximum(pre, 0.0).astype(jnp.bfloat16)
    logits = jnp.dot(hidden, w_out, preferred_element_type=jnp.float32) + b_out
    lse = jnp.log(jnp.sum(jnp.exp(logits), axis=1))
    classes_row = jnp.arange(w_out.shape[1], dtype=jnp.int32)
    onehot = (labels[:, None] == classes_row[None, :]).astype(jnp.float32)
    picked = jnp.sum(onehot * logits, axis=1)
    ce_rows = lse - picked
    local_loss = jnp.sum(onehot * ce_rows[:, None], axis=0)
    local_counts = jnp.sum(onehot, axis=0)
    loss_sum, counts = lax.psum((local_loss, local_counts), "nodes")
    difficulty = (loss_sum + 1.0) / (counts + 1.0)
    class_weight = difficulty / jnp.mean(difficulty)
    total = jnp.sum(counts)
    row_weight = jnp.sum(onehot * class_weight[None, :], axis=1) / (total + 1.0)
    probs = jnp.exp(logits - lse[:, None])
    dlogits = (row_weight[:, None] * (probs - onehot)).astype(jnp.bfloat16)
    part_out = jnp.dot(hidden.T, dlogits, preferred_element_type=jnp.float32)
    dhidden = jnp.dot(dlogits, w_out.T, preferred_element_type=jnp.float32)
    dpre = jnp.where(hidden > 0, dhidden, 0.0).astype(jnp.bfloat16)
    part_self = jnp.dot(part_x.T, dpre, preferred_element_type=jnp.float32)
    part_neigh = jnp.dot(agg.T, dpre, preferred_element_type=jnp.float32)
    grad_self, grad_neigh, grad_out = lax.psum((part_self, part_neigh, part_out), "nodes")
    return (hidden, grad_self, grad_neigh, grad_out, class_weight)


def solution(mesh):
    def body(*args):
        devices = mesh.shape["nodes"]
        rows = args[0].shape[0]
        per = rows // devices
        classes = args[9].shape[1]
        fits = devices == DEVICES and per == 2 * SUB and classes <= 256
        return (gathered_body if fits else split_body)(*args)

    return jax.shard_map(
        body,
        mesh=mesh,
        in_specs=(
            P(("groups", "nodes"), None),
            P(("groups", "nodes")),
            P(("groups", "nodes")),
            P(("groups", "nodes"), None),
            P(("groups", "nodes"), None),
            P(("groups", "nodes"), None, None),
            P(("groups", "nodes")),
            P(),
            P(),
            P(),
            P(),
        ),
        out_specs=(
            P(("groups", "nodes"), None),
            P("groups", None),
            P("groups", None),
            P("groups", None),
            P("groups"),
        ),
        check_vma=False,
    )
```

```python
import jax
import jax.numpy as jnp
from jax import lax
from jax.experimental import pallas as pl
from jax.experimental.pallas import tpu as pltpu
from jax.sharding import PartitionSpec as P

DEVICES = 16
QUAD = 4
TILE = 128
LANES = 128
SUB = 16
F32 = jnp.float32
BF16 = jnp.bfloat16


def _dot(a, b, contract=((1,), (0,))):
    return lax.dot_general(a, b, (contract, ((), ())), preferred_element_type=F32)


NT = ((1,), (1,))


def _iota(shape, dim):
    return lax.broadcasted_iota(jnp.int32, shape, dim)


def _stay(x):
    return pltpu.with_memory_space_constraint(x, pltpu.HBM)


def _fetch(sources, targets, sems):
    copies = [pltpu.make_async_copy(a, b, sems.at[i]) for i, (a, b) in enumerate(zip(sources, targets))]
    for copy in copies:
        copy.start()
    for copy in copies:
        copy.wait()


def _params(mib):
    return pltpu.CompilerParams(vmem_limit_bytes=mib << 20)


def swap(x, m):
    return lax.ppermute(x, "nodes", [(i, i ^ m) for i in range(DEVICES)])


def gather_all(block, work, cores=True):
    have = {0: block}
    done = []

    def hop(i, m):
        if work[i] is not None:
            have[m], out = lax.optimization_barrier((have[m], work[i](have)))
            done.append(out)

    def cross(*ms):
        if cores:
            have.update({m + 1: swap(have[m], 1) for m in ms})

    have[8], have[4], have[2] = (swap(block, m) for m in (8, 4, 2))
    cross(0)
    hop(0, 8)
    have[12], have[10], have[6] = swap(have[8], 4), swap(have[8], 2), swap(have[4], 2)
    cross(2, 4, 6, 8)
    hop(1, 12)
    have[14] = swap(have[12], 2)
    cross(10, 12)
    hop(2, 14)
    cross(14)
    return have, done


def gather_plane(block, first, second, third):
    have = {0: block}
    have[8], have[4], have[2], have[6] = (swap(block, m) for m in (8, 4, 2, 6))
    have[8], one = lax.optimization_barrier((have[8], first(have)))
    have[12], have[10], have[14] = swap(have[8], 4), swap(have[8], 2), swap(have[8], 6)
    have[10], two = lax.optimization_barrier((have[10], second(have)))
    have[12], three = lax.optimization_barrier((have[12], third(have)))
    return have, one, two, three


def gather_rows(block, first, second, third):
    have = {0: block}
    have[8], have[4], have[2] = (swap(block, m) for m in (8, 4, 2))
    (have[8], have[4], have[2]), one = lax.optimization_barrier(((have[8], have[4], have[2]), first(have)))
    have[12], have[10], have[6] = swap(have[8], 4), swap(have[8], 2), swap(have[4], 2)
    have[1], have[3], have[5], have[7], have[9] = (swap(have[m], 1) for m in (0, 2, 4, 6, 8))
    have[14] = swap(have[12], 2)
    have[11], have[13] = swap(have[10], 1), swap(have[12], 1)
    have[14], two = lax.optimization_barrier((have[14], second(have)))
    have[15] = swap(have[14], 1)
    have[15], three = lax.optimization_barrier((have[15], third(have, two)))
    return have, one, two, three


def pack_kernel(devices, *refs):
    sources, out_ref, targets, sems = refs[0:4], refs[4], refs[5:9], refs[9]
    _fetch(sources, targets, sems)
    feat_ref, cluster_ref, slot_ref, label_ref = targets
    rows = feat_ref.shape[0]
    per = rows // devices
    mine = lax.axis_index("nodes") % (LANES // per)
    cluster = cluster_ref[...]
    member = (_iota((devices, rows), 0) == cluster).astype(F32)
    before = (_iota((rows, rows), 0) < _iota((rows, rows), 1)).astype(BF16)
    rank = jnp.sum(member * _dot(member.astype(BF16), before), axis=0, keepdims=True).astype(jnp.int32)
    take = (_iota((rows, rows), 0) == cluster * per + rank).astype(BF16)
    out_ref[0:devices] = _dot(take, feat_ref[...]).astype(BF16).reshape(devices, per, feat_ref.shape[1])
    place = (_iota((LANES, rows), 0) == mine * per + rank).astype(BF16)
    slots = (member * (slot_ref[...] - rows // 2).astype(F32)).astype(BF16)
    out_ref[devices, 0:SUB] = _dot(slots, place, NT).astype(BF16)
    labels = jnp.concatenate([label_ref[...].astype(F32), jnp.zeros((SUB - label_ref.shape[0], LANES), F32)], axis=0)
    out_ref[devices, SUB : 2 * SUB] = labels.astype(BF16)


def pack(features, cluster, slot, labels, devices):
    rows, width = features.shape
    per = rows // devices
    inputs = (features, cluster.reshape(1, rows), slot.reshape(1, rows), labels.reshape(rows // LANES, LANES))
    inputs = [_stay(x) for x in inputs]
    return pl.pallas_call(
        lambda *refs: pack_kernel(devices, *refs),
        in_specs=[pl.BlockSpec(memory_space=pltpu.HBM)] * 4,
        out_specs=pl.BlockSpec(memory_space=pltpu.VMEM),
        out_shape=jax.ShapeDtypeStruct((devices + 1, per, width), BF16),
        scratch_shapes=[*[pltpu.VMEM(x.shape, x.dtype) for x in inputs], pltpu.SemaphoreType.DMA((4,))],
        compiler_params=_params(8),
        name="pack_rows",
    )(*inputs)


def weights_kernel(*refs):
    sources, w_out_ref, (in_t_ref, out_t_ref, out_ref, bias_ref), targets = refs[0:3], refs[3], refs[4:8], refs[8:11]
    wide, line, sems = refs[11:14]
    _fetch(sources, targets, sems)
    self_ref, neigh_ref, b_ref = targets
    classes = w_out_ref.shape[0]
    in_t_ref[...] = jnp.transpose(jnp.concatenate([self_ref[...], neigh_ref[...]], axis=0).astype(F32)).astype(BF16)
    wide[...] = jnp.zeros_like(wide)
    wide[0:classes, :] = w_out_ref[...].astype(F32)
    out_t_ref[...] = wide[...].astype(BF16)
    out_ref[...] = jnp.transpose(wide[...]).astype(BF16)
    line[...] = jnp.full_like(line, -1e30)
    line[:, 0:classes] = b_ref[...]
    bias_ref[...] = jnp.transpose(jnp.broadcast_to(line[...], (LANES, line.shape[1])))[0 : bias_ref.shape[0]]


def weights(w_self, w_neigh, w_out, b_out):
    width, units = w_self.shape
    classes = w_out.shape[1]
    padded = -(-classes // SUB) * SUB
    inputs = [_stay(x) for x in (w_self, w_neigh, b_out.reshape(1, classes))]
    return pl.pallas_call(
        weights_kernel,
        in_specs=[pl.BlockSpec(memory_space=pltpu.HBM)] * 3 + [pl.BlockSpec(memory_space=pltpu.VMEM)],
        out_specs=[pl.BlockSpec(memory_space=pltpu.VMEM)] * 4,
        out_shape=[
            jax.ShapeDtypeStruct((units, 2 * width), BF16),
            jax.ShapeDtypeStruct((padded, units), BF16),
            jax.ShapeDtypeStruct((units, padded), BF16),
            jax.ShapeDtypeStruct((padded, LANES), F32),
        ],
        scratch_shapes=[
            *[pltpu.VMEM(x.shape, x.dtype) for x in inputs],
            pltpu.VMEM((padded, units), F32),
            pltpu.VMEM((1, 2 * LANES), F32),
            pltpu.SemaphoreType.DMA((3,)),
        ],
        cost_estimate=pl.CostEstimate(flops=0, bytes_accessed=1 << 21, transcendentals=0),
        compiler_params=_params(8),
        name="weights",
    )(*inputs, w_out.T)


def _turn(adj, turned_ref, arrived=None):
    tiles, neigh = turned_ref.shape[0:2]
    side = SUB * SUB
    row = _iota((side, side), 0)
    move = ((row % SUB) * SUB + row // SUB == _iota((side, side), 1)).astype(BF16)
    for t in range(tiles):
        for b in range(TILE // SUB):
            if arrived:
                arrived(t, b)
            for j in range(neigh // (2 * SUB)):
                halves = [
                    adj[t, SUB * b : SUB * (b + 1), SUB * k : SUB * (k + 1), :].reshape(side, TILE)
                    for k in (2 * j, 2 * j + 1)
                ]
                moved = _dot(move, jnp.concatenate(halves, axis=1)).astype(BF16)
                for h in range(2):
                    k = 2 * j + h
                    turned_ref[t, SUB * k : SUB * (k + 1), SUB * b : SUB * (b + 1), :] = moved[
                        :, TILE * h : TILE * (h + 1)
                    ].reshape(SUB, SUB, TILE)


def turn_kernel(adj_ref, turned_ref, rest_ref, adj, sems, rest_sem):
    tiles = turned_ref.shape[0]
    pieces = sems.shape[1]
    part = TILE // pieces
    copies = [
        [
            pltpu.make_async_copy(
                adj_ref.at[pl.ds(t * TILE + i * part, part)], adj.at[t, pl.ds(i * part, part)], sems.at[t, i]
            )
            for i in range(pieces)
        ]
        for t in range(tiles)
    ]
    rest = pltpu.make_async_copy(adj_ref.at[pl.ds(tiles * TILE, rest_ref.shape[0])], rest_ref, rest_sem)
    for copy in sum(copies, []):
        copy.start()
    rest.start()

    def arrived(t, b):
        if b * SUB % part == 0:
            copies[t][b * SUB // part].wait()

    _turn(adj, turned_ref, arrived)
    rest.wait()


def turn(adjacency):
    rows, neigh, tile = adjacency.shape
    tiles = rows // tile // 2
    pieces = 2
    return pl.pallas_call(
        turn_kernel,
        in_specs=[pl.BlockSpec(memory_space=pltpu.HBM)],
        out_specs=[pl.BlockSpec(memory_space=pltpu.VMEM)] * 2,
        out_shape=[
            jax.ShapeDtypeStruct((tiles, neigh, tile, tile), BF16),
            jax.ShapeDtypeStruct((rows - tiles * tile, neigh, tile), BF16),
        ],
        scratch_shapes=[
            pltpu.VMEM((tiles, tile, neigh, tile), BF16),
            pltpu.SemaphoreType.DMA((tiles, pieces)),
            pltpu.SemaphoreType.DMA,
        ],
        cost_estimate=pl.CostEstimate(flops=tiles << 29, bytes_accessed=tiles << 22, transcendentals=0),
        compiler_params=_params(16),
        name="turn_adjacency",
    )(_stay(adjacency))


def turn_rest(rest):
    rows, neigh, tile = rest.shape
    shape = (rows // tile, neigh, tile, tile)
    vmem = pl.BlockSpec(memory_space=pltpu.VMEM)
    return pl.pallas_call(
        _turn,
        in_specs=[vmem],
        out_specs=vmem,
        out_shape=jax.ShapeDtypeStruct(shape, BF16),
        cost_estimate=pl.CostEstimate(flops=shape[0] << 29, bytes_accessed=shape[0] << 21, transcendentals=0),
        compiler_params=_params(12),
        name="turn_rest",
    )(rest.reshape(rows // tile, tile, neigh, tile))


def _place(ms, blocks, prior, px_ref, labels_ref, got):
    me = lax.axis_index("nodes")
    per = blocks[0].shape[1]
    rows = DEVICES * per
    if prior:
        labels_ref[...] = prior[1][...]
    slots = []
    for q in range(len(ms) // QUAD):
        held = 0.0
        for m, block in list(zip(ms, blocks))[q * QUAD : (q + 1) * QUAD]:
            at = q * LANES + ((me % QUAD) ^ (m % QUAD)) * per
            got[:, pl.ds(pl.multiple_of(at, per), per), :] = block[0:DEVICES]
            held += block[DEVICES, 0:SUB, :].astype(F32)
            labels_ref[me ^ m] = block[DEVICES, SUB : 2 * SUB, :]
        slots.append(held)
    slots = jnp.concatenate(slots, axis=1).astype(jnp.int32)
    position = _iota((rows, slots.shape[1]), 0) - rows // 2
    for p in range(DEVICES):
        put = (position == slots[p : p + 1, :]).astype(BF16)
        placed = _dot(put, got[p])
        if prior:
            placed += prior[0][p * rows : (p + 1) * rows, :].astype(F32)
        px_ref[p * rows : (p + 1) * rows, :] = placed.astype(BF16)


def _placed(per, width):
    return [
        jax.ShapeDtypeStruct((DEVICES * DEVICES * per, width), BF16),
        jax.ShapeDtypeStruct((DEVICES, SUB, LANES), BF16),
    ]


def place(have, ms, prior=()):
    per, width = have[0].shape[1:]
    vmem = pl.BlockSpec(memory_space=pltpu.VMEM)
    n = len(ms) + len(prior)
    return pl.pallas_call(
        lambda *refs: _place(ms, refs[: len(ms)], refs[len(ms) : n], *refs[n:]),
        in_specs=[vmem] * n,
        out_specs=[vmem] * 2,
        out_shape=_placed(per, width),
        scratch_shapes=[pltpu.VMEM((DEVICES, len(ms) * per, width), BF16)],
        cost_estimate=pl.CostEstimate(flops=1 << 30, bytes_accessed=1 << 22, transcendentals=0),
        compiler_params=_params(16),
        name="place",
    )(*[have[m] for m in ms], *prior)


def aggregate_kernel(ms, parts, *refs):
    n = len(ms)
    blocks, prior, turned, refs = refs[:n], refs[n : n + 2], refs[n + 2 : n + 2 + parts], refs[n + 2 + parts :]
    halo_ref, slots_ref, px_ref, labels_ref, agg_ref, got = refs
    _place(ms, blocks, prior, px_ref, labels_ref, got)
    neigh = slots_ref.shape[1]
    tiles = [ref.at[t] for ref in turned for t in range(ref.shape[0])]
    for t, adj in enumerate(tiles):
        total = jnp.zeros((TILE, px_ref.shape[1]), F32)
        for k in range(0, neigh, 2):
            sources = []
            for j in (k, k + 1):
                tile = halo_ref[0, slots_ref[t, j]]
                sources.append(px_ref[pl.ds(pl.multiple_of(tile * TILE, TILE), TILE), :])
            total += _dot(jnp.concatenate([adj[k], adj[k + 1]], axis=1), jnp.concatenate(sources, axis=0))
        agg_ref[t * TILE : (t + 1) * TILE, :] = total.astype(BF16)


def aggregate(have, ms, prior, turned, halo_tiles, tile_slots):
    per, width = have[0].shape[1:]
    scalars = pl.BlockSpec(memory_space=pltpu.SMEM)
    vmem = pl.BlockSpec(memory_space=pltpu.VMEM)
    return pl.pallas_call(
        lambda *refs: aggregate_kernel(ms, len(turned), *refs),
        in_specs=[vmem] * (len(ms) + 2 + len(turned)) + [scalars] * 2,
        out_specs=[vmem] * 3,
        out_shape=[*_placed(per, width), jax.ShapeDtypeStruct((DEVICES * per, width), BF16)],
        scratch_shapes=[pltpu.VMEM((DEVICES, len(ms) * per, width), BF16)],
        compiler_params=_params(24),
        name="aggregate",
    )(*[have[m] for m in ms], *prior, *turned, halo_tiles, tile_slots)


def _owner(pair, o):
    return pair * QUAD + 2 * o + lax.axis_index("nodes") % 2


def _hot(kinds, labels_ref, owner):
    held = labels_ref[owner].astype(F32)
    return [kinds == held[j : j + 1, :].astype(jnp.int32) for j in range(QUAD)]


def _rows(owner, px_ref, rows):
    return px_ref[pl.ds(pl.multiple_of(owner * rows, rows), rows), :]


def _inputs(pair, px_ref, agg_ref):
    rows = agg_ref.shape[0] // 2
    x = [_rows(_owner(pair, o), px_ref, rows) for o in range(2)]
    return jnp.concatenate([jnp.concatenate(x, axis=0), agg_ref[...]], axis=1)


def _forward(owners, inputs, labels_ref, in_t_ref, out_t_ref, bias_ref, keep):
    hidden = jnp.maximum(_dot(in_t_ref[...], inputs, NT), 0.0).astype(BF16)
    logits = _dot(out_t_ref[...], hidden) + jnp.concatenate([bias_ref[...]] * (hidden.shape[1] // LANES), axis=1)
    logits -= jnp.log(jnp.sum(jnp.exp(logits), axis=0, keepdims=True))
    probs = jnp.exp(logits)
    kinds = _iota(bias_ref.shape, 0)
    loss = count = jnp.zeros(bias_ref.shape, F32)
    lane = 0
    for owner in owners:
        for hot in _hot(kinds, labels_ref, owner):
            cut = slice(lane, lane + LANES)
            one = hot.astype(F32)
            loss -= jnp.where(hot, logits[:, cut], 0.0)
            count += one
            keep(cut, probs[:, cut] - one)
            lane += LANES
    return hidden, loss, count


def pair_kernel(c, *refs):
    blocks, (px_ref, *shared), outs = refs[0:2], refs[2:7], refs[7:12]
    agg_ref, hid_ref, slope_ref, loss_ref, count_ref = outs
    me = lax.axis_index("nodes")
    pair = (me // QUAD) ^ c
    rows = blocks[0].shape[0]
    for o, block in enumerate(blocks):
        at = ((me // 2 % 2) ^ o) * rows
        agg_ref[pl.ds(pl.multiple_of(at, rows), rows), :] = block[...]

    def keep(cut, x):
        slope_ref[:, cut] = x

    owners = [_owner(pair, o) for o in range(2)]
    hid_ref[...], loss_ref[...], count_ref[...] = _forward(owners, _inputs(pair, px_ref, agg_ref), *shared, keep)


def one_kernel(m, *refs):
    block, (px_ref, *shared), (hid_ref, slope_ref, loss_ref, count_ref) = refs[0], refs[1:6], refs[6:10]
    owner = lax.axis_index("nodes") ^ m
    inputs = jnp.concatenate([_rows(owner, px_ref, block.shape[0]), block[...]], axis=1)

    def keep(cut, x):
        slope_ref[:, cut] = x

    hid_ref[...], loss_ref[...], count_ref[...] = _forward([owner], inputs, *shared, keep)


def last_kernel(m, *refs):
    blocks, (px_ref, *shared), partner, prior = refs[0:2], refs[2:7], refs[7:11], refs[11:17]
    agg_ref, hid_ref, slope_ref, stats_ref, part, losses, counts = refs[17:]
    me = lax.axis_index("nodes")
    rows = blocks[0].shape[0]
    at = [pl.ds(pl.multiple_of(((me // 2 % 2) ^ o) * rows, rows), rows) for o in range(2)]
    for o, block in enumerate(blocks):
        agg_ref[at[o], :] = block[...]
    hid_ref[:, at[0]], slope_ref[:, at[0]] = partner[0][...], partner[1][...]

    def keep(cut, x):
        part[:, cut] = x

    inputs = jnp.concatenate([_rows(me ^ m, px_ref, rows), blocks[1][...]], axis=1)
    hidden, loss, count = _forward([me ^ m], inputs, *shared, keep)
    hid_ref[:, at[1]], slope_ref[:, at[1]] = hidden, part[...]
    mine = me // QUAD
    for c in range(QUAD - 1):
        losses[mine ^ c], counts[mine ^ c] = prior[2 * c][...], prior[2 * c + 1][...]
    losses[mine ^ (QUAD - 1)], counts[mine ^ (QUAD - 1)] = loss + partner[2][...], count + partner[3][...]
    loss, count = (jnp.sum(sum(x[q] for q in range(QUAD)), axis=1, keepdims=True) for x in (losses, counts))
    stats_ref[...] = jnp.where(_iota(stats_ref.shape, 1) == 0, loss, count)


def own_kernel(px_ref, agg_ref, in_t_ref, hidden_ref):
    rows = agg_ref.shape[0]
    x = px_ref[pl.ds(pl.multiple_of(lax.axis_index("nodes") * rows, rows), rows), :]
    pre = _dot(jnp.concatenate([x, agg_ref[...]], axis=1), in_t_ref[...], NT)
    hidden_ref[...] = jnp.maximum(pre, 0.0).astype(BF16)


def own(part_x, agg, in_t):
    vmem = pl.BlockSpec(memory_space=pltpu.VMEM)
    return pl.pallas_call(
        own_kernel,
        in_specs=[vmem] * 3,
        out_specs=vmem,
        out_shape=jax.ShapeDtypeStruct((agg.shape[0], in_t.shape[0]), BF16),
        cost_estimate=pl.CostEstimate(flops=1 << 26, bytes_accessed=1 << 18, transcendentals=0),
        compiler_params=_params(8),
        name="own",
    )(part_x, agg, in_t)


def _call(kernel, name, shapes, operands, scratch=()):
    vmem = pl.BlockSpec(memory_space=pltpu.VMEM)
    return pl.pallas_call(
        kernel,
        in_specs=[vmem] * len(operands),
        out_specs=[vmem] * len(shapes),
        out_shape=[jax.ShapeDtypeStruct(*x) for x in shapes],
        scratch_shapes=[pltpu.VMEM(*x) for x in scratch],
        cost_estimate=pl.CostEstimate(flops=1 << 29, bytes_accessed=1 << 21, transcendentals=1 << 18),
        compiler_params=_params(12),
        name=name,
    )(*operands)


def forward_pair(have, c, shared):
    rows, width = have[0].shape
    units, padded = shared[2].shape[0], shared[4].shape[0]
    stat = ((padded, LANES), F32)
    shapes = [((2 * rows, width), BF16), ((units, 2 * rows), BF16), ((padded, 2 * rows), F32), stat, stat]
    return _call(lambda *refs: pair_kernel(c, *refs), "forward_pair", shapes, [have[4 * c], have[4 * c + 2], *shared])


def forward_one(have, m, shared):
    rows, units, padded = have[0].shape[0], shared[2].shape[0], shared[4].shape[0]
    stat = ((padded, LANES), F32)
    shapes = [((units, rows), BF16), ((padded, rows), F32), stat, stat]
    return _call(lambda *refs: one_kernel(m, *refs), "forward_one", shapes, [have[m], *shared])


def forward_last(have, m, shared, partner, prior):
    rows, width = have[0].shape
    units, padded = shared[2].shape[0], shared[4].shape[0]
    stat = ((padded, LANES), F32)
    shapes = [((2 * rows, width), BF16), ((units, 2 * rows), BF16), ((padded, 2 * rows), F32), stat]
    stats = [x for held in prior for x in held[3:5]]
    scratch = [((padded, rows), F32)] + [((QUAD, padded, LANES), F32)] * 2
    operands = [have[m - 2], have[m], *shared, *partner, *stats]
    return _call(lambda *refs: last_kernel(m, *refs), "forward_last", shapes, operands, scratch)


def backward_kernel(classes, *refs):
    held, refs = [refs[3 * c : 3 * c + 3] for c in range(QUAD)], refs[3 * QUAD :]
    px_ref, labels_ref, out_ref, mine_ref, other_ref, sums_ref, class_ref, grads = refs
    me = lax.axis_index("nodes")
    padded = mine_ref.shape[0]
    units = out_ref.shape[0]

    both = mine_ref[...] + other_ref[...]
    loss, count = both[:, 0:1], both[:, 1:2]
    real = _iota((padded, 1), 0) < classes
    difficulty = jnp.where(real, (loss + 1.0) / (count + 1.0), 0.0)
    weight = difficulty / (jnp.sum(difficulty, axis=0, keepdims=True) / classes)
    share = 1.0 / (1.0 + jnp.sum(count, axis=0, keepdims=True))
    class_ref[...] = jnp.transpose(jnp.broadcast_to(weight, (padded, LANES)))[0:1, 0:classes]
    scaled = jnp.broadcast_to(weight * share, (padded, LANES))

    kinds = _iota((padded, LANES), 0)
    for c, (agg_ref, hid_ref, slope_ref) in enumerate(held):
        pair = (me // QUAD) ^ c
        parts = []
        for o in range(2):
            for hot in _hot(kinds, labels_ref, _owner(pair, o)):
                row = jnp.sum(jnp.where(hot, scaled, 0.0), axis=0, keepdims=True)
                cut = slice(LANES * len(parts), LANES * (len(parts) + 1))
                parts.append((row * slope_ref[:, cut]).astype(BF16))
        dlogits = jnp.concatenate(parts, axis=1)
        hidden = hid_ref[...]
        dpre = jnp.where(hidden > 0, _dot(out_ref[...], dlogits), 0.0).astype(BF16)
        grads[pair, 0:units] = _dot(dpre, _inputs(pair, px_ref, agg_ref))
        grads[pair, units : units + padded] = _dot(dlogits, hidden, NT)
    sums_ref[...] = sum(grads[q] for q in range(QUAD))


def backward(held, part_x, labels, out_p, mine, other, classes):
    units, padded = out_p.shape
    vmem = pl.BlockSpec(memory_space=pltpu.VMEM)
    operands = [*[x for h in held for x in h[0:3]], part_x, labels, out_p, mine, other]
    return pl.pallas_call(
        lambda *refs: backward_kernel(classes, *refs),
        in_specs=[vmem] * len(operands),
        out_specs=[vmem] * 2,
        out_shape=[
            jax.ShapeDtypeStruct((units + padded, 2 * part_x.shape[1]), F32),
            jax.ShapeDtypeStruct((1, classes), F32),
        ],
        scratch_shapes=[pltpu.VMEM((QUAD, units + padded, 2 * part_x.shape[1]), F32)],
        compiler_params=_params(20),
        name="backward",
    )(*operands)


def total_kernel(mine_ref, other_ref, self_ref, neigh_ref, out_ref):
    width, units = self_ref.shape
    classes = out_ref.shape[0]
    grad_in = jnp.transpose(mine_ref[0:units] + other_ref[0:units])
    self_ref[...] = grad_in[0:width]
    neigh_ref[...] = grad_in[width : 2 * width]
    out_ref[...] = (mine_ref[units:] + other_ref[units:])[0:classes]


def total(mine, other, width, units, classes):
    vmem = pl.BlockSpec(memory_space=pltpu.VMEM)
    return pl.pallas_call(
        total_kernel,
        in_specs=[vmem] * 2,
        out_specs=[vmem] * 3,
        out_shape=[
            jax.ShapeDtypeStruct((width, units), F32),
            jax.ShapeDtypeStruct((width, units), F32),
            jax.ShapeDtypeStruct((classes, units), F32),
        ],
        compiler_params=_params(8),
        name="total",
    )(mine, other)


def gathered_body(
    features, cluster, slot, halo_tiles, tile_slots, adjacency, labels, w_self, w_neigh, w_out, b_out
):
    packed = pack(features, cluster, slot, labels, DEVICES)
    raw = []

    def first(have):
        raw.extend(turn(adjacency))
        return raw

    have, (near, _), (_, far), prior = gather_rows(
        packed,
        first,
        lambda have: (place(have, range(0, 8)), turn_rest(raw[1])),
        lambda have, done: place(have, range(8, 12), done[0]),
    )
    late = range(12, 16)
    part_x, all_labels, agg = aggregate(have, late, prior, (near, far), halo_tiles, tile_slots)
    weighed = []

    def first(have):
        weighed.extend(weights(w_self, w_neigh, w_out, b_out))
        return weighed, own(part_x, agg, weighed[0])

    def ahead(cs):
        def work(have):
            in_t, out_t, _, bias = weighed
            return [forward_pair(have, c, (part_x, all_labels, in_t, out_t, bias)) for c in cs]

        return work

    have, (_, hidden), two, three = gather_plane(agg, first, ahead((0, 1)), ahead((2,)))
    held = [*two, *three]
    in_t, out_t, out_p, bias = weighed
    shared = (part_x, all_labels, in_t, out_t, bias)
    partner = forward_one(have, DEVICES - QUAD, shared)
    *last, mine = forward_last(have, DEVICES - 2, shared, partner, held)
    classes = w_out.shape[1]
    sums, class_weight = backward([*held, last], part_x, all_labels, out_p, mine, swap(mine, 1), classes)
    grad_self, grad_neigh, grad_out = total(sums, swap(sums, 1), *w_self.shape, classes)
    return hidden, grad_self, grad_neigh, grad_out.T, class_weight.reshape(-1)


def split_body(
    features, cluster, slot, halo_tiles, tile_slots, adjacency, labels, w_self, w_neigh, w_out, b_out
):
    rows = features.shape[0]
    width = features.shape[1]
    devices = lax.axis_size("nodes")
    per_peer = rows // devices
    order = jnp.argsort(cluster, stable=True)
    send_rows = features[order].reshape(devices, per_peer, width)
    send_slots = slot[order].reshape(devices, per_peer)
    recv_rows, recv_slots = (
        lax.all_to_all(send_rows, "nodes", split_axis=0, concat_axis=0, tiled=True),
        lax.all_to_all(send_slots, "nodes", split_axis=0, concat_axis=0, tiled=True),
    )
    part_x = (
        jnp.zeros((rows, width), jnp.bfloat16)
        .at[recv_slots.reshape(rows)]
        .set(recv_rows.reshape(rows, width))
    )
    local_tiles = rows // TILE
    wanted = halo_tiles[0]
    gathered = lax.all_gather(part_x, "nodes", axis=0, tiled=True)
    halo = gathered.reshape(-1, TILE, width)[wanted]
    sources = halo[tile_slots]
    adj_tiles = adjacency.reshape(local_tiles, TILE, adjacency.shape[1], TILE)
    agg = jnp.einsum("tikc,tkcf->tif", adj_tiles, sources, preferred_element_type=jnp.float32)
    agg = agg.reshape(rows, width).astype(jnp.bfloat16)
    pre = jnp.dot(part_x, w_self, preferred_element_type=jnp.float32) + jnp.dot(
        agg, w_neigh, preferred_element_type=jnp.float32
    )
    hidden = jnp.maximum(pre, 0.0).astype(jnp.bfloat16)
    logits = jnp.dot(hidden, w_out, preferred_element_type=jnp.float32) + b_out
    lse = jnp.log(jnp.sum(jnp.exp(logits), axis=1))
    classes_row = jnp.arange(w_out.shape[1], dtype=jnp.int32)
    onehot = (labels[:, None] == classes_row[None, :]).astype(jnp.float32)
    picked = jnp.sum(onehot * logits, axis=1)
    ce_rows = lse - picked
    local_loss = jnp.sum(onehot * ce_rows[:, None], axis=0)
    local_counts = jnp.sum(onehot, axis=0)
    loss_sum, counts = lax.psum((local_loss, local_counts), "nodes")
    difficulty = (loss_sum + 1.0) / (counts + 1.0)
    class_weight = difficulty / jnp.mean(difficulty)
    total = jnp.sum(counts)
    row_weight = jnp.sum(onehot * class_weight[None, :], axis=1) / (total + 1.0)
    probs = jnp.exp(logits - lse[:, None])
    dlogits = (row_weight[:, None] * (probs - onehot)).astype(jnp.bfloat16)
    part_out = jnp.dot(hidden.T, dlogits, preferred_element_type=jnp.float32)
    dhidden = jnp.dot(dlogits, w_out.T, preferred_element_type=jnp.float32)
    dpre = jnp.where(hidden > 0, dhidden, 0.0).astype(jnp.bfloat16)
    part_self = jnp.dot(part_x.T, dpre, preferred_element_type=jnp.float32)
    part_neigh = jnp.dot(agg.T, dpre, preferred_element_type=jnp.float32)
    grad_self, grad_neigh, grad_out = lax.psum((part_self, part_neigh, part_out), "nodes")
    return (hidden, grad_self, grad_neigh, grad_out, class_weight)


def solution(mesh):
    def body(*args):
        devices = mesh.shape["nodes"]
        rows = args[0].shape[0]
        per = rows // devices
        classes = args[9].shape[1]
        fits = devices == DEVICES and per == 2 * SUB and classes <= 256
        return (gathered_body if fits else split_body)(*args)

    return jax.shard_map(
        body,
        mesh=mesh,
        in_specs=(
            P(("groups", "nodes"), None),
            P(("groups", "nodes")),
            P(("groups", "nodes")),
            P(("groups", "nodes"), None),
            P(("groups", "nodes"), None),
            P(("groups", "nodes"), None, None),
            P(("groups", "nodes")),
            P(),
            P(),
            P(),
            P(),
        ),
        out_specs=(
            P(("groups", "nodes"), None),
            P("groups", None),
            P("groups", None),
            P("groups", None),
            P("groups"),
        ),
        check_vma=False,
    )
```

```python
import jax
import jax.numpy as jnp
from jax import lax
from jax.experimental import pallas as pl
from jax.experimental.pallas import tpu as pltpu
from jax.sharding import PartitionSpec as P

DEVICES = 16
QUAD = 4
TILE = 128
LANES = 128
SUB = 16
F32 = jnp.float32
BF16 = jnp.bfloat16


def _dot(a, b, contract=((1,), (0,))):
    return lax.dot_general(a, b, (contract, ((), ())), preferred_element_type=F32)


NT = ((1,), (1,))


def _iota(shape, dim):
    return lax.broadcasted_iota(jnp.int32, shape, dim)


def _stay(x):
    return pltpu.with_memory_space_constraint(x, pltpu.HBM)


def _fetch(sources, targets, sems):
    copies = [pltpu.make_async_copy(a, b, sems.at[i]) for i, (a, b) in enumerate(zip(sources, targets))]
    for copy in copies:
        copy.start()
    for copy in copies:
        copy.wait()


def _params(mib):
    return pltpu.CompilerParams(vmem_limit_bytes=mib << 20)


def swap(x, m):
    return lax.ppermute(x, "nodes", [(i, i ^ m) for i in range(DEVICES)])


def gather_all(block, work, cores=True):
    have = {0: block}
    done = []

    def hop(i, m):
        if work[i] is not None:
            have[m], out = lax.optimization_barrier((have[m], work[i](have)))
            done.append(out)

    def cross(*ms):
        if cores:
            have.update({m + 1: swap(have[m], 1) for m in ms})

    have[8], have[4], have[2] = (swap(block, m) for m in (8, 4, 2))
    cross(0)
    hop(0, 8)
    have[12], have[10], have[6] = swap(have[8], 4), swap(have[8], 2), swap(have[4], 2)
    cross(2, 4, 6, 8)
    hop(1, 12)
    have[14] = swap(have[12], 2)
    cross(10, 12)
    hop(2, 14)
    cross(14)
    return have, done


def gather_plane(block, first, second, third):
    have = {0: block}
    have[8], have[4], have[2], have[6] = (swap(block, m) for m in (8, 4, 2, 6))
    have[8], one = lax.optimization_barrier((have[8], first(have)))
    have[12], have[10], have[14] = swap(have[8], 4), swap(have[8], 2), swap(have[8], 6)
    have[10], two = lax.optimization_barrier((have[10], second(have)))
    have[12], three = lax.optimization_barrier((have[12], third(have, two)))
    return have, one, two, three


def gather_rows(block, first, second, third):
    have = {0: block}
    have[8], have[4], have[2] = (swap(block, m) for m in (8, 4, 2))
    (have[8], have[4], have[2]), one = lax.optimization_barrier(((have[8], have[4], have[2]), first(have)))
    have[12], have[10], have[6] = swap(have[8], 4), swap(have[8], 2), swap(have[4], 2)
    have[1], have[3], have[5], have[7], have[9] = (swap(have[m], 1) for m in (0, 2, 4, 6, 8))
    have[14] = swap(have[12], 2)
    have[11], have[13] = swap(have[10], 1), swap(have[12], 1)
    have[14], two = lax.optimization_barrier((have[14], second(have)))
    have[15] = swap(have[14], 1)
    have[15], three = lax.optimization_barrier((have[15], third(have, two)))
    return have, one, two, three


def pack_kernel(devices, *refs):
    sources, out_ref, targets, sems = refs[0:4], refs[4], refs[5:9], refs[9]
    _fetch(sources, targets, sems)
    feat_ref, cluster_ref, slot_ref, label_ref = targets
    rows = feat_ref.shape[0]
    per = rows // devices
    mine = lax.axis_index("nodes") % (LANES // per)
    cluster = cluster_ref[...]
    member = (_iota((devices, rows), 0) == cluster).astype(F32)
    before = (_iota((rows, rows), 0) < _iota((rows, rows), 1)).astype(BF16)
    rank = jnp.sum(member * _dot(member.astype(BF16), before), axis=0, keepdims=True).astype(jnp.int32)
    take = (_iota((rows, rows), 0) == cluster * per + rank).astype(BF16)
    out_ref[0:devices] = _dot(take, feat_ref[...]).astype(BF16).reshape(devices, per, feat_ref.shape[1])
    place = (_iota((LANES, rows), 0) == mine * per + rank).astype(BF16)
    slots = (member * (slot_ref[...] - rows // 2).astype(F32)).astype(BF16)
    out_ref[devices, 0:SUB] = _dot(slots, place, NT).astype(BF16)
    labels = jnp.concatenate([label_ref[...].astype(F32), jnp.zeros((SUB - label_ref.shape[0], LANES), F32)], axis=0)
    out_ref[devices, SUB : 2 * SUB] = labels.astype(BF16)


def pack(features, cluster, slot, labels, devices):
    rows, width = features.shape
    per = rows // devices
    inputs = (features, cluster.reshape(1, rows), slot.reshape(1, rows), labels.reshape(rows // LANES, LANES))
    inputs = [_stay(x) for x in inputs]
    return pl.pallas_call(
        lambda *refs: pack_kernel(devices, *refs),
        in_specs=[pl.BlockSpec(memory_space=pltpu.HBM)] * 4,
        out_specs=pl.BlockSpec(memory_space=pltpu.VMEM),
        out_shape=jax.ShapeDtypeStruct((devices + 1, per, width), BF16),
        scratch_shapes=[*[pltpu.VMEM(x.shape, x.dtype) for x in inputs], pltpu.SemaphoreType.DMA((4,))],
        compiler_params=_params(8),
        name="pack_rows",
    )(*inputs)


def weights_kernel(*refs):
    sources, w_out_ref, (in_t_ref, out_t_ref, out_ref, bias_ref), targets = refs[0:3], refs[3], refs[4:8], refs[8:11]
    wide, line, sems = refs[11:14]
    _fetch(sources, targets, sems)
    self_ref, neigh_ref, b_ref = targets
    classes = w_out_ref.shape[0]
    in_t_ref[...] = jnp.transpose(jnp.concatenate([self_ref[...], neigh_ref[...]], axis=0).astype(F32)).astype(BF16)
    wide[...] = jnp.zeros_like(wide)
    wide[0:classes, :] = w_out_ref[...].astype(F32)
    out_t_ref[...] = wide[...].astype(BF16)
    out_ref[...] = jnp.transpose(wide[...]).astype(BF16)
    line[...] = jnp.full_like(line, -1e30)
    line[:, 0:classes] = b_ref[...]
    bias_ref[...] = jnp.transpose(jnp.broadcast_to(line[...], (LANES, line.shape[1])))[0 : bias_ref.shape[0]]


def weights(w_self, w_neigh, w_out, b_out):
    width, units = w_self.shape
    classes = w_out.shape[1]
    padded = -(-classes // SUB) * SUB
    inputs = [_stay(x) for x in (w_self, w_neigh, b_out.reshape(1, classes))]
    return pl.pallas_call(
        weights_kernel,
        in_specs=[pl.BlockSpec(memory_space=pltpu.HBM)] * 3 + [pl.BlockSpec(memory_space=pltpu.VMEM)],
        out_specs=[pl.BlockSpec(memory_space=pltpu.VMEM)] * 4,
        out_shape=[
            jax.ShapeDtypeStruct((units, 2 * width), BF16),
            jax.ShapeDtypeStruct((padded, units), BF16),
            jax.ShapeDtypeStruct((units, padded), BF16),
            jax.ShapeDtypeStruct((padded, LANES), F32),
        ],
        scratch_shapes=[
            *[pltpu.VMEM(x.shape, x.dtype) for x in inputs],
            pltpu.VMEM((padded, units), F32),
            pltpu.VMEM((1, 2 * LANES), F32),
            pltpu.SemaphoreType.DMA((3,)),
        ],
        cost_estimate=pl.CostEstimate(flops=0, bytes_accessed=1 << 21, transcendentals=0),
        compiler_params=_params(8),
        name="weights",
    )(*inputs, w_out.T)


def _turn(adj, turned_ref, arrived=None):
    tiles, neigh = turned_ref.shape[0:2]
    side = SUB * SUB
    row = _iota((side, side), 0)
    move = ((row % SUB) * SUB + row // SUB == _iota((side, side), 1)).astype(BF16)
    for t in range(tiles):
        for b in range(TILE // SUB):
            if arrived:
                arrived(t, b)
            for j in range(neigh // (2 * SUB)):
                halves = [
                    adj[t, SUB * b : SUB * (b + 1), SUB * k : SUB * (k + 1), :].reshape(side, TILE)
                    for k in (2 * j, 2 * j + 1)
                ]
                moved = _dot(move, jnp.concatenate(halves, axis=1)).astype(BF16)
                for h in range(2):
                    k = 2 * j + h
                    turned_ref[t, SUB * k : SUB * (k + 1), SUB * b : SUB * (b + 1), :] = moved[
                        :, TILE * h : TILE * (h + 1)
                    ].reshape(SUB, SUB, TILE)


def turn_kernel(adj_ref, turned_ref, rest_ref, adj, sems, rest_sem):
    tiles = turned_ref.shape[0]
    pieces = sems.shape[1]
    part = TILE // pieces
    copies = [
        [
            pltpu.make_async_copy(
                adj_ref.at[pl.ds(t * TILE + i * part, part)], adj.at[t, pl.ds(i * part, part)], sems.at[t, i]
            )
            for i in range(pieces)
        ]
        for t in range(tiles)
    ]
    rest = pltpu.make_async_copy(adj_ref.at[pl.ds(tiles * TILE, rest_ref.shape[0])], rest_ref, rest_sem)
    for copy in sum(copies, []):
        copy.start()
    rest.start()

    def arrived(t, b):
        if b * SUB % part == 0:
            copies[t][b * SUB // part].wait()

    _turn(adj, turned_ref, arrived)
    rest.wait()


def turn(adjacency):
    rows, neigh, tile = adjacency.shape
    tiles = rows // tile // 2
    pieces = 2
    return pl.pallas_call(
        turn_kernel,
        in_specs=[pl.BlockSpec(memory_space=pltpu.HBM)],
        out_specs=[pl.BlockSpec(memory_space=pltpu.VMEM)] * 2,
        out_shape=[
            jax.ShapeDtypeStruct((tiles, neigh, tile, tile), BF16),
            jax.ShapeDtypeStruct((rows - tiles * tile, neigh, tile), BF16),
        ],
        scratch_shapes=[
            pltpu.VMEM((tiles, tile, neigh, tile), BF16),
            pltpu.SemaphoreType.DMA((tiles, pieces)),
            pltpu.SemaphoreType.DMA,
        ],
        cost_estimate=pl.CostEstimate(flops=tiles << 29, bytes_accessed=tiles << 22, transcendentals=0),
        compiler_params=_params(16),
        name="turn_adjacency",
    )(_stay(adjacency))


def turn_rest(rest):
    rows, neigh, tile = rest.shape
    shape = (rows // tile, neigh, tile, tile)
    vmem = pl.BlockSpec(memory_space=pltpu.VMEM)
    return pl.pallas_call(
        _turn,
        in_specs=[vmem],
        out_specs=vmem,
        out_shape=jax.ShapeDtypeStruct(shape, BF16),
        cost_estimate=pl.CostEstimate(flops=shape[0] << 29, bytes_accessed=shape[0] << 21, transcendentals=0),
        compiler_params=_params(12),
        name="turn_rest",
    )(rest.reshape(rows // tile, tile, neigh, tile))


def _place(ms, blocks, prior, px_ref, labels_ref, got):
    me = lax.axis_index("nodes")
    per = blocks[0].shape[1]
    rows = DEVICES * per
    if prior:
        labels_ref[...] = prior[1][...]
    slots = []
    for q in range(len(ms) // QUAD):
        held = 0.0
        for m, block in list(zip(ms, blocks))[q * QUAD : (q + 1) * QUAD]:
            at = q * LANES + ((me % QUAD) ^ (m % QUAD)) * per
            got[:, pl.ds(pl.multiple_of(at, per), per), :] = block[0:DEVICES]
            held += block[DEVICES, 0:SUB, :].astype(F32)
            labels_ref[me ^ m] = block[DEVICES, SUB : 2 * SUB, :]
        slots.append(held)
    slots = jnp.concatenate(slots, axis=1).astype(jnp.int32)
    position = _iota((rows, slots.shape[1]), 0) - rows // 2
    for p in range(DEVICES):
        put = (position == slots[p : p + 1, :]).astype(BF16)
        placed = _dot(put, got[p])
        if prior:
            placed += prior[0][p * rows : (p + 1) * rows, :].astype(F32)
        px_ref[p * rows : (p + 1) * rows, :] = placed.astype(BF16)


def _placed(per, width):
    return [
        jax.ShapeDtypeStruct((DEVICES * DEVICES * per, width), BF16),
        jax.ShapeDtypeStruct((DEVICES, SUB, LANES), BF16),
    ]


def place(have, ms, prior=()):
    per, width = have[0].shape[1:]
    vmem = pl.BlockSpec(memory_space=pltpu.VMEM)
    n = len(ms) + len(prior)
    return pl.pallas_call(
        lambda *refs: _place(ms, refs[: len(ms)], refs[len(ms) : n], *refs[n:]),
        in_specs=[vmem] * n,
        out_specs=[vmem] * 2,
        out_shape=_placed(per, width),
        scratch_shapes=[pltpu.VMEM((DEVICES, len(ms) * per, width), BF16)],
        cost_estimate=pl.CostEstimate(flops=1 << 30, bytes_accessed=1 << 22, transcendentals=0),
        compiler_params=_params(16),
        name="place",
    )(*[have[m] for m in ms], *prior)


def aggregate_kernel(ms, parts, *refs):
    n = len(ms)
    blocks, prior, turned, refs = refs[:n], refs[n : n + 2], refs[n + 2 : n + 2 + parts], refs[n + 2 + parts :]
    halo_ref, slots_ref, px_ref, labels_ref, agg_ref, got = refs
    _place(ms, blocks, prior, px_ref, labels_ref, got)
    neigh = slots_ref.shape[1]
    tiles = [ref.at[t] for ref in turned for t in range(ref.shape[0])]
    for t, adj in enumerate(tiles):
        total = jnp.zeros((TILE, px_ref.shape[1]), F32)
        for k in range(0, neigh, 2):
            sources = []
            for j in (k, k + 1):
                tile = halo_ref[0, slots_ref[t, j]]
                sources.append(px_ref[pl.ds(pl.multiple_of(tile * TILE, TILE), TILE), :])
            total += _dot(jnp.concatenate([adj[k], adj[k + 1]], axis=1), jnp.concatenate(sources, axis=0))
        agg_ref[t * TILE : (t + 1) * TILE, :] = total.astype(BF16)


def aggregate(have, ms, prior, turned, halo_tiles, tile_slots):
    per, width = have[0].shape[1:]
    scalars = pl.BlockSpec(memory_space=pltpu.SMEM)
    vmem = pl.BlockSpec(memory_space=pltpu.VMEM)
    return pl.pallas_call(
        lambda *refs: aggregate_kernel(ms, len(turned), *refs),
        in_specs=[vmem] * (len(ms) + 2 + len(turned)) + [scalars] * 2,
        out_specs=[vmem] * 3,
        out_shape=[*_placed(per, width), jax.ShapeDtypeStruct((DEVICES * per, width), BF16)],
        scratch_shapes=[pltpu.VMEM((DEVICES, len(ms) * per, width), BF16)],
        compiler_params=_params(24),
        name="aggregate",
    )(*[have[m] for m in ms], *prior, *turned, halo_tiles, tile_slots)


def _owner(pair, o):
    return pair * QUAD + 2 * o + lax.axis_index("nodes") % 2


def _hot(kinds, labels_ref, owner):
    held = labels_ref[owner].astype(F32)
    return [kinds == held[j : j + 1, :].astype(jnp.int32) for j in range(QUAD)]


def _rows(owner, px_ref, rows):
    return px_ref[pl.ds(pl.multiple_of(owner * rows, rows), rows), :]


def _inputs(pair, px_ref, agg_ref):
    rows = agg_ref.shape[0] // 2
    x = [_rows(_owner(pair, o), px_ref, rows) for o in range(2)]
    return jnp.concatenate([jnp.concatenate(x, axis=0), agg_ref[...]], axis=1)


def _forward(owners, inputs, labels_ref, in_t_ref, out_t_ref, bias_ref, keep):
    hidden = jnp.maximum(_dot(in_t_ref[...], inputs, NT), 0.0).astype(BF16)
    logits = _dot(out_t_ref[...], hidden) + jnp.concatenate([bias_ref[...]] * (hidden.shape[1] // LANES), axis=1)
    logits -= jnp.log(jnp.sum(jnp.exp(logits), axis=0, keepdims=True))
    probs = jnp.exp(logits)
    kinds = _iota(bias_ref.shape, 0)
    loss = count = jnp.zeros(bias_ref.shape, F32)
    lane = 0
    for owner in owners:
        for hot in _hot(kinds, labels_ref, owner):
            cut = slice(lane, lane + LANES)
            one = hot.astype(F32)
            loss -= jnp.where(hot, logits[:, cut], 0.0)
            count += one
            keep(cut, probs[:, cut] - one)
            lane += LANES
    return hidden, loss, count


def pair_kernel(c, *refs):
    blocks, (px_ref, *shared), outs = refs[0:2], refs[2:7], refs[7:12]
    agg_ref, hid_ref, slope_ref, loss_ref, count_ref = outs
    me = lax.axis_index("nodes")
    pair = (me // QUAD) ^ c
    rows = blocks[0].shape[0]
    for o, block in enumerate(blocks):
        at = ((me // 2 % 2) ^ o) * rows
        agg_ref[pl.ds(pl.multiple_of(at, rows), rows), :] = block[...]

    def keep(cut, x):
        slope_ref[:, cut] = x

    owners = [_owner(pair, o) for o in range(2)]
    hid_ref[...], loss_ref[...], count_ref[...] = _forward(owners, _inputs(pair, px_ref, agg_ref), *shared, keep)


def one_kernel(m, *refs):
    block, (px_ref, *shared), (hid_ref, slope_ref, loss_ref, count_ref) = refs[0], refs[1:6], refs[6:10]
    owner = lax.axis_index("nodes") ^ m
    inputs = jnp.concatenate([_rows(owner, px_ref, block.shape[0]), block[...]], axis=1)

    def keep(cut, x):
        slope_ref[:, cut] = x

    hid_ref[...], loss_ref[...], count_ref[...] = _forward([owner], inputs, *shared, keep)


def rest_kernel(m, *refs):
    blocks, (px_ref, *shared), partner, outs = refs[0:2], refs[2:7], refs[7:11], refs[11:]
    agg_ref, hid_ref, slope_ref, loss_ref, count_ref, part = outs
    me = lax.axis_index("nodes")
    rows = blocks[0].shape[0]
    at = [pl.ds(pl.multiple_of(((me // 2 % 2) ^ o) * rows, rows), rows) for o in range(2)]
    for o, block in enumerate(blocks):
        agg_ref[at[o], :] = block[...]
    hid_ref[:, at[0]], slope_ref[:, at[0]] = partner[0][...], partner[1][...]

    def keep(cut, x):
        part[:, cut] = x

    inputs = jnp.concatenate([_rows(me ^ m, px_ref, rows), blocks[1][...]], axis=1)
    hidden, loss, count = _forward([me ^ m], inputs, *shared, keep)
    hid_ref[:, at[1]], slope_ref[:, at[1]] = hidden, part[...]
    loss_ref[...], count_ref[...] = loss + partner[2][...], count + partner[3][...]


def last_kernel(m, *refs):
    prior, refs = refs[11:17], refs[:11] + refs[17:]
    stats_ref, part, loss_ref, count_ref, losses, counts = refs[14:]
    rest_kernel(m, *refs[:14], loss_ref, count_ref, part)
    mine = lax.axis_index("nodes") // QUAD
    for c in range(QUAD - 1):
        losses[mine ^ c], counts[mine ^ c] = prior[2 * c][...], prior[2 * c + 1][...]
    losses[mine ^ (QUAD - 1)], counts[mine ^ (QUAD - 1)] = loss_ref[...], count_ref[...]
    loss, count = (jnp.sum(sum(x[q] for q in range(QUAD)), axis=1, keepdims=True) for x in (losses, counts))
    stats_ref[...] = jnp.where(_iota(stats_ref.shape, 1) == 0, loss, count)


def own_kernel(px_ref, agg_ref, in_t_ref, hidden_ref):
    rows = agg_ref.shape[0]
    x = px_ref[pl.ds(pl.multiple_of(lax.axis_index("nodes") * rows, rows), rows), :]
    pre = _dot(jnp.concatenate([x, agg_ref[...]], axis=1), in_t_ref[...], NT)
    hidden_ref[...] = jnp.maximum(pre, 0.0).astype(BF16)


def own(part_x, agg, in_t):
    vmem = pl.BlockSpec(memory_space=pltpu.VMEM)
    return pl.pallas_call(
        own_kernel,
        in_specs=[vmem] * 3,
        out_specs=vmem,
        out_shape=jax.ShapeDtypeStruct((agg.shape[0], in_t.shape[0]), BF16),
        cost_estimate=pl.CostEstimate(flops=1 << 26, bytes_accessed=1 << 18, transcendentals=0),
        compiler_params=_params(8),
        name="own",
    )(part_x, agg, in_t)


def _call(kernel, name, shapes, operands, scratch=()):
    vmem = pl.BlockSpec(memory_space=pltpu.VMEM)
    return pl.pallas_call(
        kernel,
        in_specs=[vmem] * len(operands),
        out_specs=[vmem] * len(shapes),
        out_shape=[jax.ShapeDtypeStruct(*x) for x in shapes],
        scratch_shapes=[pltpu.VMEM(*x) for x in scratch],
        cost_estimate=pl.CostEstimate(flops=1 << 29, bytes_accessed=1 << 21, transcendentals=1 << 18),
        compiler_params=_params(12),
        name=name,
    )(*operands)


def forward_pair(have, c, shared):
    rows, width = have[0].shape
    units, padded = shared[2].shape[0], shared[4].shape[0]
    stat = ((padded, LANES), F32)
    shapes = [((2 * rows, width), BF16), ((units, 2 * rows), BF16), ((padded, 2 * rows), F32), stat, stat]
    return _call(lambda *refs: pair_kernel(c, *refs), "forward_pair", shapes, [have[4 * c], have[4 * c + 2], *shared])


def forward_one(have, m, shared):
    rows, units, padded = have[0].shape[0], shared[2].shape[0], shared[4].shape[0]
    stat = ((padded, LANES), F32)
    shapes = [((units, rows), BF16), ((padded, rows), F32), stat, stat]
    return _call(lambda *refs: one_kernel(m, *refs), "forward_one", shapes, [have[m], *shared])


def forward_rest(have, m, shared, partner, prior=()):
    rows, width = have[0].shape
    units, padded = shared[2].shape[0], shared[4].shape[0]
    stat = ((padded, LANES), F32)
    shapes = [((2 * rows, width), BF16), ((units, 2 * rows), BF16), ((padded, 2 * rows), F32), stat]
    scratch = [((padded, rows), F32)]
    operands = [have[m - 2], have[m], *shared, *partner]
    if not prior:
        return _call(lambda *refs: rest_kernel(m, *refs), "forward_rest", [*shapes, stat], operands, scratch)
    operands += [x for held in prior for x in held[3:5]]
    scratch += [stat] * 2 + [((QUAD, padded, LANES), F32)] * 2
    return _call(lambda *refs: last_kernel(m, *refs), "forward_last", shapes, operands, scratch)


def backward_kernel(classes, *refs):
    held, refs = [refs[3 * c : 3 * c + 3] for c in range(QUAD)], refs[3 * QUAD :]
    px_ref, labels_ref, out_ref, mine_ref, other_ref, sums_ref, class_ref, grads = refs
    me = lax.axis_index("nodes")
    padded = mine_ref.shape[0]
    units = out_ref.shape[0]

    both = mine_ref[...] + other_ref[...]
    loss, count = both[:, 0:1], both[:, 1:2]
    real = _iota((padded, 1), 0) < classes
    difficulty = jnp.where(real, (loss + 1.0) / (count + 1.0), 0.0)
    weight = difficulty / (jnp.sum(difficulty, axis=0, keepdims=True) / classes)
    share = 1.0 / (1.0 + jnp.sum(count, axis=0, keepdims=True))
    class_ref[...] = jnp.transpose(jnp.broadcast_to(weight, (padded, LANES)))[0:1, 0:classes]
    scaled = jnp.broadcast_to(weight * share, (padded, LANES))

    kinds = _iota((padded, LANES), 0)
    for c, (agg_ref, hid_ref, slope_ref) in enumerate(held):
        pair = (me // QUAD) ^ c
        parts = []
        for o in range(2):
            for hot in _hot(kinds, labels_ref, _owner(pair, o)):
                row = jnp.sum(jnp.where(hot, scaled, 0.0), axis=0, keepdims=True)
                cut = slice(LANES * len(parts), LANES * (len(parts) + 1))
                parts.append((row * slope_ref[:, cut]).astype(BF16))
        dlogits = jnp.concatenate(parts, axis=1)
        hidden = hid_ref[...]
        dpre = jnp.where(hidden > 0, _dot(out_ref[...], dlogits), 0.0).astype(BF16)
        grads[pair, 0:units] = _dot(dpre, _inputs(pair, px_ref, agg_ref))
        grads[pair, units : units + padded] = _dot(dlogits, hidden, NT)
    sums_ref[...] = sum(grads[q] for q in range(QUAD))


def backward(held, part_x, labels, out_p, mine, other, classes):
    units, padded = out_p.shape
    vmem = pl.BlockSpec(memory_space=pltpu.VMEM)
    operands = [*[x for h in held for x in h[0:3]], part_x, labels, out_p, mine, other]
    return pl.pallas_call(
        lambda *refs: backward_kernel(classes, *refs),
        in_specs=[vmem] * len(operands),
        out_specs=[vmem] * 2,
        out_shape=[
            jax.ShapeDtypeStruct((units + padded, 2 * part_x.shape[1]), F32),
            jax.ShapeDtypeStruct((1, classes), F32),
        ],
        scratch_shapes=[pltpu.VMEM((QUAD, units + padded, 2 * part_x.shape[1]), F32)],
        compiler_params=_params(20),
        name="backward",
    )(*operands)


def total_kernel(mine_ref, other_ref, self_ref, neigh_ref, out_ref):
    width, units = self_ref.shape
    classes = out_ref.shape[0]
    grad_in = jnp.transpose(mine_ref[0:units] + other_ref[0:units])
    self_ref[...] = grad_in[0:width]
    neigh_ref[...] = grad_in[width : 2 * width]
    out_ref[...] = (mine_ref[units:] + other_ref[units:])[0:classes]


def total(mine, other, width, units, classes):
    vmem = pl.BlockSpec(memory_space=pltpu.VMEM)
    return pl.pallas_call(
        total_kernel,
        in_specs=[vmem] * 2,
        out_specs=[vmem] * 3,
        out_shape=[
            jax.ShapeDtypeStruct((width, units), F32),
            jax.ShapeDtypeStruct((width, units), F32),
            jax.ShapeDtypeStruct((classes, units), F32),
        ],
        compiler_params=_params(8),
        name="total",
    )(mine, other)


def gathered_body(
    features, cluster, slot, halo_tiles, tile_slots, adjacency, labels, w_self, w_neigh, w_out, b_out
):
    packed = pack(features, cluster, slot, labels, DEVICES)
    raw = []

    def first(have):
        raw.extend(turn(adjacency))
        return raw

    have, (near, _), (_, far), prior = gather_rows(
        packed,
        first,
        lambda have: (place(have, range(0, 8)), turn_rest(raw[1])),
        lambda have, done: place(have, range(8, 12), done[0]),
    )
    late = range(12, 16)
    part_x, all_labels, agg = aggregate(have, late, prior, (near, far), halo_tiles, tile_slots)
    weighed = []

    def first(have):
        weighed.extend(weights(w_self, w_neigh, w_out, b_out))
        return weighed, own(part_x, agg, weighed[0])

    def shared():
        in_t, out_t, _, bias = weighed
        return part_x, all_labels, in_t, out_t, bias

    def second(have):
        return [forward_pair(have, c, shared()) for c in (0, 1)]

    def third(have, done):
        return forward_rest(have, 10, shared(), forward_one(have, 8, shared()))

    have, (_, hidden), held, more = gather_plane(agg, first, second, third)
    held = [*held, more]
    out_p = weighed[2]
    partner = forward_one(have, 12, shared())
    *last, mine = forward_rest(have, 14, shared(), partner, held)
    classes = w_out.shape[1]
    sums, class_weight = backward([*held, last], part_x, all_labels, out_p, mine, swap(mine, 1), classes)
    grad_self, grad_neigh, grad_out = total(sums, swap(sums, 1), *w_self.shape, classes)
    return hidden, grad_self, grad_neigh, grad_out.T, class_weight.reshape(-1)


def split_body(
    features, cluster, slot, halo_tiles, tile_slots, adjacency, labels, w_self, w_neigh, w_out, b_out
):
    rows = features.shape[0]
    width = features.shape[1]
    devices = lax.axis_size("nodes")
    per_peer = rows // devices
    order = jnp.argsort(cluster, stable=True)
    send_rows = features[order].reshape(devices, per_peer, width)
    send_slots = slot[order].reshape(devices, per_peer)
    recv_rows, recv_slots = (
        lax.all_to_all(send_rows, "nodes", split_axis=0, concat_axis=0, tiled=True),
        lax.all_to_all(send_slots, "nodes", split_axis=0, concat_axis=0, tiled=True),
    )
    part_x = (
        jnp.zeros((rows, width), jnp.bfloat16)
        .at[recv_slots.reshape(rows)]
        .set(recv_rows.reshape(rows, width))
    )
    local_tiles = rows // TILE
    wanted = halo_tiles[0]
    gathered = lax.all_gather(part_x, "nodes", axis=0, tiled=True)
    halo = gathered.reshape(-1, TILE, width)[wanted]
    sources = halo[tile_slots]
    adj_tiles = adjacency.reshape(local_tiles, TILE, adjacency.shape[1], TILE)
    agg = jnp.einsum("tikc,tkcf->tif", adj_tiles, sources, preferred_element_type=jnp.float32)
    agg = agg.reshape(rows, width).astype(jnp.bfloat16)
    pre = jnp.dot(part_x, w_self, preferred_element_type=jnp.float32) + jnp.dot(
        agg, w_neigh, preferred_element_type=jnp.float32
    )
    hidden = jnp.maximum(pre, 0.0).astype(jnp.bfloat16)
    logits = jnp.dot(hidden, w_out, preferred_element_type=jnp.float32) + b_out
    lse = jnp.log(jnp.sum(jnp.exp(logits), axis=1))
    classes_row = jnp.arange(w_out.shape[1], dtype=jnp.int32)
    onehot = (labels[:, None] == classes_row[None, :]).astype(jnp.float32)
    picked = jnp.sum(onehot * logits, axis=1)
    ce_rows = lse - picked
    local_loss = jnp.sum(onehot * ce_rows[:, None], axis=0)
    local_counts = jnp.sum(onehot, axis=0)
    loss_sum, counts = lax.psum((local_loss, local_counts), "nodes")
    difficulty = (loss_sum + 1.0) / (counts + 1.0)
    class_weight = difficulty / jnp.mean(difficulty)
    total = jnp.sum(counts)
    row_weight = jnp.sum(onehot * class_weight[None, :], axis=1) / (total + 1.0)
    probs = jnp.exp(logits - lse[:, None])
    dlogits = (row_weight[:, None] * (probs - onehot)).astype(jnp.bfloat16)
    part_out = jnp.dot(hidden.T, dlogits, preferred_element_type=jnp.float32)
    dhidden = jnp.dot(dlogits, w_out.T, preferred_element_type=jnp.float32)
    dpre = jnp.where(hidden > 0, dhidden, 0.0).astype(jnp.bfloat16)
    part_self = jnp.dot(part_x.T, dpre, preferred_element_type=jnp.float32)
    part_neigh = jnp.dot(agg.T, dpre, preferred_element_type=jnp.float32)
    grad_self, grad_neigh, grad_out = lax.psum((part_self, part_neigh, part_out), "nodes")
    return (hidden, grad_self, grad_neigh, grad_out, class_weight)


def solution(mesh):
    def body(*args):
        devices = mesh.shape["nodes"]
        rows = args[0].shape[0]
        per = rows // devices
        classes = args[9].shape[1]
        fits = devices == DEVICES and per == 2 * SUB and classes <= 256
        return (gathered_body if fits else split_body)(*args)

    return jax.shard_map(
        body,
        mesh=mesh,
        in_specs=(
            P(("groups", "nodes"), None),
            P(("groups", "nodes")),
            P(("groups", "nodes")),
            P(("groups", "nodes"), None),
            P(("groups", "nodes"), None),
            P(("groups", "nodes"), None, None),
            P(("groups", "nodes")),
            P(),
            P(),
            P(),
            P(),
        ),
        out_specs=(
            P(("groups", "nodes"), None),
            P("groups", None),
            P("groups", None),
            P("groups", None),
            P("groups"),
        ),
        check_vma=False,
    )
```
